32 devices in a mesh: seg: 4 (over y, x), exp: 8 (over z, core).
Axes of the slice: x: 2, y: 2, z: 4, core: 2. Of those that a mesh axis runs over, the one named last changes fastest.
Arguments:
- images: float32 [8, 2048, 4096], P('exp', 'seg'), may hold values from -6 to 6
- psf_coef: float32 [8, 2, 3], P('exp'), may hold values from 0.2 to 1
- phases: int32 [8, 2], P('exp'), may hold values from 0 to 15
- col_shift: int32 [8], P('exp'), may hold values from -40 to 40
- band_offset: int32 [8], P('exp'), may hold values from 0 to 16
- exposure_weight: bfloat16 [8], P('exp'), may hold values from 0.5 to 4
- patch_site: int32 [160], replicated, may hold values from 0 to 159, each once
Outputs:
- coadded: float32 [160, 32, 2048], P('exp', 'seg')
The draws below stay inside these ranges and needn't reach their ends.
Inputs may be any that keep to these rules, and one draw needn't show every extreme that they name: `phases`: a phase index p moves the sampling point by p / 16 of a pixel, the first entry along rows, the second along columns. An exposure's pixel column j lands on sky column j + col_shift. An exposure covers the sky bands band_offset to band_offset + 2048 / 32 - 1. `patch_site`: every sky position 2 * band + half is the site of exactly one stored patch.
All inputs are finite; a program needn't handle non-finite values.
Results may differ from the reference program's by a relative error of at most 0.0029.
Values may be sent and summed in bfloat16 or wider, within the bound.
No kernel may reach another device: no remote copies, remote signals or barrier semaphores. Data moves between devices by JAX's collectives and lax.ppermute only.
A program may use at most 128 MiB of HBM per device.

```python
import math
import jax
import jax.numpy as jnp
from jax import lax

W = 4096
BAND_ROWS = 32
SEG_BANDS = 16
TAPS = 21
NBASIS = 3
PHASES = 16
DXMAX = 40
EXPOSURES = 8
CCD_ROWS = 2048
SKY_BANDS = 80
PATCHES = 160
N_SEG = 4


def touch_ends(drawn, stream_key, smallest, high):
    extent = drawn.shape
    index_at = [jax.random.randint(jax.random.fold_in(stream_key, axis), (), 0, extent[axis]) for axis in range(len(extent))]
    drawn = drawn.at[tuple(index_at)].set(smallest)
    longest = extent.index(max(extent))
    index_at[longest] = (index_at[longest] + 1) % extent[longest]
    return drawn.at[tuple(index_at)].set(high)


def levels(stream_key, shape, split, least, high):
    def one(axis_at, shards_of):
        draws = jax.random.uniform(jax.random.fold_in(jax.random.fold_in(stream_key, 6), axis_at), (shards_of,), jnp.float32, least / len(split), high / len(split))
        return jnp.repeat(jnp.exp(draws), shape[axis_at] // shards_of).reshape((-1,) + (1,) * (len(shape) - axis_at - 1))

    gain = one(*split[0])
    for cut in split[1:]:
        gain = gain * one(*cut)
    return gain


def scatter_about(rng, extent, scale, most, split=(), dtype=jnp.bfloat16):
    level = levels(rng, extent, split, -0.22, 0.18) if split else 1.0
    drawn = jax.random.normal(rng, extent, jnp.float32) * scale * level
    return jnp.minimum(jnp.maximum(drawn, -most), most).astype(dtype)


def setup_inputs(seed: int = 0) -> dict:
    key_list = jax.random.split(jax.random.key(seed), 8)
    return {
        "images": scatter_about(key_list[0], (EXPOSURES, CCD_ROWS, W), 1.0, 6.0, ((0, 8), (1, 4)), jnp.float32),
        "psf_coef": jnp.clip(jnp.exp(math.log(1.0) - 1.609438 * jax.random.uniform(key_list[1], (EXPOSURES, 2, NBASIS), jnp.float32) ** levels(key_list[1], (EXPOSURES, 2, NBASIS), ((0, 8),), -0.2, 0.2)), 0.2, 1.0),
        "phases": touch_ends(jax.random.randint(key_list[2], (EXPOSURES, 2), 0, PHASES), jax.random.fold_in(key_list[2], 1), 0, PHASES - 1).astype(jnp.int32),
        "col_shift": touch_ends(jax.random.randint(key_list[3], (EXPOSURES,), 0 - DXMAX, DXMAX + 1), jax.random.fold_in(key_list[3], 1), 0 - DXMAX, DXMAX).astype(jnp.int32),
        "band_offset": touch_ends(jax.random.randint(key_list[4], (EXPOSURES,), 0, SKY_BANDS - N_SEG * SEG_BANDS + 1), jax.random.fold_in(key_list[4], 1), 0, SKY_BANDS - N_SEG * SEG_BANDS).astype(jnp.int32),
        "exposure_weight": jnp.clip(jnp.exp(math.log(4.0) - 2.0794415 * jax.random.uniform(key_list[5], (EXPOSURES,), jnp.float32) ** levels(key_list[5], (EXPOSURES,), ((0, 8),), -0.2, 0.2)), 0.5, 4.0).astype(jnp.bfloat16),
        "patch_site": jax.random.permutation(key_list[6], PATCHES).astype(jnp.int32),
    }


sigmas = (1.0, 2.0, 3.5)


def basis_table():
    offsets = jnp.arange(TAPS).astype(jnp.float32) - (TAPS // 2)
    table_rows = []
    for spread in sigmas:
        curve = jnp.exp(-offsets * offsets / (2.0 * spread * spread))
        table_rows.append(curve / jnp.sum(curve))
    return jnp.stack(table_rows)


def lanczos_weights(phase):
    fraction = phase.astype(jnp.float32) / PHASES
    offsets = jnp.arange(6).astype(jnp.float32) - 2.0
    shifted = offsets - fraction
    values = jnp.sinc(shifted) * jnp.sinc(shifted / 3.0)
    return values / jnp.sum(values)


def convolve(source, kernel, before, after, axis):
    length_axis = source.shape[axis]
    padding = [(0, 0), (0, 0)]
    padding[axis] = (before, after)
    padded = jnp.pad(source, padding)
    total = jnp.zeros(source.shape, jnp.float32)
    for position in range(kernel.shape[0]):
        total = total + kernel[position] * lax.slice_in_dim(padded, position, position + length_axis, axis=axis)
    return total


def warp_one(exposure, coef_pair, phase_pair, shift):
    basis_rows = basis_table()
    kernel_rows = jnp.sum(coef_pair[0][:, None] * basis_rows, axis=0)
    kernel_cols = jnp.sum(coef_pair[1][:, None] * basis_rows, axis=0)
    reach = TAPS // 2
    matched = convolve(exposure, kernel_rows, reach, reach, 0)
    matched = convolve(matched, kernel_cols, reach, reach, 1)
    shift_rows = lanczos_weights(phase_pair[0])
    shift_cols = lanczos_weights(phase_pair[1])
    along_rows = convolve(matched, shift_rows, 2, 3, 0)
    count_cols = exposure.shape[1]
    padded = jnp.pad(along_rows, ((0, 0), (DXMAX + 2, DXMAX + 3)))
    total = jnp.zeros(exposure.shape, jnp.float32)
    for position in range(6):
        row_start = (position + DXMAX - shift).astype(jnp.int32)
        total = total + shift_cols[position] * lax.dynamic_slice_in_dim(padded, row_start, count_cols, 1)
    return total


def reference(images, psf_coef, phases, col_shift, band_offset, exposure_weight, patch_site):
    count_cols = images.shape[2]
    half_cols = count_cols // 2
    columns = jnp.arange(count_cols).astype(jnp.int32)

    def add_exposure(state_pair, inputs):
        sky_sum, weight_sum = state_pair
        exposure, coef_pair, phase_pair, shift, offset, scale_weight = inputs
        warped = warp_one(exposure, coef_pair, phase_pair, shift)
        sent_rows = (scale_weight.astype(jnp.float32) * warped).astype(jnp.bfloat16)
        sent_rows = lax.optimization_barrier(sent_rows)
        inside = (columns - shift >= 0) & (columns - shift < count_cols)
        coverage = jnp.where(inside, scale_weight, jnp.zeros((), jnp.bfloat16))
        anchor = jnp.zeros((), jnp.int32)
        row_start = (offset * BAND_ROWS).astype(jnp.int32)
        sky_block = lax.dynamic_slice(sky_sum, (row_start, anchor), (CCD_ROWS, count_cols))
        sky_sum = lax.dynamic_update_slice(sky_sum, sky_block + sent_rows.astype(jnp.float32), (row_start, anchor))
        band_start = offset.astype(jnp.int32)
        band_block = lax.dynamic_slice(weight_sum, (band_start, anchor), (CCD_ROWS // BAND_ROWS, count_cols))
        weight_sum = lax.dynamic_update_slice(weight_sum, band_block + coverage.astype(jnp.float32)[None, :], (band_start, anchor))
        return (sky_sum, weight_sum), None

    sky_start = jnp.zeros((SKY_BANDS * BAND_ROWS, count_cols), jnp.float32)
    weight_start = jnp.zeros((SKY_BANDS, count_cols), jnp.float32)
    (sky_sum, weight_sum), _ = lax.scan(add_exposure, (sky_start, weight_start),
                                        (images, psf_coef, phases, col_shift, band_offset, exposure_weight))
    sky_sum = sky_sum.reshape(SKY_BANDS, BAND_ROWS, 2, half_cols).transpose(0, 2, 1, 3).reshape(PATCHES, BAND_ROWS, half_cols)
    weight_sum = weight_sum.reshape(PATCHES, half_cols)
    picked = jnp.take(sky_sum, patch_site, axis=0)
    totals = jnp.take(weight_sum, patch_site, axis=0)
    return picked / jnp.maximum(totals, 1.0)[:, None, :]
```

```python
import functools

import jax
import jax.numpy as jnp
import numpy as np
from jax import lax
from jax.experimental import pallas as pl
from jax.experimental.pallas import tpu as pltpu
from jax.sharding import Mesh, PartitionSpec as P

BAND_ROWS = 32
TAPS = 21
PHASES = 16
LANCZOS = 6
SPAN = TAPS + LANCZOS - 1
LEAD = TAPS // 2 + 2
HALO = 16
SIDE = 128
TILE = 256
STRIP = 128
CHUNKS = 2
VMEM = 48 * 1024 * 1024

sigmas = (1.0, 2.0, 3.5)


def basis_table():
    offsets = np.arange(TAPS) - TAPS // 2
    curves = [np.exp(-offsets * offsets / (2.0 * spread * spread)) for spread in sigmas]
    return [[float(value) for value in curve / curve.sum()] for curve in curves]


def lanczos_table():
    shifted = np.arange(LANCZOS)[None, :] - 2.0 - np.arange(PHASES)[:, None] / PHASES
    values = np.sinc(shifted) * np.sinc(shifted / 3.0)
    return (values / values.sum(axis=1, keepdims=True)).astype(np.float32)


def split(value):
    high = value.astype(jnp.bfloat16)
    return high, (value - high.astype(jnp.float32)).astype(jnp.bfloat16)


def banded(taps, masks, distance):
    matrix = jnp.zeros(distance.shape, jnp.float32)
    kernel, lanczos = taps
    weighted = [jnp.where(mask, lanczos[n], 0.0) for n, mask in enumerate(masks)]
    for t in range(SPAN):
        row = jnp.zeros_like(weighted[0])
        for n in range(LANCZOS):
            if 0 <= t - n < TAPS:
                row = row + kernel[t - n] * weighted[n]
        matrix = matrix + jnp.where(distance == t, row, 0.0)
    return matrix


def matrices_kernel(place, coef, phases, shift, table, rows_out, cols_out, *, rows, width, segments):
    basis = basis_table()

    def taps_of(axis):
        kernel = [sum(coef[axis, k] * basis[k][t] for k in range(len(sigmas))) for t in range(TAPS)]
        return kernel, [table[phases[axis], n] for n in range(LANCZOS)]

    taps = taps_of(1)
    offset = shift[0]
    zero = jnp.zeros((SIDE, SIDE), jnp.bfloat16)
    for variant, first in enumerate((0, None, width - TILE)):
        for part in range(2):
            for block in range(4):
                if not part <= block <= part + 2:
                    for term in range(2):
                        cols_out[variant, term, pl.ds(block * SIDE, SIDE), pl.ds(part * SIDE, SIDE)] = zero
                    continue
                output = part * SIDE + lax.broadcasted_iota(jnp.int32, (1, SIDE), 1)
                if first is None:
                    masks = [jnp.full((1, SIDE), True)] * LANCZOS
                else:
                    matched = first + output - offset
                    masks = [
                        (matched + (n - 2) >= 0) & (matched + (n - 2) < width) for n in range(LANCZOS)
                    ]
                distance = (
                    lax.broadcasted_iota(jnp.int32, (SIDE, SIDE), 0)
                    - lax.broadcasted_iota(jnp.int32, (SIDE, SIDE), 1)
                    + (offset + LEAD - SIDE + (block - part) * SIDE)
                )
                high, low = split(banded(taps, masks, distance))
                cols_out[variant, 0, pl.ds(block * SIDE, SIDE), pl.ds(part * SIDE, SIDE)] = high
                cols_out[variant, 1, pl.ds(block * SIDE, SIDE), pl.ds(part * SIDE, SIDE)] = low

    taps = taps_of(0)
    span = STRIP + 2 * HALO
    quarter = BAND_ROWS // segments
    bands = STRIP // BAND_ROWS
    order = lax.broadcasted_iota(jnp.int32, (1, STRIP), 1)
    within = lax.rem(order, bands * quarter)
    output = (
        lax.div(within, quarter) * BAND_ROWS + lax.div(order, bands * quarter) * quarter + lax.rem(within, quarter)
    )
    depth = cols_pad(3 * span)
    stacked = lax.broadcasted_iota(jnp.int32, (depth, STRIP), 0)
    term = jnp.where(stacked >= 2 * span, 2, jnp.where(stacked >= span, 1, 0))
    distance = stacked - term * span - output + (LEAD - HALO)
    for variant, first in enumerate((0, STRIP, rows - STRIP)):
        matched = place[0] * rows + first + output
        masks = [
            (matched + (n - 2) >= 0) & (matched + (n - 2) < rows * segments) for n in range(LANCZOS)
        ]
        matrix = banded(taps, masks, distance).T
        high, low = split(matrix)
        column = lax.broadcasted_iota(jnp.int32, matrix.shape, 1)
        both = jnp.where(column >= 2 * span, low.astype(jnp.float32), high.astype(jnp.float32))
        rows_out[variant] = both.astype(jnp.bfloat16)[:, : 3 * span]


def cols_pad(count):
    return -(-count // 128) * 128


def build_matrices(place, coef, phases, shift, rows, width, segments):
    span = 3 * (STRIP + 2 * HALO)
    smem = pl.BlockSpec(memory_space=pltpu.SMEM)
    vmem = pl.BlockSpec(memory_space=pltpu.VMEM)
    return pl.pallas_call(
        functools.partial(matrices_kernel, rows=rows, width=width, segments=segments),
        out_shape=(
            jax.ShapeDtypeStruct((3, STRIP, span), jnp.bfloat16),
            jax.ShapeDtypeStruct((3, 2, TILE + 2 * SIDE, TILE), jnp.bfloat16),
        ),
        in_specs=[smem] * 5,
        out_specs=(vmem, vmem),
        compiler_params=pltpu.CompilerParams(vmem_limit_bytes=VMEM),
        cost_estimate=pl.CostEstimate(flops=4_000_000, bytes_accessed=4_000_000, transcendentals=0),
        name="band_matrices",
    )(place, coef, phases, shift, jnp.asarray(lanczos_table()))


def filter_kernel(
    weight, low_l, low_c, low_r, mid_l, mid_c, mid_r, high_l, high_c, high_r, rows_m, cols_m, out,
    ext_high, ext_low, mat_high, mat_low, *, first_chunk, last_chunk, segments,
):
    half = pl.program_id(0)
    halves = pl.num_programs(0)
    rows, chunk = mid_c.shape
    at_left = first_chunk & (half == 0)
    at_right = last_chunk & (half == halves - 1)
    span = STRIP + 2 * HALO

    for row, parts in (
        (0, (low_l, low_c, low_r)),
        (HALO, (mid_l, mid_c, mid_r)),
        (HALO + rows, (high_l, high_c, high_r)),
    ):
        count = parts[0].shape[0]
        for part, column, outside in zip(parts, (0, SIDE, SIDE + chunk), (at_left, False, at_right)):
            value = part[...]
            if outside is not False:
                value = jnp.where(outside, 0.0, value)
            high, low = split(value)
            place = (pl.ds(row, count), pl.ds(column, value.shape[1]))
            ext_high[place] = high
            ext_low[place] = low

    strips = rows // STRIP
    quarters = rows // segments
    piece = STRIP // segments
    for tile in range((chunk + 2 * SIDE) // TILE):
        columns = pl.ds(tile * TILE, TILE)
        for strip in range(strips):
            window = pl.ds(strip * STRIP, span)
            variant = 0 if strip == 0 else (2 if strip == strips - 1 else 1)
            high = ext_high[window, columns]
            stack = jnp.concatenate([high, ext_low[window, columns], high], axis=0)
            matched = jnp.dot(rows_m[variant], stack, preferred_element_type=jnp.float32)
            high, low = split(matched)
            for quarter in range(segments):
                target = (pl.ds(quarter * quarters + strip * piece, piece), columns)
                mat_high[target] = high[quarter * piece : (quarter + 1) * piece]
                mat_low[target] = low[quarter * piece : (quarter + 1) * piece]

    tiles = chunk // TILE
    for tile in range(tiles):
        variant = jnp.int32(1)
        if tile == 0:
            variant = jnp.where(at_left, 0, variant)
        if tile == tiles - 1:
            variant = jnp.where(at_right, 2, variant)
        taps_high = cols_m[variant, 0]
        taps_low = cols_m[variant, 1]
        window = pl.ds(tile * TILE, TILE + 2 * SIDE)
        for strip in range(strips):
            place = pl.ds(strip * STRIP, STRIP)
            high = mat_high[place, window]
            warped = jnp.dot(high, taps_high, preferred_element_type=jnp.float32)
            warped += jnp.dot(mat_low[place, window], taps_high, preferred_element_type=jnp.float32)
            warped += jnp.dot(high, taps_low, preferred_element_type=jnp.float32)
            out[place, pl.ds(tile * TILE, TILE)] = (weight[0] * warped).astype(jnp.bfloat16)


def filter_chunk(weight, low, image, high, rows_m, cols_m, index, chunk, segments):
    rows, width = image.shape
    halves = 2
    half_blocks = width // halves // SIDE
    start = index * chunk // SIDE
    blocks = chunk // SIDE
    last = width // SIDE - 1

    def left(h):
        return 0, jnp.maximum(h * half_blocks + start - 1, 0)

    def centre(h):
        return 0, h * (half_blocks // blocks) + index

    def right(h):
        return 0, jnp.minimum(h * half_blocks + start + blocks, last)

    def whole(array):
        return pl.BlockSpec(array.shape, lambda h: (0,) * array.ndim)

    specs = [pl.BlockSpec(memory_space=pltpu.SMEM)]
    for source in (low, image, high):
        specs += [
            pl.BlockSpec((source.shape[0], SIDE), left),
            pl.BlockSpec((source.shape[0], chunk), centre),
            pl.BlockSpec((source.shape[0], SIDE), right),
        ]
    wide = chunk + 2 * SIDE
    return pl.pallas_call(
        functools.partial(
            filter_kernel,
            first_chunk=index == 0,
            last_chunk=(index + 1) * chunk == width // halves,
            segments=segments,
        ),
        out_shape=jax.ShapeDtypeStruct((rows, halves * chunk), jnp.bfloat16),
        grid=(halves,),
        in_specs=specs + [whole(rows_m), whole(cols_m)],
        out_specs=pl.BlockSpec((rows, chunk), lambda h: (0, h)),
        scratch_shapes=[
            pltpu.VMEM((rows + 2 * HALO, wide), jnp.bfloat16),
            pltpu.VMEM((rows + 2 * HALO, wide), jnp.bfloat16),
            pltpu.VMEM((rows, wide), jnp.bfloat16),
            pltpu.VMEM((rows, wide), jnp.bfloat16),
        ],
        compiler_params=pltpu.CompilerParams(vmem_limit_bytes=VMEM),
        cost_estimate=pl.CostEstimate(
            flops=halves * 2 * rows * chunk * 2048, bytes_accessed=halves * rows * chunk * 6, transcendentals=0
        ),
        name="warp_filter",
    )(weight, *([low] * 3), *([image] * 3), *([high] * 3), rows_m, cols_m)


def pair_kernel(info, sites, mine, other, out, *, quarter):
    chunk = out.shape[1]
    rows_two = 2 * quarter
    bands = mine.shape[0] // quarter

    def rows_of(source, offset, site):
        relative = lax.shift_right_logical(site, 1) - offset
        present = (relative >= 0) & (relative < bands)
        safe = jnp.clip(relative, 0, bands - 1)
        tile = source[
            pl.ds(pl.multiple_of(lax.shift_right_logical(safe, 1) * rows_two, rows_two), rows_two),
            pl.ds(pl.multiple_of((site & 1) * chunk, 128), chunk),
        ].astype(jnp.float32)
        rows = jnp.where((safe & 1) == 1, tile[quarter:], tile[:quarter])
        return jnp.where(present, rows, 0.0)

    def two_slots(step, carry):
        parts = []
        for slot in range(2):
            site = sites[step * 2 + slot]
            parts.append(rows_of(mine, info[0], site) + rows_of(other, info[1], site))
        out[pl.ds(pl.multiple_of(step * rows_two, rows_two), rows_two), :] = jnp.concatenate(parts, axis=0).astype(jnp.bfloat16)
        return carry

    lax.fori_loop(0, out.shape[0] // rows_two, two_slots, 0)


def pair_sum(info, sites, mine, other, slots, quarter):
    rows, double = mine.shape
    chunk = double // 2
    smem = pl.BlockSpec(memory_space=pltpu.SMEM)
    vmem = pl.BlockSpec(memory_space=pltpu.VMEM)
    return pl.pallas_call(
        functools.partial(pair_kernel, quarter=quarter),
        out_shape=jax.ShapeDtypeStruct((slots * quarter, chunk), jnp.bfloat16),
        in_specs=[smem, smem, vmem, vmem],
        out_specs=vmem,
        compiler_params=pltpu.CompilerParams(vmem_limit_bytes=VMEM),
        cost_estimate=pl.CostEstimate(
            flops=8 * slots * quarter * chunk,
            bytes_accessed=4 * rows * double + 2 * slots * quarter * chunk,
            transcendentals=0,
        ),
        name="pair_sum",
    )(info, sites, mine, other)


def finish_kernel(pieces, scale, *rest):
    out = rest[-1]
    total = pieces[0].astype(jnp.float32)
    for index in range(1, pieces.shape[0]):
        total += pieces[index].astype(jnp.float32)
    out[...] = total / scale[...]


def finish_chunk(pieces, scale, result, index):
    count, rows, chunk = pieces.shape
    column = pl.BlockSpec((rows, chunk), lambda i: (0, index))
    specs = [pl.BlockSpec(pieces.shape, lambda i: (0, 0, 0)), column]
    operands = [pieces, scale]
    aliases = {}
    if result is not None:
        specs.append(pl.BlockSpec(memory_space=pl.ANY))
        operands.append(result)
        aliases = {2: 0}
    return pl.pallas_call(
        finish_kernel,
        out_shape=jax.ShapeDtypeStruct(scale.shape, jnp.float32),
        grid=(1,),
        in_specs=specs,
        out_specs=column,
        input_output_aliases=aliases,
        compiler_params=pltpu.CompilerParams(vmem_limit_bytes=VMEM),
        cost_estimate=pl.CostEstimate(
            flops=count * rows * chunk, bytes_accessed=rows * chunk * (2 * count + 8), transcendentals=0
        ),
        name="patch_mean",
    )(*operands)


def per_device(images, psf_coef, phases, col_shift, band_offset, exposure_weight, patch_site):
    image = images[0]
    rows, width = image.shape
    segments = lax.axis_size("seg")
    lines = lax.axis_size("line")
    cores = lax.axis_size("core")
    quarter = BAND_ROWS // segments
    half_cols = width // 2
    chunk = half_cols // CHUNKS
    patches = patch_site.shape[0]
    own_slots = patches // (lines * cores)
    core = lax.axis_index("core")
    line = lax.axis_index("line")

    forward = [(i, i + 1) for i in range(segments - 1)]
    backward = [(i + 1, i) for i in range(segments - 1)]
    low = lax.ppermute(image[rows - HALO :], "seg", forward)
    high = lax.ppermute(image[:HALO], "seg", backward)
    weight = exposure_weight.astype(jnp.float32)
    facts = jnp.stack([col_shift[0].astype(jnp.float32), band_offset[0].astype(jnp.float32), weight[0]])
    facts = lax.all_gather(facts, ("line", "core"), axis=0, tiled=False)

    place = lax.axis_index("seg").astype(jnp.int32).reshape(1)
    rows_m, cols_m = build_matrices(place, psf_coef[0], phases[0], col_shift, rows, width, segments)

    sites = patch_site.reshape(lines, cores, own_slots)
    own_sites = lax.dynamic_index_in_dim(
        lax.dynamic_index_in_dim(sites, line, 0, keepdims=False), core, 0, keepdims=False
    )
    bands = segments * rows // BAND_ROWS
    site = jnp.repeat(own_sites, quarter)[:, None]
    column = (site % 2) * half_cols + jnp.arange(half_cols, dtype=jnp.int32)[None, :]
    total = jnp.zeros((own_slots * quarter, half_cols), jnp.float32)
    for exposure in range(lines * cores):
        moved = column - facts[exposure, 0].astype(jnp.int32)
        relative = site // 2 - facts[exposure, 1].astype(jnp.int32)
        inside = (moved >= 0) & (moved < width) & (relative >= 0) & (relative < bands)
        total = total + jnp.where(inside, facts[exposure, 2], 0.0)
    scale = jnp.maximum(total, 1.0)

    offsets = facts[:, 1].astype(jnp.int32).reshape(lines, cores)
    pair = lax.dynamic_index_in_dim(offsets, line, 0, keepdims=False)
    info = jnp.stack([pair[core], pair[1 - core]])
    pair_sites = lax.dynamic_index_in_dim(sites, core, 1, keepdims=False).reshape(-1)

    result = None
    swap = [(i, i ^ 1) for i in range(cores)]
    for index in range(CHUNKS):
        sent = filter_chunk(weight, low, image, high, rows_m, cols_m, index, chunk, segments)
        mine = lax.all_to_all(
            sent.reshape(segments, rows // segments, 2 * chunk), "seg", split_axis=0, concat_axis=0, tiled=True
        ).reshape(rows, 2 * chunk)
        other = lax.ppermute(mine, "core", swap)
        pieces = pair_sum(info, pair_sites, mine, other, lines * own_slots, quarter)
        pieces = lax.all_to_all(
            pieces.reshape(lines, own_slots * quarter, chunk), "line", split_axis=0, concat_axis=0, tiled=True
        )
        result = finish_chunk(pieces, scale, result, index)
    return result.reshape(own_slots, quarter, half_cols)


def solution(mesh):
    segments, exposures = mesh.shape["seg"], mesh.shape["exp"]
    parted = Mesh(mesh.devices.reshape(segments, exposures // 2, 2), ("seg", "line", "core"))
    spread = ("line", "core")
    placed = (
        P(spread, "seg", None),
        P(spread, None, None),
        P(spread, None),
        P(spread),
        P(spread),
        P(spread),
        P(),
    )
    return jax.shard_map(
        per_device, mesh=parted, in_specs=placed, out_specs=P(spread, "seg", None), check_vma=False
    )
```

```python
import functools

import jax
import jax.numpy as jnp
import numpy as np
from jax import lax
from jax.experimental import pallas as pl
from jax.experimental.pallas import tpu as pltpu
from jax.sharding import Mesh, PartitionSpec as P

BAND_ROWS = 32
TAPS = 21
PHASES = 16
LANCZOS = 6
SPAN = TAPS + LANCZOS - 1
LEAD = TAPS // 2 + 2
HALO = 16
SIDE = 128
TILE = 256
STRIP = 128
PARTS = (4, 4, 4, 4)
VMEM = 48 * 1024 * 1024

sigmas = (1.0, 2.0, 3.5)


def basis_table():
    offsets = np.arange(TAPS) - TAPS // 2
    curves = [np.exp(-offsets * offsets / (2.0 * spread * spread)) for spread in sigmas]
    return [[float(value) for value in curve / curve.sum()] for curve in curves]


def lanczos_table():
    shifted = np.arange(LANCZOS)[None, :] - 2.0 - np.arange(PHASES)[:, None] / PHASES
    values = np.sinc(shifted) * np.sinc(shifted / 3.0)
    return (values / values.sum(axis=1, keepdims=True)).astype(np.float32)


def lanczos_taps(phase):
    table = lanczos_table()
    taps = []
    for n in range(LANCZOS):
        tap = jnp.float32(table[0, n])
        for index in range(1, PHASES):
            tap = jnp.where(phase == index, jnp.float32(table[index, n]), tap)
        taps.append(tap)
    return taps


def split(value):
    high = value.astype(jnp.bfloat16)
    return high, (value - high.astype(jnp.float32)).astype(jnp.bfloat16)


def banded(taps, masks, distance):
    matrix = jnp.zeros(distance.shape, jnp.float32)
    kernel, lanczos = taps
    weighted = [jnp.where(mask, lanczos[n], 0.0) for n, mask in enumerate(masks)]
    for t in range(SPAN):
        row = jnp.zeros_like(weighted[0])
        for n in range(LANCZOS):
            if 0 <= t - n < TAPS:
                row = row + kernel[t - n] * weighted[n]
        matrix = matrix + jnp.where(distance == t, row, 0.0)
    return matrix


def matrices_kernel(place, coef, phases, shift, rows_out, cols_out, *, rows, width, segments):
    basis = basis_table()

    def taps_of(axis):
        kernel = [sum(coef[axis, k] * basis[k][t] for k in range(len(sigmas))) for t in range(TAPS)]
        return kernel, lanczos_taps(phases[axis])

    taps = taps_of(1)
    offset = shift[0]
    zero = jnp.zeros((SIDE, SIDE), jnp.bfloat16)
    for variant, first in enumerate((0, None, width - TILE)):
        for part in range(2):
            for block in range(4):
                if not part <= block <= part + 2:
                    for term in range(2):
                        cols_out[variant, term, pl.ds(block * SIDE, SIDE), pl.ds(part * SIDE, SIDE)] = zero
                    continue
                output = part * SIDE + lax.broadcasted_iota(jnp.int32, (1, SIDE), 1)
                if first is None:
                    masks = [jnp.full((1, SIDE), True)] * LANCZOS
                else:
                    matched = first + output - offset
                    masks = [
                        (matched + (n - 2) >= 0) & (matched + (n - 2) < width) for n in range(LANCZOS)
                    ]
                distance = (
                    lax.broadcasted_iota(jnp.int32, (SIDE, SIDE), 0)
                    - lax.broadcasted_iota(jnp.int32, (SIDE, SIDE), 1)
                    + (offset + LEAD - SIDE + (block - part) * SIDE)
                )
                high, low = split(banded(taps, masks, distance))
                cols_out[variant, 0, pl.ds(block * SIDE, SIDE), pl.ds(part * SIDE, SIDE)] = high
                cols_out[variant, 1, pl.ds(block * SIDE, SIDE), pl.ds(part * SIDE, SIDE)] = low

    taps = taps_of(0)
    span = STRIP + 2 * HALO
    quarter = BAND_ROWS // segments
    bands = STRIP // BAND_ROWS
    order = lax.broadcasted_iota(jnp.int32, (1, STRIP), 1)
    within = lax.rem(order, bands * quarter)
    owner = lax.div(order, bands * quarter) ^ place[0]
    output = lax.div(within, quarter) * BAND_ROWS + owner * quarter + lax.rem(within, quarter)
    depth = cols_pad(3 * span)
    stacked = lax.broadcasted_iota(jnp.int32, (depth, STRIP), 0)
    term = jnp.where(stacked >= 2 * span, 2, jnp.where(stacked >= span, 1, 0))
    distance = stacked - term * span - output + (LEAD - HALO)
    for variant, first in enumerate((0, STRIP, rows - STRIP)):
        matched = place[0] * rows + first + output
        masks = [
            (matched + (n - 2) >= 0) & (matched + (n - 2) < rows * segments) for n in range(LANCZOS)
        ]
        matrix = banded(taps, masks, distance).T
        high, low = split(matrix)
        column = lax.broadcasted_iota(jnp.int32, matrix.shape, 1)
        both = jnp.where(column >= 2 * span, low.astype(jnp.float32), high.astype(jnp.float32))
        rows_out[variant] = both.astype(jnp.bfloat16)[:, : 3 * span]


def cols_pad(count):
    return -(-count // 128) * 128


def build_matrices(place, coef, phases, shift, rows, width, segments):
    span = 3 * (STRIP + 2 * HALO)
    smem = pl.BlockSpec(memory_space=pltpu.SMEM)
    vmem = pl.BlockSpec(memory_space=pltpu.VMEM)
    return pl.pallas_call(
        functools.partial(matrices_kernel, rows=rows, width=width, segments=segments),
        out_shape=(
            jax.ShapeDtypeStruct((3, STRIP, span), jnp.bfloat16),
            jax.ShapeDtypeStruct((3, 2, TILE + 2 * SIDE, TILE), jnp.bfloat16),
        ),
        in_specs=[smem] * 4,
        out_specs=(vmem, vmem),
        compiler_params=pltpu.CompilerParams(vmem_limit_bytes=VMEM),
        cost_estimate=pl.CostEstimate(flops=4_000_000, bytes_accessed=4_000_000, transcendentals=0),
        name="band_matrices",
    )(place, coef, phases, shift)


def filter_kernel(
    weight, low_l, low_c, low_r, mid_l, mid_c, mid_r, high_l, high_c, high_r, rows_m, cols_m, *rest,
    first_chunk, last_chunk, segments,
):
    outs, (ext_high, ext_low, mat_high, mat_low) = rest[:segments], rest[segments:]
    half = pl.program_id(0)
    halves = pl.num_programs(0)
    rows, chunk = mid_c.shape
    at_left = first_chunk & (half == 0)
    at_right = last_chunk & (half == halves - 1)
    span = STRIP + 2 * HALO

    for row, parts in (
        (0, (low_l, low_c, low_r)),
        (HALO, (mid_l, mid_c, mid_r)),
        (HALO + rows, (high_l, high_c, high_r)),
    ):
        count = parts[0].shape[0]
        for part, column, outside in zip(parts, (0, SIDE, SIDE + chunk), (at_left, False, at_right)):
            value = part[...]
            if outside is not False:
                value = jnp.where(outside, 0.0, value)
            high, low = split(value)
            place = (pl.ds(row, count), pl.ds(column, value.shape[1]))
            ext_high[place] = high
            ext_low[place] = low

    strips = rows // STRIP
    for tile in range((chunk + 2 * SIDE) // TILE):
        columns = pl.ds(tile * TILE, TILE)
        for strip in range(strips):
            window = pl.ds(strip * STRIP, span)
            variant = 0 if strip == 0 else (2 if strip == strips - 1 else 1)
            high = ext_high[window, columns]
            stack = jnp.concatenate([high, ext_low[window, columns], high], axis=0)
            matched = jnp.dot(rows_m[variant], stack, preferred_element_type=jnp.float32)
            high, low = split(matched)
            mat_high[pl.ds(strip * STRIP, STRIP), columns] = high
            mat_low[pl.ds(strip * STRIP, STRIP), columns] = low

    tiles = chunk // TILE
    piece = STRIP // segments
    for tile in range(tiles):
        variant = jnp.int32(1)
        if tile == 0:
            variant = jnp.where(at_left, 0, variant)
        if tile == tiles - 1:
            variant = jnp.where(at_right, 2, variant)
        taps_high = cols_m[variant, 0]
        taps_low = cols_m[variant, 1]
        window = pl.ds(tile * TILE, TILE + 2 * SIDE)
        for strip in range(strips):
            place = pl.ds(strip * STRIP, STRIP)
            high = mat_high[place, window]
            warped = jnp.dot(high, taps_high, preferred_element_type=jnp.float32)
            warped += jnp.dot(mat_low[place, window], taps_high, preferred_element_type=jnp.float32)
            warped += jnp.dot(high, taps_low, preferred_element_type=jnp.float32)
            sent = (weight[0] * warped).astype(jnp.bfloat16)
            for owner, out in enumerate(outs):
                out[pl.ds(strip * piece, piece), pl.ds(tile * TILE, TILE)] = sent[owner * piece : (owner + 1) * piece]


def filter_chunk(weight, low, image, high, rows_m, cols_m, start, chunk, segments):
    rows, width = image.shape
    halves = 2
    half_blocks = width // halves // SIDE
    first = start // SIDE
    blocks = chunk // SIDE
    last = width // SIDE - 1

    def left(h):
        return 0, jnp.maximum(h * half_blocks + first - 1, 0)

    def centre(h):
        return 0, h * (half_blocks // blocks) + start // chunk

    def right(h):
        return 0, jnp.minimum(h * half_blocks + first + blocks, last)

    def whole(array):
        return pl.BlockSpec(array.shape, lambda h: (0,) * array.ndim)

    specs = [pl.BlockSpec(memory_space=pltpu.SMEM)]
    for source in (low, image, high):
        specs += [
            pl.BlockSpec((source.shape[0], SIDE), left),
            pl.BlockSpec((source.shape[0], chunk), centre),
            pl.BlockSpec((source.shape[0], SIDE), right),
        ]
    wide = chunk + 2 * SIDE
    return pl.pallas_call(
        functools.partial(
            filter_kernel,
            first_chunk=start == 0,
            last_chunk=start + chunk == width // halves,
            segments=segments,
        ),
        out_shape=[jax.ShapeDtypeStruct((rows // segments, halves * chunk), jnp.bfloat16)] * segments,
        grid=(halves,),
        in_specs=specs + [whole(rows_m), whole(cols_m)],
        out_specs=[pl.BlockSpec((rows // segments, chunk), lambda h: (0, h))] * segments,
        scratch_shapes=[
            pltpu.VMEM((rows + 2 * HALO, wide), jnp.bfloat16),
            pltpu.VMEM((rows + 2 * HALO, wide), jnp.bfloat16),
            pltpu.VMEM((rows, wide), jnp.bfloat16),
            pltpu.VMEM((rows, wide), jnp.bfloat16),
        ],
        compiler_params=pltpu.CompilerParams(vmem_limit_bytes=VMEM),
        cost_estimate=pl.CostEstimate(
            flops=halves * 2 * rows * chunk * 2048, bytes_accessed=halves * rows * chunk * 6, transcendentals=0
        ),
        name="warp_filter",
    )(weight, *([low] * 3), *([image] * 3), *([high] * 3), rows_m, cols_m)


def pair_kernel(place, offset, other_offset, sites, *rest, segments, lines, cores, quarter):
    mine, other = rest[:segments], rest[segments : 2 * segments]
    outs, (mine_all, other_all) = rest[2 * segments : 2 * segments + lines], rest[2 * segments + lines :]
    block = mine[0].shape[0]
    chunk = outs[0].shape[1]
    block_bands = block // quarter
    bands = block_bands * segments
    slots = outs[0].shape[0] // quarter
    two = 2 * quarter
    for step in range(segments):
        mine_all[pl.ds(step * block, block), :] = mine[step][...]
        other_all[pl.ds(step * block, block), :] = other[step][...]
    segment, line, core = place[0], place[1], place[2]

    def rows_of(source, from_offset, site):
        relative = lax.shift_right_logical(site, 1) - from_offset
        present = (relative >= 0) & (relative < bands)
        safe = jnp.clip(relative, 0, bands - 1)
        held = (lax.div(safe, block_bands) ^ segment) * block + lax.rem(safe, block_bands) // 2 * two
        tile = source[
            pl.ds(pl.multiple_of(held, two), two), pl.ds(pl.multiple_of((site & 1) * chunk, 128), chunk)
        ].astype(jnp.float32)
        rows = jnp.where((safe & 1) == 1, tile[quarter:], tile[:quarter])
        return jnp.where(present, rows, 0.0)

    for target, out in reversed(list(enumerate(outs))):
        owner = (line ^ target) * cores + core

        def summed(slot, owner=owner):
            site = sites[owner * slots + slot]
            return rows_of(mine_all, offset[0], site) + rows_of(other_all, other_offset[0], site)

        def two_slots(step, carry, summed=summed, out=out):
            rows = jnp.concatenate([summed(2 * step), summed(2 * step + 1)], axis=0)
            out[pl.ds(pl.multiple_of(step * two, two), two), :] = rows.astype(jnp.bfloat16)
            return carry

        lax.fori_loop(0, slots // 2, two_slots, 0)
        if slots % 2:
            out[pl.ds((slots - 1) * quarter, quarter), :] = summed(slots - 1).astype(jnp.bfloat16)


def pair_sum(place, offset, other_offset, sites, mine, other, slots, lines, cores, quarter):
    block, double = mine[0].shape
    chunk = double // 2
    segments = len(mine)
    smem = pl.BlockSpec(memory_space=pltpu.SMEM)
    vmem = pl.BlockSpec(memory_space=pltpu.VMEM)
    return pl.pallas_call(
        functools.partial(pair_kernel, segments=segments, lines=lines, cores=cores, quarter=quarter),
        out_shape=[jax.ShapeDtypeStruct((slots * quarter, chunk), jnp.bfloat16)] * lines,
        in_specs=[smem] * 4 + [vmem] * (2 * segments),
        out_specs=[vmem] * lines,
        scratch_shapes=[pltpu.VMEM((segments * block, double), jnp.bfloat16)] * 2,
        compiler_params=pltpu.CompilerParams(vmem_limit_bytes=VMEM),
        cost_estimate=pl.CostEstimate(
            flops=8 * lines * slots * quarter * chunk,
            bytes_accessed=4 * segments * block * double + 2 * lines * slots * quarter * chunk,
            transcendentals=0,
        ),
        name="pair_sum",
    )(place, offset, other_offset, sites, *mine, *other)


def weight_kernel(place, sites, facts, out, *, cores, quarter, width, bands):
    slots = out.shape[0] // quarter
    half_cols = out.shape[1]
    owner = place[1] * cores + place[2]
    column = lax.broadcasted_iota(jnp.int32, (quarter, half_cols), 1)

    def one_slot(slot, carry):
        site = sites[owner * slots + slot]
        band = lax.shift_right_logical(site, 1)
        total = jnp.zeros((quarter, half_cols), jnp.float32)
        for exposure in range(facts.shape[0]):
            first = facts[exposure, 0].astype(jnp.int32) - (site & 1) * half_cols
            relative = band - facts[exposure, 1].astype(jnp.int32)
            weight = jnp.where((relative >= 0) & (relative < bands), facts[exposure, 2], 0.0)
            total = total + jnp.where((column >= first) & (column < first + width), weight, 0.0)
        out[pl.ds(pl.multiple_of(slot * quarter, quarter), quarter), :] = jnp.maximum(total, 1.0)
        return carry

    lax.fori_loop(0, slots, one_slot, 0)


def patch_weights(place, sites, facts, slots, quarter, cores, width, bands):
    smem = pl.BlockSpec(memory_space=pltpu.SMEM)
    return pl.pallas_call(
        functools.partial(weight_kernel, cores=cores, quarter=quarter, width=width, bands=bands),
        out_shape=jax.ShapeDtypeStruct((slots * quarter, width // 2), jnp.float32),
        in_specs=[smem] * 3,
        out_specs=pl.BlockSpec(memory_space=pltpu.VMEM),
        cost_estimate=pl.CostEstimate(
            flops=40 * slots * quarter * width // 2, bytes_accessed=2 * slots * quarter * width, transcendentals=0
        ),
        name="patch_weights",
    )(place, sites, facts)


def finish_kernel(*refs, count):
    pieces, scale, out = refs[:count], refs[count], refs[-1]
    total = pieces[0][...].astype(jnp.float32)
    for piece in pieces[1:]:
        total += piece[...].astype(jnp.float32)
    out[...] = total / scale[...]


def finish_chunk(pieces, scale, result, start):
    rows, chunk = pieces[0].shape
    column = pl.BlockSpec((rows, chunk), lambda i: (0, start // chunk))
    specs = [pl.BlockSpec((rows, chunk), lambda i: (0, 0))] * len(pieces) + [column]
    operands = [*pieces, scale]
    aliases = {}
    if result is not None:
        specs.append(pl.BlockSpec(memory_space=pl.ANY))
        aliases = {len(operands): 0}
        operands.append(result)
    return pl.pallas_call(
        functools.partial(finish_kernel, count=len(pieces)),
        out_shape=jax.ShapeDtypeStruct(scale.shape, jnp.float32),
        grid=(1,),
        in_specs=specs,
        out_specs=column,
        input_output_aliases=aliases,
        compiler_params=pltpu.CompilerParams(vmem_limit_bytes=VMEM),
        cost_estimate=pl.CostEstimate(
            flops=len(pieces) * rows * chunk, bytes_accessed=rows * chunk * (2 * len(pieces) + 8), transcendentals=0
        ),
        name="patch_mean",
    )(*operands)


def swapped(value, axis, distance):
    count = lax.axis_size(axis)
    return lax.ppermute(value, axis, [(i, i ^ distance) for i in range(count)])


def scatter_sum(pieces):
    lines = len(pieces)
    pieces = list(pieces)
    kept = [pieces[0]]
    step = 1
    while step < lines:
        for distance in reversed(range(step, lines, 2 * step)):
            received = swapped(pieces[distance], "line", step)
            target = distance ^ step
            if target == 0:
                kept.append(received)
            else:
                both = pieces[target].astype(jnp.float32) + received.astype(jnp.float32)
                pieces[target] = both.astype(jnp.bfloat16)
        step *= 2
    return kept


def per_device(images, psf_coef, phases, col_shift, band_offset, exposure_weight, patch_site):
    image = images[0]
    rows, width = image.shape
    segments = lax.axis_size("seg")
    lines = lax.axis_size("line")
    cores = lax.axis_size("core")
    quarter = BAND_ROWS // segments
    half_cols = width // 2
    slots = patch_site.shape[0] // (lines * cores)
    bands = segments * rows // BAND_ROWS
    place = jnp.stack([lax.axis_index(axis) for axis in ("seg", "line", "core")]).astype(jnp.int32)

    forward = [(i, i + 1) for i in range(segments - 1)]
    backward = [(i + 1, i) for i in range(segments - 1)]
    low = lax.ppermute(image[rows - HALO :], "seg", forward)
    high = lax.ppermute(image[:HALO], "seg", backward)
    rows_m, cols_m = build_matrices(place, psf_coef[0], phases[0], col_shift, rows, width, segments)
    weight = exposure_weight.astype(jnp.float32)

    chunks = []
    start = 0
    for part in PARTS:
        chunks.append((start, half_cols // part))
        start += half_cols // part
    sent = [
        filter_chunk(weight, low, image, high, rows_m, cols_m, start, chunk, segments) for start, chunk in chunks
    ]

    other_offset = swapped(band_offset, "core", 1)
    facts = jnp.stack([col_shift.astype(jnp.float32), band_offset.astype(jnp.float32), weight], axis=1)
    facts = jnp.concatenate([facts, swapped(facts, "core", 1)], axis=0)
    step = 1
    while step < lines:
        facts = jnp.concatenate([facts, swapped(facts, "line", step)], axis=0)
        step *= 2
    scale = patch_weights(place, patch_site, facts, slots, quarter, cores, width, bands)

    result = None
    for (start, chunk), outgoing in zip(chunks, sent):
        mine = [outgoing[0]] + [swapped(outgoing[d], "seg", d) for d in range(1, segments)]
        other = [swapped(block, "core", 1) for block in mine]
        pieces = pair_sum(
            place, band_offset, other_offset, patch_site, mine, other, slots, lines, cores, quarter
        )
        result = finish_chunk(scatter_sum(pieces), scale, result, start)
    return result.reshape(slots, quarter, half_cols)


def solution(mesh):
    segments, exposures = mesh.shape["seg"], mesh.shape["exp"]
    parted = Mesh(mesh.devices.reshape(segments, exposures // 2, 2), ("seg", "line", "core"))
    spread = ("line", "core")
    placed = (
        P(spread, "seg", None),
        P(spread, None, None),
        P(spread, None),
        P(spread),
        P(spread),
        P(spread),
        P(),
    )
    return jax.shard_map(
        per_device, mesh=parted, in_specs=placed, out_specs=P(spread, "seg", None), check_vma=False
    )
```

```python
import functools

import jax
import jax.numpy as jnp
import numpy as np
from jax import lax
from jax.experimental import pallas as pl
from jax.experimental.pallas import tpu as pltpu
from jax.sharding import Mesh, PartitionSpec as P

BAND_ROWS = 32
TAPS = 21
PHASES = 16
LANCZOS = 6
SPAN = TAPS + LANCZOS - 1
LEAD = TAPS // 2 + 2
HALO = 16
SIDE = 128
TILE = 256
STRIP = 128
PARTS = (4, 4, 4, 4)
VMEM = 48 * 1024 * 1024
COST = pl.CostEstimate(flops=1, bytes_accessed=1, transcendentals=0)

sigmas = (1.0, 2.0, 3.5)


def basis_table():
    offsets = np.arange(TAPS) - TAPS // 2
    curves = [np.exp(-offsets * offsets / (2.0 * spread * spread)) for spread in sigmas]
    return [[float(value) for value in curve / curve.sum()] for curve in curves]


def lanczos_table():
    shifted = np.arange(LANCZOS)[None, :] - 2.0 - np.arange(PHASES)[:, None] / PHASES
    values = np.sinc(shifted) * np.sinc(shifted / 3.0)
    return (values / values.sum(axis=1, keepdims=True)).astype(np.float32)


def lanczos_taps(phase):
    table = lanczos_table()
    taps = []
    for n in range(LANCZOS):
        tap = jnp.float32(table[0, n])
        for index in range(1, PHASES):
            tap = jnp.where(phase == index, jnp.float32(table[index, n]), tap)
        taps.append(tap)
    return taps


def split(value):
    high = value.astype(jnp.bfloat16)
    return high, (value - high.astype(jnp.float32)).astype(jnp.bfloat16)


def banded(taps, mask_sets, distance):
    kernel, lanczos = taps
    sets = [[jnp.where(mask, lanczos[n], 0.0) for n, mask in enumerate(masks)] for masks in mask_sets]
    matrices = [jnp.zeros(distance.shape, jnp.float32) for _ in sets]
    for t in range(SPAN):
        here = distance == t
        for index, weighted in enumerate(sets):
            row = jnp.zeros_like(weighted[0])
            for n in range(LANCZOS):
                if 0 <= t - n < TAPS:
                    row = row + kernel[t - n] * weighted[n]
            matrices[index] = jnp.where(here, row, matrices[index])
    return matrices


def matrices_kernel(place, coef, phases, shift, rows_out, cols_out, *, rows, width, segments):
    basis = basis_table()

    def taps_of(axis):
        kernel = [sum(coef[0, axis, k] * basis[k][t] for k in range(len(sigmas))) for t in range(TAPS)]
        return kernel, lanczos_taps(phases[0, axis])

    def kept(matched, extent):
        return [(matched + (n - 2) >= 0) & (matched + (n - 2) < extent) for n in range(LANCZOS)]

    taps = taps_of(1)
    offset = shift[0]
    column = lax.broadcasted_iota(jnp.int32, (1, SIDE), 1)
    everything = [jnp.full((1, SIDE), True)] * LANCZOS
    mask_sets = [kept(column - offset, width), everything, kept(column + (width - SIDE) - offset, width)]
    for part, block in ((0, 3), (1, 0)):
        for variant in range(3):
            for term in range(2):
                place_out = (pl.ds(block * SIDE, SIDE), pl.ds(part * SIDE, SIDE))
                cols_out[(variant, term, *place_out)] = jnp.zeros((SIDE, SIDE), jnp.bfloat16)
    for step in range(3):
        distance = (
            lax.broadcasted_iota(jnp.int32, (SIDE, SIDE), 0)
            - lax.broadcasted_iota(jnp.int32, (SIDE, SIDE), 1)
            + (offset + LEAD - SIDE + step * SIDE)
        )
        pairs = [split(matrix) for matrix in banded(taps, mask_sets, distance)]
        for part in range(2):
            for variant in range(3):
                chosen = variant if variant == 2 * part else 1
                for term in range(2):
                    place_out = (pl.ds((part + step) * SIDE, SIDE), pl.ds(part * SIDE, SIDE))
                    cols_out[(variant, term, *place_out)] = pairs[chosen][term]

    taps = taps_of(0)
    span = STRIP + 2 * HALO
    quarter = BAND_ROWS // segments
    bands = STRIP // BAND_ROWS
    order = lax.broadcasted_iota(jnp.int32, (1, STRIP), 1)
    within = lax.rem(order, bands * quarter)
    owner = lax.div(order, bands * quarter) ^ place[0]
    output = lax.div(within, quarter) * BAND_ROWS + owner * quarter + lax.rem(within, quarter)
    distance = lax.broadcasted_iota(jnp.int32, (span, STRIP), 0) - output + (LEAD - HALO)
    mask_sets = [
        kept(place[0] * rows + first + output, rows * segments) for first in (0, STRIP, rows - STRIP)
    ]
    rest = jnp.zeros((cols_pad(3 * span) - 3 * span, STRIP), jnp.float32)
    for variant, matrix in enumerate(banded(taps, mask_sets, distance)):
        high = matrix.astype(jnp.bfloat16).astype(jnp.float32)
        stacked = jnp.concatenate([high, high, matrix - high, rest], axis=0).T
        rows_out[variant] = stacked.astype(jnp.bfloat16)[:, : 3 * span]


def cols_pad(count):
    return -(-count // 128) * 128


def build_matrices(place, coef, phases, shift, rows, width, segments):
    span = 3 * (STRIP + 2 * HALO)
    smem = pl.BlockSpec(memory_space=pltpu.SMEM)
    vmem = pl.BlockSpec(memory_space=pltpu.VMEM)
    return pl.pallas_call(
        functools.partial(matrices_kernel, rows=rows, width=width, segments=segments),
        out_shape=(
            jax.ShapeDtypeStruct((3, STRIP, span), jnp.bfloat16),
            jax.ShapeDtypeStruct((3, 2, TILE + 2 * SIDE, TILE), jnp.bfloat16),
        ),
        in_specs=[smem] * 4,
        out_specs=(vmem, vmem),
        compiler_params=pltpu.CompilerParams(vmem_limit_bytes=VMEM),
        cost_estimate=COST,
        name="band_matrices",
    )(place, coef, phases, shift)


def filter_kernel(
    weight, low_l, low_c, low_r, mid_l, mid_c, mid_r, high_l, high_c, high_r, rows_m, cols_m, *rest,
    first_chunk, last_chunk, segments,
):
    *outs, ext_high, ext_low, mat_high, mat_low = rest[-segments - 4 :]
    half = pl.program_id(0)
    halves = pl.num_programs(0)
    rows, chunk = mid_c.shape
    at_left = first_chunk & (half == 0)
    at_right = last_chunk & (half == halves - 1)
    span = STRIP + 2 * HALO

    for row, parts in (
        (0, (low_l, low_c, low_r)),
        (HALO, (mid_l, mid_c, mid_r)),
        (HALO + rows, (high_l, high_c, high_r)),
    ):
        count = parts[0].shape[0]
        for part, column, outside in zip(parts, (0, SIDE, SIDE + chunk), (at_left, False, at_right)):
            value = part[...]
            if outside is not False:
                value = jnp.where(outside, 0.0, value)
            high, low = split(value)
            place = (pl.ds(row, count), pl.ds(column, value.shape[1]))
            ext_high[place] = high
            ext_low[place] = low

    strips = rows // STRIP
    for tile in range((chunk + 2 * SIDE) // TILE):
        columns = pl.ds(tile * TILE, TILE)
        for strip in range(strips):
            window = pl.ds(strip * STRIP, span)
            variant = 0 if strip == 0 else (2 if strip == strips - 1 else 1)
            high = ext_high[window, columns]
            stack = jnp.concatenate([high, ext_low[window, columns], high], axis=0)
            matched = jnp.dot(rows_m[variant], stack, preferred_element_type=jnp.float32)
            high, low = split(matched)
            mat_high[pl.ds(strip * STRIP, STRIP), columns] = high
            mat_low[pl.ds(strip * STRIP, STRIP), columns] = low

    tiles = chunk // TILE
    piece = STRIP // segments
    for tile in range(tiles):
        variant = jnp.int32(1)
        if tile == 0:
            variant = jnp.where(at_left, 0, variant)
        if tile == tiles - 1:
            variant = jnp.where(at_right, 2, variant)
        taps_high = cols_m[variant, 0]
        taps_low = cols_m[variant, 1]
        window = pl.ds(tile * TILE, TILE + 2 * SIDE)
        for strip in range(strips):
            place = pl.ds(strip * STRIP, STRIP)
            high = mat_high[place, window]
            warped = jnp.dot(high, taps_high, preferred_element_type=jnp.float32)
            warped += jnp.dot(mat_low[place, window], taps_high, preferred_element_type=jnp.float32)
            warped += jnp.dot(high, taps_low, preferred_element_type=jnp.float32)
            sent = (weight[0] * warped).astype(jnp.bfloat16)
            for owner, out in enumerate(outs):
                out[pl.ds(strip * piece, piece), pl.ds(tile * TILE, TILE)] = sent[owner * piece : (owner + 1) * piece]


def filter_chunk(weight, low, image, high, rows_m, cols_m, after, start, chunk, segments):
    rows, width = image.shape
    halves = 2
    half_blocks = width // halves // SIDE
    first = start // SIDE
    blocks = chunk // SIDE
    last = width // SIDE - 1

    def left(h):
        return 0, jnp.maximum(h * half_blocks + first - 1, 0)

    def centre(h):
        return 0, h * (half_blocks // blocks) + start // chunk

    def right(h):
        return 0, jnp.minimum(h * half_blocks + first + blocks, last)

    def whole(array):
        return pl.BlockSpec(array.shape, lambda h: (0,) * array.ndim)

    specs = [pl.BlockSpec(memory_space=pltpu.SMEM)]
    for source in (low, image, high):
        specs += [
            pl.BlockSpec((source.shape[0], SIDE), left),
            pl.BlockSpec((source.shape[0], chunk), centre),
            pl.BlockSpec((source.shape[0], SIDE), right),
        ]
    wide = chunk + 2 * SIDE
    return pl.pallas_call(
        functools.partial(
            filter_kernel,
            first_chunk=start == 0,
            last_chunk=start + chunk == width // halves,
            segments=segments,
        ),
        out_shape=[jax.ShapeDtypeStruct((rows // segments, halves * chunk), jnp.bfloat16)] * segments,
        grid=(halves,),
        in_specs=specs + [whole(rows_m), whole(cols_m)] + [pl.BlockSpec(memory_space=pl.ANY)] * len(after),
        out_specs=[pl.BlockSpec((rows // segments, chunk), lambda h: (0, h))] * segments,
        scratch_shapes=[
            pltpu.VMEM((rows + 2 * HALO, wide), jnp.bfloat16),
            pltpu.VMEM((rows + 2 * HALO, wide), jnp.bfloat16),
            pltpu.VMEM((rows, wide), jnp.bfloat16),
            pltpu.VMEM((rows, wide), jnp.bfloat16),
        ],
        compiler_params=pltpu.CompilerParams(vmem_limit_bytes=VMEM),
        cost_estimate=COST,
        name="warp_filter",
    )(weight, *([low] * 3), *([image] * 3), *([high] * 3), rows_m, cols_m, *after)


def join_kernel(*refs):
    block = refs[0].shape[0]
    for step, ref in enumerate(refs[:-1]):
        refs[-1][pl.ds(step * block, block), :] = ref[...]


def joined(blocks):
    block, columns = blocks[0].shape
    vmem = pl.BlockSpec(memory_space=pltpu.VMEM)
    return pl.pallas_call(
        join_kernel,
        out_shape=jax.ShapeDtypeStruct((len(blocks) * block, columns), blocks[0].dtype),
        in_specs=[vmem] * len(blocks),
        out_specs=vmem,
        compiler_params=pltpu.CompilerParams(vmem_limit_bytes=VMEM),
        cost_estimate=COST,
        name="join_blocks",
    )(*blocks)


def groups_of(lines):
    groups = []
    step = 1
    while step < lines:
        groups.append(list(range(step, lines, 2 * step)))
        step *= 2
    return groups + [[0]]


def pair_kernel(place, table, mine, other, *rest, slots, groups, quarter):
    outs, (mine_all, other_all) = rest[: len(groups)], rest[len(groups) :]
    rows = mine.shape[0]
    chunk = outs[0].shape[2]
    count = table.shape[0] // 3
    for source, held in ((mine, mine_all), (other, other_all)):
        held[pl.ds(0, rows), :] = source[...].astype(jnp.float32)
        held[pl.ds(rows, quarter), :] = jnp.zeros((quarter, source.shape[1]), jnp.float32)
    line = place[1]

    for group, out in zip(groups, outs):
        for index, distance in enumerate(group):
            first = (line ^ distance) * slots

            def summed(slot, first=first):
                column = pl.ds(pl.multiple_of(table[first + slot] * chunk, 128), chunk)
                from_mine = pl.ds(pl.multiple_of(table[count + first + slot], quarter), quarter)
                from_other = pl.ds(pl.multiple_of(table[2 * count + first + slot], quarter), quarter)
                return mine_all[from_mine, column] + other_all[from_other, column]

            for slot in range(0, slots - 1, 2):
                rows_two = jnp.concatenate([summed(slot), summed(slot + 1)], axis=0)
                out[index, pl.ds(slot * quarter, 2 * quarter), :] = rows_two.astype(jnp.bfloat16)
            if slots % 2:
                out[index, pl.ds((slots - 1) * quarter, quarter), :] = summed(slots - 1).astype(jnp.bfloat16)


def pair_sum(place, table, mine, other, after, slots, lines, quarter):
    rows, double = mine.shape
    chunk = double // 2
    groups = groups_of(lines)
    smem = pl.BlockSpec(memory_space=pltpu.SMEM)
    vmem = pl.BlockSpec(memory_space=pltpu.VMEM)

    def kernel(*refs):
        pair_kernel(*refs[:4], *refs[4 + len(after) :], slots=slots, groups=groups, quarter=quarter)

    return pl.pallas_call(
        kernel,
        out_shape=[jax.ShapeDtypeStruct((len(group), slots * quarter, chunk), jnp.bfloat16) for group in groups],
        in_specs=[smem, smem, vmem, vmem] + [pl.BlockSpec(memory_space=pl.ANY)] * len(after),
        out_specs=[vmem] * len(groups),
        scratch_shapes=[pltpu.VMEM((rows + quarter, double), jnp.float32)] * 2,
        compiler_params=pltpu.CompilerParams(vmem_limit_bytes=VMEM),
        cost_estimate=COST,
        name="pair_sum",
    )(place, table, mine, other, *after)


def weight_kernel(place, sites, facts, out, covers, *, cores, quarter, width, bands):
    slots = out.shape[0] // quarter
    half_cols = out.shape[1]
    exposures = facts.shape[0]
    owner = place[1] * cores + place[2]
    column = lax.broadcasted_iota(jnp.int32, (quarter, half_cols), 1)
    for half in range(2):
        for exposure in range(exposures):
            first = facts[exposure, 0].astype(jnp.int32) - half * half_cols
            inside = (column >= first) & (column < first + width)
            covers[half * exposures + exposure] = jnp.where(inside, facts[exposure, 2], 0.0)

    def one_slot(slot, carry):
        site = sites[owner * slots + slot]
        total = jnp.zeros((quarter, half_cols), jnp.float32)
        for exposure in range(exposures):
            relative = lax.shift_right_logical(site, 1) - facts[exposure, 1].astype(jnp.int32)
            present = jnp.where((relative >= 0) & (relative < bands), jnp.float32(1.0), jnp.float32(0.0))
            total = total + present * covers[(site & 1) * exposures + exposure]
        out[pl.ds(pl.multiple_of(slot * quarter, quarter), quarter), :] = jnp.maximum(total, 1.0)
        return carry

    lax.fori_loop(0, slots, one_slot, 0)


def patch_weights(place, sites, facts, slots, quarter, cores, width, bands):
    smem = pl.BlockSpec(memory_space=pltpu.SMEM)
    return pl.pallas_call(
        functools.partial(weight_kernel, cores=cores, quarter=quarter, width=width, bands=bands),
        out_shape=jax.ShapeDtypeStruct((slots * quarter, width // 2), jnp.float32),
        in_specs=[smem] * 3,
        out_specs=pl.BlockSpec(memory_space=pltpu.VMEM),
        scratch_shapes=[pltpu.VMEM((2 * facts.shape[0], quarter, width // 2), jnp.float32)],
        compiler_params=pltpu.CompilerParams(vmem_limit_bytes=VMEM),
        cost_estimate=COST,
        name="patch_weights",
    )(place, sites, facts)


def finish_kernel(*refs, count):
    pieces, scale, out = refs[:count], refs[count], refs[-1]
    total = pieces[0][...].astype(jnp.float32)
    for piece in pieces[1:]:
        total += piece[...].astype(jnp.float32)
    out[...] = total / scale[...]


def finish_chunk(pieces, scale, result, start):
    _, rows, chunk = pieces[0].shape
    column = pl.BlockSpec((rows, chunk), lambda i: (0, start // chunk))
    specs = [pl.BlockSpec((None, rows, chunk), lambda i: (0, 0, 0))] * len(pieces) + [column]
    operands = [*pieces, scale]
    aliases = {}
    if result is not None:
        specs.append(pl.BlockSpec(memory_space=pl.ANY))
        aliases = {len(operands): 0}
        operands.append(result)
    return pl.pallas_call(
        functools.partial(finish_kernel, count=len(pieces)),
        out_shape=jax.ShapeDtypeStruct(scale.shape, jnp.float32),
        grid=(1,),
        in_specs=specs,
        out_specs=column,
        input_output_aliases=aliases,
        compiler_params=pltpu.CompilerParams(vmem_limit_bytes=VMEM),
        cost_estimate=pl.CostEstimate(
            flops=len(pieces) * rows * chunk, bytes_accessed=rows * chunk * (2 * len(pieces) + 8), transcendentals=0
        ),
        name="patch_mean",
    )(*operands)


def swapped(value, axis, distance):
    count = lax.axis_size(axis)
    return lax.ppermute(value, axis, [(i, i ^ distance) for i in range(count)])


def scatter_sum(pieces):
    pieces = list(pieces)
    kept = [pieces[-1]]
    for stage in range(len(pieces) - 1):
        received = swapped(pieces[stage], "line", 1 << stage)
        kept.append(received)
        for later in range(stage + 1, len(pieces) - 1):
            step = 1 << (later - stage - 1)
            part = received[step :: 2 * step].astype(jnp.float32)
            pieces[later] = (pieces[later].astype(jnp.float32) + part).astype(jnp.bfloat16)
    return kept, pieces[-2]


def per_device(images, psf_coef, phases, col_shift, band_offset, exposure_weight, patch_site):
    image = images[0]
    rows, width = image.shape
    segments = lax.axis_size("seg")
    lines = lax.axis_size("line")
    cores = lax.axis_size("core")
    quarter = BAND_ROWS // segments
    half_cols = width // 2
    slots = patch_site.shape[0] // (lines * cores)
    bands = segments * rows // BAND_ROWS
    place = jnp.stack([lax.axis_index(axis) for axis in ("seg", "line", "core")]).astype(jnp.int32)

    forward = [(i, i + 1) for i in range(segments - 1)]
    backward = [(i + 1, i) for i in range(segments - 1)]
    low = lax.ppermute(image[rows - HALO :], "seg", forward)
    high = lax.ppermute(image[:HALO], "seg", backward)
    rows_m, cols_m = build_matrices(place, psf_coef, phases, col_shift, rows, width, segments)
    weight = exposure_weight.astype(jnp.float32)

    chunks = []
    start = 0
    for part in PARTS:
        chunks.append((start, half_cols // part))
        start += half_cols // part
    other_offset = swapped(band_offset, "core", 1)
    sites = lax.dynamic_index_in_dim(patch_site.reshape(lines, cores, slots), place[2], 1, keepdims=False).reshape(-1)
    here = rows // BAND_ROWS

    def rows_from(offset):
        relative = sites // 2 - offset
        held = ((relative // here) ^ place[0]) * here + relative % here
        return jnp.where((relative >= 0) & (relative < bands), held, bands) * quarter

    table = jnp.concatenate([sites % 2, rows_from(band_offset), rows_from(other_offset)])
    facts = jnp.stack([col_shift.astype(jnp.float32), band_offset.astype(jnp.float32), weight], axis=1)
    facts = jnp.concatenate([facts, swapped(facts, "core", 1)], axis=0)
    early = facts
    step = 1
    while step < lines:
        early = facts
        facts = jnp.concatenate([facts, swapped(facts, "line", step)], axis=0)
        step *= 2
    scale = patch_weights(place, patch_site, facts, slots, quarter, cores, width, bands)

    def tied(values, others):
        return lax.optimization_barrier((values, others))[0]

    result = None
    count = len(chunks)
    sent, sums, partial, kept = [None] * count, [None] * count, [None] * count, [None] * count

    def filtered(index):
        start, chunk = chunks[index]
        sent[index] = filter_chunk(weight, low, image, high, rows_m, cols_m, [], start, chunk, segments)

    filtered(0)
    for index, (start, chunk) in enumerate(chunks):
        outgoing = sent[index]
        received = [swapped(outgoing[d], "seg", d) for d in range(1, segments)]
        if index + 1 < count:
            filtered(index + 1)
            received = tied(received, sent[index + 1])
        if index == 0:
            received = tied(received, early)
        if index == 1:
            received = tied(received, scale)
        if index >= 1:
            received = tied(received, partial[index - 1])
        if index >= 2:
            received = tied(received, kept[index - 2])
        mine = joined([outgoing[0]] + received)
        other = swapped(mine, "core", 1)
        sums[index] = pair_sum(place, table, mine, other, [], slots, lines, quarter)
        kept[index], partial[index] = scatter_sum(sums[index])
        result = finish_chunk(kept[index], scale, result, start)
    return result.reshape(slots, quarter, half_cols)


def solution(mesh):
    segments, exposures = mesh.shape["seg"], mesh.shape["exp"]
    parted = Mesh(mesh.devices.reshape(segments, exposures // 2, 2), ("seg", "line", "core"))
    spread = ("line", "core")
    placed = (
        P(spread, "seg", None),
        P(spread, None, None),
        P(spread, None),
        P(spread),
        P(spread),
        P(spread),
        P(),
    )
    return jax.shard_map(
        per_device, mesh=parted, in_specs=placed, out_specs=P(spread, "seg", None), check_vma=False
    )
```

```python
import functools

import jax
import jax.numpy as jnp
import numpy as np
from jax import lax
from jax.experimental import pallas as pl
from jax.experimental.pallas import tpu as pltpu
from jax.sharding import Mesh, PartitionSpec as P

BAND_ROWS = 32
TAPS = 21
PHASES = 16
LANCZOS = 6
SPAN = TAPS + LANCZOS - 1
LEAD = TAPS // 2 + 2
HALO = 16
SIDE = 128
TILE = 256
STRIP = 128
PARTS = (4, 4, 4, 4)
VMEM = 48 * 1024 * 1024
COST = pl.CostEstimate(flops=1, bytes_accessed=1, transcendentals=0)

sigmas = (1.0, 2.0, 3.5)


def basis_table():
    offsets = np.arange(TAPS) - TAPS // 2
    curves = [np.exp(-offsets * offsets / (2.0 * spread * spread)) for spread in sigmas]
    return [[float(value) for value in curve / curve.sum()] for curve in curves]


def lanczos_table():
    shifted = np.arange(LANCZOS)[None, :] - 2.0 - np.arange(PHASES)[:, None] / PHASES
    values = np.sinc(shifted) * np.sinc(shifted / 3.0)
    return (values / values.sum(axis=1, keepdims=True)).astype(np.float32)


def lanczos_taps(phase):
    table = lanczos_table()
    taps = []
    for n in range(LANCZOS):
        tap = jnp.float32(table[0, n])
        for index in range(1, PHASES):
            tap = jnp.where(phase == index, jnp.float32(table[index, n]), tap)
        taps.append(tap)
    return taps


def split(value):
    high = value.astype(jnp.bfloat16)
    return high, (value - high.astype(jnp.float32)).astype(jnp.bfloat16)


def banded(taps, mask_sets, distance):
    kernel, lanczos = taps
    sets = [[jnp.where(mask, lanczos[n], 0.0) for n, mask in enumerate(masks)] for masks in mask_sets]
    matrices = [jnp.zeros(distance.shape, jnp.float32) for _ in sets]
    for t in range(SPAN):
        here = distance == t
        for index, weighted in enumerate(sets):
            row = jnp.zeros_like(weighted[0])
            for n in range(LANCZOS):
                if 0 <= t - n < TAPS:
                    row = row + kernel[t - n] * weighted[n]
            matrices[index] = jnp.where(here, row, matrices[index])
    return matrices


def matrices_kernel(place, coef, phases, shift, rows_out, cols_out, *, rows, width, segments):
    basis = basis_table()

    def taps_of(axis):
        kernel = [sum(coef[0, axis, k] * basis[k][t] for k in range(len(sigmas))) for t in range(TAPS)]
        return kernel, lanczos_taps(phases[0, axis])

    def kept(matched, extent):
        return [(matched + (n - 2) >= 0) & (matched + (n - 2) < extent) for n in range(LANCZOS)]

    taps = taps_of(1)
    offset = shift[0]
    column = lax.broadcasted_iota(jnp.int32, (1, SIDE), 1)
    everything = [jnp.full((1, SIDE), True)] * LANCZOS
    mask_sets = [kept(column - offset, width), everything, kept(column + (width - SIDE) - offset, width)]
    for part, block in ((0, 3), (1, 0)):
        for variant in range(3):
            for term in range(2):
                place_out = (pl.ds(block * SIDE, SIDE), pl.ds(part * SIDE, SIDE))
                cols_out[(variant, term, *place_out)] = jnp.zeros((SIDE, SIDE), jnp.bfloat16)
    for step in range(3):
        distance = (
            lax.broadcasted_iota(jnp.int32, (SIDE, SIDE), 0)
            - lax.broadcasted_iota(jnp.int32, (SIDE, SIDE), 1)
            + (offset + LEAD - SIDE + step * SIDE)
        )
        pairs = [split(matrix) for matrix in banded(taps, mask_sets, distance)]
        for part in range(2):
            for variant in range(3):
                chosen = variant if variant == 2 * part else 1
                for term in range(2):
                    place_out = (pl.ds((part + step) * SIDE, SIDE), pl.ds(part * SIDE, SIDE))
                    cols_out[(variant, term, *place_out)] = pairs[chosen][term]

    taps = taps_of(0)
    span = STRIP + 2 * HALO
    quarter = BAND_ROWS // segments
    bands = STRIP // BAND_ROWS
    order = lax.broadcasted_iota(jnp.int32, (1, STRIP), 1)
    within = lax.rem(order, bands * quarter)
    owner = lax.div(order, bands * quarter) ^ place[0]
    output = lax.div(within, quarter) * BAND_ROWS + owner * quarter + lax.rem(within, quarter)
    distance = lax.broadcasted_iota(jnp.int32, (span, STRIP), 0) - output + (LEAD - HALO)
    mask_sets = [
        kept(place[0] * rows + first + output, rows * segments) for first in (0, STRIP, rows - STRIP)
    ]
    rest = jnp.zeros((cols_pad(3 * span) - 3 * span, STRIP), jnp.float32)
    for variant, matrix in enumerate(banded(taps, mask_sets, distance)):
        high = matrix.astype(jnp.bfloat16).astype(jnp.float32)
        stacked = jnp.concatenate([high, high, matrix - high, rest], axis=0).T
        rows_out[variant] = stacked.astype(jnp.bfloat16)[:, : 3 * span]


def cols_pad(count):
    return -(-count // 128) * 128


def build_matrices(place, coef, phases, shift, rows, width, segments):
    span = 3 * (STRIP + 2 * HALO)
    smem = pl.BlockSpec(memory_space=pltpu.SMEM)
    vmem = pl.BlockSpec(memory_space=pltpu.VMEM)
    return pl.pallas_call(
        functools.partial(matrices_kernel, rows=rows, width=width, segments=segments),
        out_shape=(
            jax.ShapeDtypeStruct((3, STRIP, span), jnp.bfloat16),
            jax.ShapeDtypeStruct((3, 2, TILE + 2 * SIDE, TILE), jnp.bfloat16),
        ),
        in_specs=[smem] * 4,
        out_specs=(vmem, vmem),
        compiler_params=pltpu.CompilerParams(vmem_limit_bytes=VMEM),
        cost_estimate=COST,
        name="band_matrices",
    )(place, coef, phases, shift)


def filter_kernel(
    weight, low_l, low_c, low_r, mid_l, mid_c, mid_r, high_l, high_c, high_r, rows_m, cols_m, *rest,
    first_chunk, last_chunk, segments,
):
    *outs, ext_high, ext_low, mat_high, mat_low = rest[-segments - 4 :]
    half = pl.program_id(0)
    halves = pl.num_programs(0)
    rows, chunk = mid_c.shape
    at_left = first_chunk & (half == 0)
    at_right = last_chunk & (half == halves - 1)
    span = STRIP + 2 * HALO

    for row, parts in (
        (0, (low_l, low_c, low_r)),
        (HALO, (mid_l, mid_c, mid_r)),
        (HALO + rows, (high_l, high_c, high_r)),
    ):
        count = parts[0].shape[0]
        for part, column, outside in zip(parts, (0, SIDE, SIDE + chunk), (at_left, False, at_right)):
            value = part[...]
            if outside is not False:
                value = jnp.where(outside, 0.0, value)
            high, low = split(value)
            place = (pl.ds(row, count), pl.ds(column, value.shape[1]))
            ext_high[place] = high
            ext_low[place] = low

    strips = rows // STRIP
    for tile in range((chunk + 2 * SIDE) // TILE):
        columns = pl.ds(tile * TILE, TILE)
        for strip in range(strips):
            window = pl.ds(strip * STRIP, span)
            variant = 0 if strip == 0 else (2 if strip == strips - 1 else 1)
            high = ext_high[window, columns]
            stack = jnp.concatenate([high, ext_low[window, columns], high], axis=0)
            matched = jnp.dot(rows_m[variant], stack, preferred_element_type=jnp.float32)
            high, low = split(matched)
            mat_high[pl.ds(strip * STRIP, STRIP), columns] = high
            mat_low[pl.ds(strip * STRIP, STRIP), columns] = low

    tiles = chunk // TILE
    piece = STRIP // segments
    for tile in range(tiles):
        variant = jnp.int32(1)
        if tile == 0:
            variant = jnp.where(at_left, 0, variant)
        if tile == tiles - 1:
            variant = jnp.where(at_right, 2, variant)
        taps_high = cols_m[variant, 0]
        taps_low = cols_m[variant, 1]
        window = pl.ds(tile * TILE, TILE + 2 * SIDE)
        for strip in range(strips):
            place = pl.ds(strip * STRIP, STRIP)
            high = mat_high[place, window]
            warped = jnp.dot(high, taps_high, preferred_element_type=jnp.float32)
            warped += jnp.dot(mat_low[place, window], taps_high, preferred_element_type=jnp.float32)
            warped += jnp.dot(high, taps_low, preferred_element_type=jnp.float32)
            sent = (weight[0] * warped).astype(jnp.bfloat16)
            for owner, out in enumerate(outs):
                out[pl.ds(strip * piece, piece), pl.ds(tile * TILE, TILE)] = sent[owner * piece : (owner + 1) * piece]


def filter_chunk(weight, low, image, high, rows_m, cols_m, after, start, chunk, segments):
    rows, width = image.shape
    halves = 2
    half_blocks = width // halves // SIDE
    first = start // SIDE
    blocks = chunk // SIDE
    last = width // SIDE - 1

    def left(h):
        return 0, jnp.maximum(h * half_blocks + first - 1, 0)

    def centre(h):
        return 0, h * (half_blocks // blocks) + start // chunk

    def right(h):
        return 0, jnp.minimum(h * half_blocks + first + blocks, last)

    def whole(array):
        return pl.BlockSpec(array.shape, lambda h: (0,) * array.ndim)

    specs = [pl.BlockSpec(memory_space=pltpu.SMEM)]
    for source in (low, image, high):
        specs += [
            pl.BlockSpec((source.shape[0], SIDE), left),
            pl.BlockSpec((source.shape[0], chunk), centre),
            pl.BlockSpec((source.shape[0], SIDE), right),
        ]
    wide = chunk + 2 * SIDE
    return pl.pallas_call(
        functools.partial(
            filter_kernel,
            first_chunk=start == 0,
            last_chunk=start + chunk == width // halves,
            segments=segments,
        ),
        out_shape=[jax.ShapeDtypeStruct((rows // segments, halves * chunk), jnp.bfloat16)] * segments,
        grid=(halves,),
        in_specs=specs + [whole(rows_m), whole(cols_m)] + [pl.BlockSpec(memory_space=pl.ANY)] * len(after),
        out_specs=[pl.BlockSpec((rows // segments, chunk), lambda h: (0, h))] * segments,
        scratch_shapes=[
            pltpu.VMEM((rows + 2 * HALO, wide), jnp.bfloat16),
            pltpu.VMEM((rows + 2 * HALO, wide), jnp.bfloat16),
            pltpu.VMEM((rows, wide), jnp.bfloat16),
            pltpu.VMEM((rows, wide), jnp.bfloat16),
        ],
        compiler_params=pltpu.CompilerParams(vmem_limit_bytes=VMEM),
        cost_estimate=COST,
        name="warp_filter",
    )(weight, *([low] * 3), *([image] * 3), *([high] * 3), rows_m, cols_m, *after)


def join_kernel(*refs):
    block = refs[0].shape[0]
    for step, ref in enumerate(refs[:-1]):
        refs[-1][pl.ds(step * block, block), :] = ref[...]


def joined(blocks):
    block, columns = blocks[0].shape
    vmem = pl.BlockSpec(memory_space=pltpu.VMEM)
    return pl.pallas_call(
        join_kernel,
        out_shape=jax.ShapeDtypeStruct((len(blocks) * block, columns), blocks[0].dtype),
        in_specs=[vmem] * len(blocks),
        out_specs=vmem,
        compiler_params=pltpu.CompilerParams(vmem_limit_bytes=VMEM),
        cost_estimate=COST,
        name="join_blocks",
    )(*blocks)


def groups_of(lines):
    return [list(range(lines))]


def pair_kernel(place, table, mine, other, *rest, slots, groups, quarter):
    outs, (mine_all, other_all) = rest[: len(groups)], rest[len(groups) :]
    rows = mine.shape[0]
    chunk = outs[0].shape[2]
    count = table.shape[0] // 3
    for source, held in ((mine, mine_all), (other, other_all)):
        held[pl.ds(0, rows), :] = source[...].astype(jnp.float32)
        held[pl.ds(rows, quarter), :] = jnp.zeros((quarter, source.shape[1]), jnp.float32)
    line = place[1]

    for group, out in zip(groups, outs):
        for index, distance in enumerate(group):
            first = distance * slots

            def summed(slot, first=first):
                column = pl.ds(pl.multiple_of(table[first + slot] * chunk, 128), chunk)
                from_mine = pl.ds(pl.multiple_of(table[count + first + slot], quarter), quarter)
                from_other = pl.ds(pl.multiple_of(table[2 * count + first + slot], quarter), quarter)
                return mine_all[from_mine, column] + other_all[from_other, column]

            for slot in range(0, slots - 1, 2):
                rows_two = jnp.concatenate([summed(slot), summed(slot + 1)], axis=0)
                out[index, pl.ds(slot * quarter, 2 * quarter), :] = rows_two.astype(jnp.bfloat16)
            if slots % 2:
                out[index, pl.ds((slots - 1) * quarter, quarter), :] = summed(slots - 1).astype(jnp.bfloat16)


def pair_sum(place, table, mine, other, after, slots, lines, quarter):
    rows, double = mine.shape
    chunk = double // 2
    groups = groups_of(lines)
    smem = pl.BlockSpec(memory_space=pltpu.SMEM)
    vmem = pl.BlockSpec(memory_space=pltpu.VMEM)

    def kernel(*refs):
        pair_kernel(*refs[:4], *refs[4 + len(after) :], slots=slots, groups=groups, quarter=quarter)

    return pl.pallas_call(
        kernel,
        out_shape=[jax.ShapeDtypeStruct((len(group), slots * quarter, chunk), jnp.bfloat16) for group in groups],
        in_specs=[smem, smem, vmem, vmem] + [pl.BlockSpec(memory_space=pl.ANY)] * len(after),
        out_specs=[vmem] * len(groups),
        scratch_shapes=[pltpu.VMEM((rows + quarter, double), jnp.float32)] * 2,
        compiler_params=pltpu.CompilerParams(vmem_limit_bytes=VMEM),
        cost_estimate=COST,
        name="pair_sum",
    )(place, table, mine, other, *after)


def weight_kernel(place, sites, facts, out, covers, *, cores, quarter, width, bands):
    slots = out.shape[0] // quarter
    half_cols = out.shape[1]
    exposures = facts.shape[0]
    owner = place[1] * cores + place[2]
    column = lax.broadcasted_iota(jnp.int32, (quarter, half_cols), 1)
    for half in range(2):
        for exposure in range(exposures):
            first = facts[exposure, 0].astype(jnp.int32) - half * half_cols
            inside = (column >= first) & (column < first + width)
            covers[half * exposures + exposure] = jnp.where(inside, facts[exposure, 2], 0.0)

    def one_slot(slot, carry):
        site = sites[owner * slots + slot]
        total = jnp.zeros((quarter, half_cols), jnp.float32)
        for exposure in range(exposures):
            relative = lax.shift_right_logical(site, 1) - facts[exposure, 1].astype(jnp.int32)
            present = jnp.where((relative >= 0) & (relative < bands), jnp.float32(1.0), jnp.float32(0.0))
            total = total + present * covers[(site & 1) * exposures + exposure]
        out[pl.ds(pl.multiple_of(slot * quarter, quarter), quarter), :] = jnp.maximum(total, 1.0)
        return carry

    lax.fori_loop(0, slots, one_slot, 0)


def patch_weights(place, sites, facts, slots, quarter, cores, width, bands):
    smem = pl.BlockSpec(memory_space=pltpu.SMEM)
    return pl.pallas_call(
        functools.partial(weight_kernel, cores=cores, quarter=quarter, width=width, bands=bands),
        out_shape=jax.ShapeDtypeStruct((slots * quarter, width // 2), jnp.float32),
        in_specs=[smem] * 3,
        out_specs=pl.BlockSpec(memory_space=pltpu.VMEM),
        scratch_shapes=[pltpu.VMEM((2 * facts.shape[0], quarter, width // 2), jnp.float32)],
        compiler_params=pltpu.CompilerParams(vmem_limit_bytes=VMEM),
        cost_estimate=COST,
        name="patch_weights",
    )(place, sites, facts)


def finish_kernel(*refs, count):
    pieces, scale, out = refs[:count], refs[count], refs[-1]
    total = pieces[0][...].astype(jnp.float32)
    for piece in pieces[1:]:
        total += piece[...].astype(jnp.float32)
    out[...] = total / scale[...]


def finish_chunk(pieces, scale, result, start):
    _, rows, chunk = pieces[0].shape
    column = pl.BlockSpec((rows, chunk), lambda i: (0, start // chunk))
    specs = [pl.BlockSpec((None, rows, chunk), lambda i: (0, 0, 0))] * len(pieces) + [column]
    operands = [*pieces, scale]
    aliases = {}
    if result is not None:
        specs.append(pl.BlockSpec(memory_space=pl.ANY))
        aliases = {len(operands): 0}
        operands.append(result)
    return pl.pallas_call(
        functools.partial(finish_kernel, count=len(pieces)),
        out_shape=jax.ShapeDtypeStruct(scale.shape, jnp.float32),
        grid=(1,),
        in_specs=specs,
        out_specs=column,
        input_output_aliases=aliases,
        compiler_params=pltpu.CompilerParams(vmem_limit_bytes=VMEM),
        cost_estimate=pl.CostEstimate(
            flops=len(pieces) * rows * chunk, bytes_accessed=rows * chunk * (2 * len(pieces) + 8), transcendentals=0
        ),
        name="patch_mean",
    )(*operands)


def swapped(value, axis, distance):
    count = lax.axis_size(axis)
    return lax.ppermute(value, axis, [(i, i ^ distance) for i in range(count)])


def scatter_sum(pieces):
    return lax.psum_scatter(pieces, "line", scatter_dimension=0, tiled=True)


def per_device(images, psf_coef, phases, col_shift, band_offset, exposure_weight, patch_site):
    image = images[0]
    rows, width = image.shape
    segments = lax.axis_size("seg")
    lines = lax.axis_size("line")
    cores = lax.axis_size("core")
    quarter = BAND_ROWS // segments
    half_cols = width // 2
    slots = patch_site.shape[0] // (lines * cores)
    bands = segments * rows // BAND_ROWS
    place = jnp.stack([lax.axis_index(axis) for axis in ("seg", "line", "core")]).astype(jnp.int32)

    forward = [(i, i + 1) for i in range(segments - 1)]
    backward = [(i + 1, i) for i in range(segments - 1)]
    low = lax.ppermute(image[rows - HALO :], "seg", forward)
    high = lax.ppermute(image[:HALO], "seg", backward)
    rows_m, cols_m = build_matrices(place, psf_coef, phases, col_shift, rows, width, segments)
    weight = exposure_weight.astype(jnp.float32)

    chunks = []
    start = 0
    for part in PARTS:
        chunks.append((start, half_cols // part))
        start += half_cols // part
    other_offset = swapped(band_offset, "core", 1)
    sites = lax.dynamic_index_in_dim(patch_site.reshape(lines, cores, slots), place[2], 1, keepdims=False).reshape(-1)
    here = rows // BAND_ROWS

    def rows_from(offset):
        relative = sites // 2 - offset
        held = ((relative // here) ^ place[0]) * here + relative % here
        return jnp.where((relative >= 0) & (relative < bands), held, bands) * quarter

    table = jnp.concatenate([sites % 2, rows_from(band_offset), rows_from(other_offset)])
    facts = jnp.stack([col_shift.astype(jnp.float32), band_offset.astype(jnp.float32), weight], axis=1)
    facts = jnp.concatenate([facts, swapped(facts, "core", 1)], axis=0)
    early = facts
    step = 1
    while step < lines:
        early = facts
        facts = jnp.concatenate([facts, swapped(facts, "line", step)], axis=0)
        step *= 2
    scale = patch_weights(place, patch_site, facts, slots, quarter, cores, width, bands)

    def tied(values, others):
        return lax.optimization_barrier((values, others))[0]

    result = None
    count = len(chunks)
    sent, sums, kept = [None] * count, [None] * count, [None] * count

    def filtered(index):
        start, chunk = chunks[index]
        held = tied(weight, sums[index - 2]) if index >= 2 else weight
        sent[index] = filter_chunk(held, low, image, high, rows_m, cols_m, [], start, chunk, segments)

    filtered(0)
    for index, (start, chunk) in enumerate(chunks):
        outgoing = sent[index]
        received = [swapped(outgoing[d], "seg", d) for d in range(1, segments)]
        if index + 1 < count:
            filtered(index + 1)
            received = tied(received, sent[index + 1])
        if index == 0:
            received = tied(received, early)
        if index == 1:
            received = tied(received, scale)
        if index >= 1:
            received = tied(received, sums[index - 1])
        if index >= 2:
            received = tied(received, kept[index - 2])
        mine = joined([outgoing[0]] + received)
        other = swapped(mine, "core", 1)
        sums[index] = pair_sum(place, table, mine, other, [], slots, lines, quarter)[0]
        kept[index] = scatter_sum(sums[index])
        result = finish_chunk([kept[index]], scale, result, start)
    return result.reshape(slots, quarter, half_cols)


def solution(mesh):
    segments, exposures = mesh.shape["seg"], mesh.shape["exp"]
    parted = Mesh(mesh.devices.reshape(segments, exposures // 2, 2), ("seg", "line", "core"))
    spread = ("line", "core")
    placed = (
        P(spread, "seg", None),
        P(spread, None, None),
        P(spread, None),
        P(spread),
        P(spread),
        P(spread),
        P(),
    )
    return jax.shard_map(
        per_device, mesh=parted, in_specs=placed, out_specs=P(spread, "seg", None), check_vma=False
    )
```

```python
import functools

import jax
import jax.numpy as jnp
import numpy as np
from jax import lax
from jax.experimental import pallas as pl
from jax.experimental.pallas import tpu as pltpu
from jax.sharding import Mesh, PartitionSpec as P

BAND_ROWS = 32
TAPS = 21
PHASES = 16
LANCZOS = 6
SPAN = TAPS + LANCZOS - 1
LEAD = TAPS // 2 + 2
HALO = 16
SIDE = 128
TILE = 256
STRIP = 128
PARTS = (2, 2)
VMEM = 48 * 1024 * 1024
COST = pl.CostEstimate(flops=1, bytes_accessed=1, transcendentals=0)

sigmas = (1.0, 2.0, 3.5)


def basis_table():
    offsets = np.arange(TAPS) - TAPS // 2
    curves = [np.exp(-offsets * offsets / (2.0 * spread * spread)) for spread in sigmas]
    return [[float(value) for value in curve / curve.sum()] for curve in curves]


def lanczos_table():
    shifted = np.arange(LANCZOS)[None, :] - 2.0 - np.arange(PHASES)[:, None] / PHASES
    values = np.sinc(shifted) * np.sinc(shifted / 3.0)
    return (values / values.sum(axis=1, keepdims=True)).astype(np.float32)


def lanczos_taps(phase):
    table = lanczos_table()
    taps = []
    for n in range(LANCZOS):
        tap = jnp.float32(table[0, n])
        for index in range(1, PHASES):
            tap = jnp.where(phase == index, jnp.float32(table[index, n]), tap)
        taps.append(tap)
    return taps


def split(value):
    high = value.astype(jnp.bfloat16)
    return high, (value - high.astype(jnp.float32)).astype(jnp.bfloat16)


def banded(taps, mask_sets, distance):
    kernel, lanczos = taps
    sets = [[jnp.where(mask, lanczos[n], 0.0) for n, mask in enumerate(masks)] for masks in mask_sets]
    matrices = [jnp.zeros(distance.shape, jnp.float32) for _ in sets]
    for t in range(SPAN):
        here = distance == t
        for index, weighted in enumerate(sets):
            row = jnp.zeros_like(weighted[0])
            for n in range(LANCZOS):
                if 0 <= t - n < TAPS:
                    row = row + kernel[t - n] * weighted[n]
            matrices[index] = jnp.where(here, row, matrices[index])
    return matrices


def matrices_kernel(place, coef, phases, shift, rows_out, cols_out, *, rows, width, segments):
    basis = basis_table()

    def taps_of(axis):
        kernel = [sum(coef[0, axis, k] * basis[k][t] for k in range(len(sigmas))) for t in range(TAPS)]
        return kernel, lanczos_taps(phases[0, axis])

    def kept(matched, extent):
        return [(matched + (n - 2) >= 0) & (matched + (n - 2) < extent) for n in range(LANCZOS)]

    taps = taps_of(1)
    offset = shift[0]
    column = lax.broadcasted_iota(jnp.int32, (1, SIDE), 1)
    everything = [jnp.full((1, SIDE), True)] * LANCZOS
    mask_sets = [kept(column - offset, width), everything, kept(column + (width - SIDE) - offset, width)]
    for part, block in ((0, 3), (1, 0)):
        for variant in range(3):
            for term in range(2):
                place_out = (pl.ds(block * SIDE, SIDE), pl.ds(part * SIDE, SIDE))
                cols_out[(variant, term, *place_out)] = jnp.zeros((SIDE, SIDE), jnp.bfloat16)
    for step in range(3):
        distance = (
            lax.broadcasted_iota(jnp.int32, (SIDE, SIDE), 0)
            - lax.broadcasted_iota(jnp.int32, (SIDE, SIDE), 1)
            + (offset + LEAD - SIDE + step * SIDE)
        )
        pairs = [split(matrix) for matrix in banded(taps, mask_sets, distance)]
        for part in range(2):
            for variant in range(3):
                chosen = variant if variant == 2 * part else 1
                for term in range(2):
                    place_out = (pl.ds((part + step) * SIDE, SIDE), pl.ds(part * SIDE, SIDE))
                    cols_out[(variant, term, *place_out)] = pairs[chosen][term]

    taps = taps_of(0)
    span = STRIP + 2 * HALO
    quarter = BAND_ROWS // segments
    bands = STRIP // BAND_ROWS
    order = lax.broadcasted_iota(jnp.int32, (1, STRIP), 1)
    within = lax.rem(order, bands * quarter)
    owner = lax.div(order, bands * quarter) ^ place[0]
    output = lax.div(within, quarter) * BAND_ROWS + owner * quarter + lax.rem(within, quarter)
    distance = lax.broadcasted_iota(jnp.int32, (span, STRIP), 0) - output + (LEAD - HALO)
    mask_sets = [
        kept(place[0] * rows + first + output, rows * segments) for first in (0, STRIP, rows - STRIP)
    ]
    rest = jnp.zeros((cols_pad(3 * span) - 3 * span, STRIP), jnp.float32)
    for variant, matrix in enumerate(banded(taps, mask_sets, distance)):
        high = matrix.astype(jnp.bfloat16).astype(jnp.float32)
        stacked = jnp.concatenate([high, high, matrix - high, rest], axis=0).T
        rows_out[variant] = stacked.astype(jnp.bfloat16)[:, : 3 * span]


def cols_pad(count):
    return -(-count // 128) * 128


def build_matrices(place, coef, phases, shift, rows, width, segments):
    span = 3 * (STRIP + 2 * HALO)
    smem = pl.BlockSpec(memory_space=pltpu.SMEM)
    vmem = pl.BlockSpec(memory_space=pltpu.VMEM)
    return pl.pallas_call(
        functools.partial(matrices_kernel, rows=rows, width=width, segments=segments),
        out_shape=(
            jax.ShapeDtypeStruct((3, STRIP, span), jnp.bfloat16),
            jax.ShapeDtypeStruct((3, 2, TILE + 2 * SIDE, TILE), jnp.bfloat16),
        ),
        in_specs=[smem] * 4,
        out_specs=(vmem, vmem),
        compiler_params=pltpu.CompilerParams(vmem_limit_bytes=VMEM),
        cost_estimate=COST,
        name="band_matrices",
    )(place, coef, phases, shift)


def filter_kernel(
    weight, low_l, low_c, low_r, mid_l, mid_c, mid_r, high_l, high_c, high_r, rows_m, cols_m, *rest,
    first_chunk, last_chunk, segments,
):
    *outs, ext_high, ext_low, mat_high, mat_low = rest
    half = pl.program_id(0)
    halves = pl.num_programs(0)
    rows, chunk = mid_c.shape
    at_left = first_chunk & (half == 0)
    at_right = last_chunk & (half == halves - 1)
    span = STRIP + 2 * HALO

    for row, parts in (
        (0, (low_l, low_c, low_r)),
        (HALO, (mid_l, mid_c, mid_r)),
        (HALO + rows, (high_l, high_c, high_r)),
    ):
        count = parts[0].shape[0]
        for part, column, outside in zip(parts, (0, SIDE, SIDE + chunk), (at_left, False, at_right)):
            value = part[...]
            if outside is not False:
                value = jnp.where(outside, 0.0, value)
            high, low = split(value)
            place = (pl.ds(row, count), pl.ds(column, value.shape[1]))
            ext_high[place] = high
            ext_low[place] = low

    strips = rows // STRIP
    for tile in range((chunk + 2 * SIDE) // TILE):
        columns = pl.ds(tile * TILE, TILE)
        for strip in range(strips):
            window = pl.ds(strip * STRIP, span)
            variant = 0 if strip == 0 else (2 if strip == strips - 1 else 1)
            high = ext_high[window, columns]
            stack = jnp.concatenate([high, ext_low[window, columns], high], axis=0)
            matched = jnp.dot(rows_m[variant], stack, preferred_element_type=jnp.float32)
            high, low = split(matched)
            mat_high[pl.ds(strip * STRIP, STRIP), columns] = high
            mat_low[pl.ds(strip * STRIP, STRIP), columns] = low

    tiles = chunk // TILE
    piece = STRIP // segments
    for tile in range(tiles):
        variant = jnp.int32(1)
        if tile == 0:
            variant = jnp.where(at_left, 0, variant)
        if tile == tiles - 1:
            variant = jnp.where(at_right, 2, variant)
        taps_high = cols_m[variant, 0]
        taps_low = cols_m[variant, 1]
        window = pl.ds(tile * TILE, TILE + 2 * SIDE)
        for strip in range(strips):
            place = pl.ds(strip * STRIP, STRIP)
            high = mat_high[place, window]
            warped = jnp.dot(high, taps_high, preferred_element_type=jnp.float32)
            warped += jnp.dot(mat_low[place, window], taps_high, preferred_element_type=jnp.float32)
            warped += jnp.dot(high, taps_low, preferred_element_type=jnp.float32)
            sent = (weight[0] * warped).astype(jnp.bfloat16)
            for owner, out in enumerate(outs):
                out[pl.ds(strip * piece, piece), pl.ds(tile * TILE, TILE)] = sent[owner * piece : (owner + 1) * piece]


def filter_chunk(weight, low, image, high, rows_m, cols_m, start, chunk, segments):
    rows, width = image.shape
    halves = 2
    half_blocks = width // halves // SIDE
    first = start // SIDE
    blocks = chunk // SIDE
    last = width // SIDE - 1

    def left(h):
        return 0, jnp.maximum(h * half_blocks + first - 1, 0)

    def centre(h):
        return 0, h * (half_blocks // blocks) + start // chunk

    def right(h):
        return 0, jnp.minimum(h * half_blocks + first + blocks, last)

    def whole(array):
        return pl.BlockSpec(array.shape, lambda h: (0,) * array.ndim)

    specs = [pl.BlockSpec(memory_space=pltpu.SMEM)]
    for source in (low, image, high):
        specs += [
            pl.BlockSpec((source.shape[0], SIDE), left),
            pl.BlockSpec((source.shape[0], chunk), centre),
            pl.BlockSpec((source.shape[0], SIDE), right),
        ]
    wide = chunk + 2 * SIDE
    return pl.pallas_call(
        functools.partial(
            filter_kernel,
            first_chunk=start == 0,
            last_chunk=start + chunk == width // halves,
            segments=segments,
        ),
        out_shape=[jax.ShapeDtypeStruct((rows // segments, halves * chunk), jnp.bfloat16)] * segments,
        grid=(halves,),
        in_specs=specs + [whole(rows_m), whole(cols_m)],
        out_specs=[pl.BlockSpec((rows // segments, chunk), lambda h: (0, h))] * segments,
        scratch_shapes=[
            pltpu.VMEM((rows + 2 * HALO, wide), jnp.bfloat16),
            pltpu.VMEM((rows + 2 * HALO, wide), jnp.bfloat16),
            pltpu.VMEM((rows, wide), jnp.bfloat16),
            pltpu.VMEM((rows, wide), jnp.bfloat16),
        ],
        compiler_params=pltpu.CompilerParams(vmem_limit_bytes=VMEM),
        cost_estimate=COST,
        name="warp_filter",
    )(weight, *([low] * 3), *([image] * 3), *([high] * 3), rows_m, cols_m)


def join_kernel(*refs):
    block = refs[0].shape[0]
    for step, ref in enumerate(refs[:-1]):
        refs[-1][pl.ds(step * block, block), :] = ref[...]


def joined(blocks):
    block, columns = blocks[0].shape
    vmem = pl.BlockSpec(memory_space=pltpu.VMEM)
    return pl.pallas_call(
        join_kernel,
        out_shape=jax.ShapeDtypeStruct((len(blocks) * block, columns), blocks[0].dtype),
        in_specs=[vmem] * len(blocks),
        out_specs=vmem,
        compiler_params=pltpu.CompilerParams(vmem_limit_bytes=VMEM),
        cost_estimate=COST,
        name="join_blocks",
    )(*blocks)


def stage_distances(lines):
    stages = []
    step = 1
    while step < lines:
        stages.append(list(reversed(range(step, lines, 2 * step))))
        step *= 2
    return stages


def pair_kernel(place, table, mine, other, *rest, slots, distances, quarter):
    *outs, mine_all, other_all = rest
    rows = mine.shape[0]
    chunk = outs[0].shape[1]
    count = table.shape[0] // 3
    for source, held in ((mine, mine_all), (other, other_all)):
        held[pl.ds(0, rows), :] = source[...].astype(jnp.float32)
        held[pl.ds(rows, quarter), :] = jnp.zeros((quarter, source.shape[1]), jnp.float32)
    line = place[1]

    for distance, out in zip(distances, outs):
        first = (line ^ distance) * slots

        def summed(slot, first=first):
            column = pl.ds(pl.multiple_of(table[first + slot] * chunk, 128), chunk)
            from_mine = pl.ds(pl.multiple_of(table[count + first + slot], quarter), quarter)
            from_other = pl.ds(pl.multiple_of(table[2 * count + first + slot], quarter), quarter)
            return mine_all[from_mine, column] + other_all[from_other, column]

        for slot in range(0, slots - 1, 2):
            rows_two = jnp.concatenate([summed(slot), summed(slot + 1)], axis=0)
            out[pl.ds(slot * quarter, 2 * quarter), :] = rows_two.astype(jnp.bfloat16)
        if slots % 2:
            out[pl.ds((slots - 1) * quarter, quarter), :] = summed(slots - 1).astype(jnp.bfloat16)


def pair_sum(place, table, mine, other, slots, lines, quarter):
    rows, double = mine.shape
    chunk = double // 2
    distances = sum(stage_distances(lines), []) + [0]
    smem = pl.BlockSpec(memory_space=pltpu.SMEM)
    vmem = pl.BlockSpec(memory_space=pltpu.VMEM)
    outs = pl.pallas_call(
        functools.partial(pair_kernel, slots=slots, distances=distances, quarter=quarter),
        out_shape=[jax.ShapeDtypeStruct((slots * quarter, chunk), jnp.bfloat16)] * lines,
        in_specs=[smem, smem, vmem, vmem],
        out_specs=[vmem] * lines,
        scratch_shapes=[pltpu.VMEM((rows + quarter, double), jnp.float32)] * 2,
        compiler_params=pltpu.CompilerParams(vmem_limit_bytes=VMEM),
        cost_estimate=COST,
        name="pair_sum",
    )(place, table, mine, other)
    return dict(zip(distances, outs))


def weight_kernel(place, sites, facts, out, covers, *, cores, quarter, width, bands):
    slots = out.shape[0] // quarter
    half_cols = out.shape[1]
    exposures = facts.shape[0]
    owner = place[1] * cores + place[2]
    column = lax.broadcasted_iota(jnp.int32, (quarter, half_cols), 1)
    for half in range(2):
        for exposure in range(exposures):
            first = facts[exposure, 0].astype(jnp.int32) - half * half_cols
            inside = (column >= first) & (column < first + width)
            covers[half * exposures + exposure] = jnp.where(inside, facts[exposure, 2], 0.0)

    def one_slot(slot, carry):
        site = sites[owner * slots + slot]
        total = jnp.zeros((quarter, half_cols), jnp.float32)
        for exposure in range(exposures):
            relative = lax.shift_right_logical(site, 1) - facts[exposure, 1].astype(jnp.int32)
            present = jnp.where((relative >= 0) & (relative < bands), jnp.float32(1.0), jnp.float32(0.0))
            total = total + present * covers[(site & 1) * exposures + exposure]
        out[pl.ds(pl.multiple_of(slot * quarter, quarter), quarter), :] = jnp.maximum(total, 1.0)
        return carry

    lax.fori_loop(0, slots, one_slot, 0)


def patch_weights(place, sites, facts, slots, quarter, cores, width, bands):
    smem = pl.BlockSpec(memory_space=pltpu.SMEM)
    return pl.pallas_call(
        functools.partial(weight_kernel, cores=cores, quarter=quarter, width=width, bands=bands),
        out_shape=jax.ShapeDtypeStruct((slots * quarter, width // 2), jnp.float32),
        in_specs=[smem] * 3,
        out_specs=pl.BlockSpec(memory_space=pltpu.VMEM),
        scratch_shapes=[pltpu.VMEM((2 * facts.shape[0], quarter, width // 2), jnp.float32)],
        compiler_params=pltpu.CompilerParams(vmem_limit_bytes=VMEM),
        cost_estimate=COST,
        name="patch_weights",
    )(place, sites, facts)


def finish_kernel(*refs, count):
    pieces, scale, out = refs[:count], refs[count], refs[-1]
    total = pieces[0][...].astype(jnp.float32)
    for piece in pieces[1:]:
        total += piece[...].astype(jnp.float32)
    out[...] = total / scale[...]


def finish_chunk(pieces, scale, result, start):
    rows, chunk = pieces[0].shape
    column = pl.BlockSpec((rows, chunk), lambda i: (0, start // chunk))
    specs = [pl.BlockSpec((rows, chunk), lambda i: (0, 0))] * len(pieces) + [column]
    operands = [*pieces, scale]
    aliases = {}
    if result is not None:
        specs.append(pl.BlockSpec(memory_space=pl.ANY))
        aliases = {len(operands): 0}
        operands.append(result)
    return pl.pallas_call(
        functools.partial(finish_kernel, count=len(pieces)),
        out_shape=jax.ShapeDtypeStruct(scale.shape, jnp.float32),
        grid=(1,),
        in_specs=specs,
        out_specs=column,
        input_output_aliases=aliases,
        compiler_params=pltpu.CompilerParams(vmem_limit_bytes=VMEM),
        cost_estimate=pl.CostEstimate(
            flops=len(pieces) * rows * chunk, bytes_accessed=rows * chunk * (2 * len(pieces) + 8), transcendentals=0
        ),
        name="patch_mean",
    )(*operands)


def swapped(value, axis, distance):
    count = lax.axis_size(axis)
    return lax.ppermute(value, axis, [(i, i ^ distance) for i in range(count)])


def scatter_sum(pieces):
    pieces = dict(pieces)
    kept, added = [pieces[0]], []
    for stage, distances in enumerate(stage_distances(len(pieces))):
        for distance in distances:
            received = swapped(pieces[distance], "line", 1 << stage)
            target = distance ^ (1 << stage)
            if target:
                both = pieces[target].astype(jnp.float32) + received.astype(jnp.float32)
                pieces[target] = both.astype(jnp.bfloat16)
                added = [pieces[target]]
            else:
                kept.append(received)
    return kept, added


def per_device(images, psf_coef, phases, col_shift, band_offset, exposure_weight, patch_site):
    image = images[0]
    rows, width = image.shape
    segments = lax.axis_size("seg")
    lines = lax.axis_size("line")
    cores = lax.axis_size("core")
    quarter = BAND_ROWS // segments
    half_cols = width // 2
    slots = patch_site.shape[0] // (lines * cores)
    bands = segments * rows // BAND_ROWS
    place = jnp.stack([lax.axis_index(axis) for axis in ("seg", "line", "core")]).astype(jnp.int32)

    forward = [(i, i + 1) for i in range(segments - 1)]
    backward = [(i + 1, i) for i in range(segments - 1)]
    low = lax.ppermute(image[rows - HALO :], "seg", forward)
    high = lax.ppermute(image[:HALO], "seg", backward)
    rows_m, cols_m = build_matrices(place, psf_coef, phases, col_shift, rows, width, segments)
    weight = exposure_weight.astype(jnp.float32)

    chunks = []
    start = 0
    for part in PARTS:
        chunks.append((start, half_cols // part))
        start += half_cols // part
    other_offset = swapped(band_offset, "core", 1)
    sites = lax.dynamic_index_in_dim(patch_site.reshape(lines, cores, slots), place[2], 1, keepdims=False).reshape(-1)
    here = rows // BAND_ROWS

    def rows_from(offset):
        relative = sites // 2 - offset
        held = ((relative // here) ^ place[0]) * here + relative % here
        return jnp.where((relative >= 0) & (relative < bands), held, bands) * quarter

    table = jnp.concatenate([sites % 2, rows_from(band_offset), rows_from(other_offset)])
    facts = jnp.stack([col_shift.astype(jnp.float32), band_offset.astype(jnp.float32), weight], axis=1)
    facts = jnp.concatenate([facts, swapped(facts, "core", 1)], axis=0)
    early = facts
    step = 1
    while step < lines:
        early = facts
        facts = jnp.concatenate([facts, swapped(facts, "line", step)], axis=0)
        step *= 2
    scale = patch_weights(place, patch_site, facts, slots, quarter, cores, width, bands)

    def tied(values, others):
        return lax.optimization_barrier((values, others))[0]

    result = None
    count = len(chunks)
    sent, sums, kept, added = [None] * count, [None] * count, [None] * count, [None] * count

    def filtered(index):
        start, chunk = chunks[index]
        held = tied(weight, sums[index - 2]) if index >= 2 else weight
        sent[index] = filter_chunk(held, low, image, high, rows_m, cols_m, start, chunk, segments)

    filtered(0)
    for index, (start, chunk) in enumerate(chunks):
        outgoing = sent[index]
        received = [swapped(outgoing[d], "seg", d) for d in range(1, segments)]
        if index + 1 < count:
            filtered(index + 1)
            received = tied(received, sent[index + 1])
        if index == 0:
            received = tied(received, early)
        if index == 1:
            received = tied(received, scale)
        if index >= 1:
            received = tied(received, (added[index - 1], kept[index - 1][:-1]))
        mine = joined([outgoing[0]] + received)
        other = swapped(mine, "core", 1)
        sums[index] = pair_sum(place, table, mine, other, slots, lines, quarter)
        kept[index], added[index] = scatter_sum(sums[index])
        result = finish_chunk(kept[index], scale, result, start)
    return result.reshape(slots, quarter, half_cols)


def solution(mesh):
    segments, exposures = mesh.shape["seg"], mesh.shape["exp"]
    parted = Mesh(mesh.devices.reshape(segments, exposures // 2, 2), ("seg", "line", "core"))
    spread = ("line", "core")
    placed = (
        P(spread, "seg", None),
        P(spread, None, None),
        P(spread, None),
        P(spread),
        P(spread),
        P(spread),
        P(),
    )
    return jax.shard_map(
        per_device, mesh=parted, in_specs=placed, out_specs=P(spread, "seg", None), check_vma=False
    )
```

```python
import functools

import jax
import jax.numpy as jnp
import numpy as np
from jax import lax
from jax.experimental import pallas as pl
from jax.experimental.pallas import tpu as pltpu
from jax.sharding import Mesh, PartitionSpec as P

BAND_ROWS = 32
TAPS = 21
PHASES = 16
LANCZOS = 6
SPAN = TAPS + LANCZOS - 1
LEAD = TAPS // 2 + 2
HALO = 16
SIDE = 128
TILE = 256
STRIP = 128
PARTS = (3, 3, 2)
WHOLE = 8
VMEM = 48 * 1024 * 1024
COST = pl.CostEstimate(flops=1, bytes_accessed=1, transcendentals=0)

sigmas = (1.0, 2.0, 3.5)


def basis_table():
    offsets = np.arange(TAPS) - TAPS // 2
    curves = [np.exp(-offsets * offsets / (2.0 * spread * spread)) for spread in sigmas]
    return [[float(value) for value in curve / curve.sum()] for curve in curves]


def lanczos_table():
    shifted = np.arange(LANCZOS)[None, :] - 2.0 - np.arange(PHASES)[:, None] / PHASES
    values = np.sinc(shifted) * np.sinc(shifted / 3.0)
    return (values / values.sum(axis=1, keepdims=True)).astype(np.float32)


def lanczos_taps(phase):
    table = lanczos_table()
    taps = []
    for n in range(LANCZOS):
        tap = jnp.float32(table[0, n])
        for index in range(1, PHASES):
            tap = jnp.where(phase == index, jnp.float32(table[index, n]), tap)
        taps.append(tap)
    return taps


def split(value):
    high = value.astype(jnp.bfloat16)
    return high, (value - high.astype(jnp.float32)).astype(jnp.bfloat16)


def banded(taps, mask_sets, distance):
    kernel, lanczos = taps
    sets = [[jnp.where(mask, lanczos[n], 0.0) for n, mask in enumerate(masks)] for masks in mask_sets]
    matrices = [jnp.zeros(distance.shape, jnp.float32) for _ in sets]
    for t in range(SPAN):
        here = distance == t
        for index, weighted in enumerate(sets):
            row = jnp.zeros_like(weighted[0])
            for n in range(LANCZOS):
                if 0 <= t - n < TAPS:
                    row = row + kernel[t - n] * weighted[n]
            matrices[index] = jnp.where(here, row, matrices[index])
    return matrices


def matrices_kernel(place, coef, phases, shift, rows_out, cols_out, *, rows, width, segments):
    basis = basis_table()

    def taps_of(axis):
        kernel = [sum(coef[0, axis, k] * basis[k][t] for k in range(len(sigmas))) for t in range(TAPS)]
        return kernel, lanczos_taps(phases[0, axis])

    def kept(matched, extent):
        return [(matched + (n - 2) >= 0) & (matched + (n - 2) < extent) for n in range(LANCZOS)]

    taps = taps_of(1)
    offset = shift[0]
    column = lax.broadcasted_iota(jnp.int32, (1, SIDE), 1)
    everything = [jnp.full((1, SIDE), True)] * LANCZOS
    mask_sets = [kept(column - offset, width), everything, kept(column + (width - SIDE) - offset, width)]
    for part, block in ((0, 3), (1, 0)):
        for variant in range(3):
            for term in range(2):
                place_out = (pl.ds(block * SIDE, SIDE), pl.ds(part * SIDE, SIDE))
                cols_out[(variant, term, *place_out)] = jnp.zeros((SIDE, SIDE), jnp.bfloat16)
    for step in range(3):
        distance = (
            lax.broadcasted_iota(jnp.int32, (SIDE, SIDE), 0)
            - lax.broadcasted_iota(jnp.int32, (SIDE, SIDE), 1)
            + (offset + LEAD - SIDE + step * SIDE)
        )
        pairs = [split(matrix) for matrix in banded(taps, mask_sets, distance)]
        for part in range(2):
            for variant in range(3):
                chosen = variant if variant == 2 * part else 1
                for term in range(2):
                    place_out = (pl.ds((part + step) * SIDE, SIDE), pl.ds(part * SIDE, SIDE))
                    cols_out[(variant, term, *place_out)] = pairs[chosen][term]

    taps = taps_of(0)
    span = STRIP + 2 * HALO
    quarter = BAND_ROWS // segments
    bands = STRIP // BAND_ROWS
    order = lax.broadcasted_iota(jnp.int32, (1, STRIP), 1)
    within = lax.rem(order, bands * quarter)
    owner = lax.div(order, bands * quarter) ^ place[0]
    output = lax.div(within, quarter) * BAND_ROWS + owner * quarter + lax.rem(within, quarter)
    distance = lax.broadcasted_iota(jnp.int32, (span, STRIP), 0) - output + (LEAD - HALO)
    mask_sets = [
        kept(place[0] * rows + first + output, rows * segments) for first in (0, STRIP, rows - STRIP)
    ]
    rest = jnp.zeros((cols_pad(3 * span) - 3 * span, STRIP), jnp.float32)
    for variant, matrix in enumerate(banded(taps, mask_sets, distance)):
        high = matrix.astype(jnp.bfloat16).astype(jnp.float32)
        stacked = jnp.concatenate([high, high, matrix - high, rest], axis=0).T
        rows_out[variant] = stacked.astype(jnp.bfloat16)[:, : 3 * span]


def cols_pad(count):
    return -(-count // 128) * 128


def build_matrices(place, coef, phases, shift, rows, width, segments):
    span = 3 * (STRIP + 2 * HALO)
    smem = pl.BlockSpec(memory_space=pltpu.SMEM)
    vmem = pl.BlockSpec(memory_space=pltpu.VMEM)
    return pl.pallas_call(
        functools.partial(matrices_kernel, rows=rows, width=width, segments=segments),
        out_shape=(
            jax.ShapeDtypeStruct((3, STRIP, span), jnp.bfloat16),
            jax.ShapeDtypeStruct((3, 2, TILE + 2 * SIDE, TILE), jnp.bfloat16),
        ),
        in_specs=[smem] * 4,
        out_specs=(vmem, vmem),
        compiler_params=pltpu.CompilerParams(vmem_limit_bytes=VMEM),
        cost_estimate=COST,
        name="band_matrices",
    )(place, coef, phases, shift)


def filter_kernel(weight, place, *rest, first_chunk, last_chunk, segments, pieces):
    sources, (rows_m, cols_m), refs = rest[: 3 * pieces], rest[3 * pieces : 3 * pieces + 2], rest[3 * pieces + 2 :]
    image, even, odd = sources[:pieces], sources[pieces : 2 * pieces], sources[2 * pieces :]
    *outs, ext_high, ext_low, mat_high, mat_low = refs
    half = pl.program_id(0)
    halves = pl.num_programs(0)
    rows = image[0].shape[0]
    chunk = (pieces - 2) * TILE
    at_left = first_chunk & (half == 0)
    at_right = last_chunk & (half == halves - 1)
    span = STRIP + 2 * HALO
    is_odd = (place[0] & 1) == 1

    column = 0
    for index in range(pieces):
        wide = image[index].shape[1]
        low = jnp.where(is_odd, even[index][...], odd[index][...])
        high = jnp.where(is_odd, odd[index][...], even[index][...])
        for row, value in ((0, low), (HALO, image[index][...]), (HALO + rows, high)):
            if index == 0:
                value = jnp.where(at_left, 0.0, value)
            if index == pieces - 1:
                value = jnp.where(at_right, 0.0, value)
            target = (pl.ds(row, value.shape[0]), pl.ds(column, wide))
            ext_high[target], ext_low[target] = split(value)
        column += wide

    strips = rows // STRIP
    for tile in range((chunk + 2 * SIDE) // TILE):
        columns = pl.ds(tile * TILE, TILE)
        for strip in range(strips):
            window = pl.ds(strip * STRIP, span)
            variant = 0 if strip == 0 else (2 if strip == strips - 1 else 1)
            high = ext_high[window, columns]
            stack = jnp.concatenate([high, ext_low[window, columns], high], axis=0)
            matched = jnp.dot(rows_m[variant], stack, preferred_element_type=jnp.float32)
            high, low = split(matched)
            mat_high[pl.ds(strip * STRIP, STRIP), columns] = high
            mat_low[pl.ds(strip * STRIP, STRIP), columns] = low

    tiles = chunk // TILE
    piece = STRIP // segments
    for tile in range(tiles):
        variant = jnp.int32(1)
        if tile == 0:
            variant = jnp.where(at_left, 0, variant)
        if tile == tiles - 1:
            variant = jnp.where(at_right, 2, variant)
        taps_high = cols_m[variant, 0]
        taps_low = cols_m[variant, 1]
        window = pl.ds(tile * TILE, TILE + 2 * SIDE)
        for strip in range(strips):
            place = pl.ds(strip * STRIP, STRIP)
            high = mat_high[place, window]
            warped = jnp.dot(high, taps_high, preferred_element_type=jnp.float32)
            warped += jnp.dot(mat_low[place, window], taps_high, preferred_element_type=jnp.float32)
            warped += jnp.dot(high, taps_low, preferred_element_type=jnp.float32)
            sent = (weight[0] * warped).astype(jnp.bfloat16)
            for owner, out in enumerate(outs):
                out[pl.ds(strip * piece, piece), pl.ds(tile * TILE, TILE)] = sent[owner * piece : (owner + 1) * piece]


def filter_chunk(weight, place, image, even, odd, rows_m, cols_m, start, chunk, segments):
    rows, width = image.shape
    halves = 2
    half_cols = width // halves
    last = width // SIDE - 1

    def left(h):
        return 0, jnp.maximum((h * half_cols + start) // SIDE - 1, 0)

    def right(h):
        return 0, jnp.minimum((h * half_cols + start + chunk) // SIDE, last)

    def inner(index):
        return lambda h: (0, (h * half_cols + start) // TILE + index)

    def whole(array):
        return pl.BlockSpec(array.shape, lambda h: (0,) * array.ndim)

    pieces = chunk // TILE + 2
    specs = [pl.BlockSpec(memory_space=pltpu.SMEM)] * 2
    operands = [weight, place]
    for source in (image, even, odd):
        count = source.shape[0]
        specs.append(pl.BlockSpec((count, SIDE), left))
        specs += [pl.BlockSpec((count, TILE), inner(index)) for index in range(pieces - 2)]
        specs.append(pl.BlockSpec((count, SIDE), right))
        operands += [source] * pieces
    wide = chunk + 2 * SIDE
    return pl.pallas_call(
        functools.partial(
            filter_kernel,
            first_chunk=start == 0,
            last_chunk=start + chunk == width // halves,
            segments=segments,
            pieces=pieces,
        ),
        out_shape=[jax.ShapeDtypeStruct((rows // segments, halves * chunk), jnp.bfloat16)] * segments,
        grid=(halves,),
        in_specs=specs + [whole(rows_m), whole(cols_m)],
        out_specs=[pl.BlockSpec((rows // segments, chunk), lambda h: (0, h))] * segments,
        scratch_shapes=[
            pltpu.VMEM((rows + 2 * HALO, wide), jnp.bfloat16),
            pltpu.VMEM((rows + 2 * HALO, wide), jnp.bfloat16),
            pltpu.VMEM((rows, wide), jnp.bfloat16),
            pltpu.VMEM((rows, wide), jnp.bfloat16),
        ],
        compiler_params=pltpu.CompilerParams(vmem_limit_bytes=VMEM),
        cost_estimate=COST,
        name="warp_filter",
    )(*operands, rows_m, cols_m)


def join_kernel(*refs):
    block = refs[0].shape[0]
    for step, ref in enumerate(refs[:-1]):
        refs[-1][pl.ds(step * block, block), :] = ref[...]


def joined(blocks):
    block, columns = blocks[0].shape
    vmem = pl.BlockSpec(memory_space=pltpu.VMEM)
    return pl.pallas_call(
        join_kernel,
        out_shape=jax.ShapeDtypeStruct((len(blocks) * block, columns), blocks[0].dtype),
        in_specs=[vmem] * len(blocks),
        out_specs=vmem,
        compiler_params=pltpu.CompilerParams(vmem_limit_bytes=VMEM),
        cost_estimate=COST,
        name="join_blocks",
    )(*blocks)


def stage_distances(lines):
    stages = []
    step = 1
    while step < lines:
        stages.append(list(reversed(range(step, lines, 2 * step))))
        step *= 2
    return stages


def pair_kernel(place, table, mine, other, *rest, slots, distances, quarter):
    *outs, mine_all, other_all = rest
    rows = mine.shape[0]
    chunk = outs[0].shape[1]
    count = table.shape[0] // 3
    for source, held in ((mine, mine_all), (other, other_all)):
        held[pl.ds(0, rows), :] = source[...].astype(jnp.float32)
        held[pl.ds(rows, quarter), :] = jnp.zeros((quarter, source.shape[1]), jnp.float32)
    line = place[1]

    for distance, out in zip(distances, outs):
        first = (line ^ distance) * slots

        def summed(slot, first=first):
            column = pl.ds(pl.multiple_of(table[first + slot] * chunk, 128), chunk)
            from_mine = pl.ds(pl.multiple_of(table[count + first + slot], quarter), quarter)
            from_other = pl.ds(pl.multiple_of(table[2 * count + first + slot], quarter), quarter)
            return mine_all[from_mine, column] + other_all[from_other, column]

        for slot in range(0, slots - 1, 2):
            rows_two = jnp.concatenate([summed(slot), summed(slot + 1)], axis=0)
            out[pl.ds(slot * quarter, 2 * quarter), :] = rows_two.astype(jnp.bfloat16)
        if slots % 2:
            out[pl.ds((slots - 1) * quarter, quarter), :] = summed(slots - 1).astype(jnp.bfloat16)


def pair_sum(place, table, mine, other, slots, lines, quarter):
    rows, double = mine.shape
    chunk = double // 2
    distances = sum(stage_distances(lines), []) + [0]
    smem = pl.BlockSpec(memory_space=pltpu.SMEM)
    vmem = pl.BlockSpec(memory_space=pltpu.VMEM)
    outs = pl.pallas_call(
        functools.partial(pair_kernel, slots=slots, distances=distances, quarter=quarter),
        out_shape=[jax.ShapeDtypeStruct((slots * quarter, chunk), jnp.bfloat16)] * lines,
        in_specs=[smem, smem, vmem, vmem],
        out_specs=[vmem] * lines,
        scratch_shapes=[pltpu.VMEM((rows + quarter, double), jnp.float32)] * 2,
        compiler_params=pltpu.CompilerParams(vmem_limit_bytes=VMEM),
        cost_estimate=COST,
        name="pair_sum",
    )(place, table, mine, other)
    return dict(zip(distances, outs))


def weight_kernel(place, sites, facts, out, covers, *, cores, quarter, width, bands):
    slots = out.shape[0] // quarter
    half_cols = out.shape[1]
    exposures = facts.shape[0]
    owner = place[1] * cores + place[2]
    column = lax.broadcasted_iota(jnp.int32, (quarter, half_cols), 1)
    for half in range(2):
        for exposure in range(exposures):
            first = facts[exposure, 0].astype(jnp.int32) - half * half_cols
            inside = (column >= first) & (column < first + width)
            covers[half * exposures + exposure] = jnp.where(inside, facts[exposure, 2], 0.0)

    def one_slot(slot, carry):
        site = sites[owner * slots + slot]
        total = jnp.zeros((quarter, half_cols), jnp.float32)
        for exposure in range(exposures):
            relative = lax.shift_right_logical(site, 1) - facts[exposure, 1].astype(jnp.int32)
            present = jnp.where((relative >= 0) & (relative < bands), jnp.float32(1.0), jnp.float32(0.0))
            total = total + present * covers[(site & 1) * exposures + exposure]
        out[pl.ds(pl.multiple_of(slot * quarter, quarter), quarter), :] = jnp.maximum(total, 1.0)
        return carry

    lax.fori_loop(0, slots, one_slot, 0)


def patch_weights(place, sites, facts, slots, quarter, cores, width, bands):
    smem = pl.BlockSpec(memory_space=pltpu.SMEM)
    return pl.pallas_call(
        functools.partial(weight_kernel, cores=cores, quarter=quarter, width=width, bands=bands),
        out_shape=jax.ShapeDtypeStruct((slots * quarter, width // 2), jnp.float32),
        in_specs=[smem] * 3,
        out_specs=pl.BlockSpec(memory_space=pltpu.VMEM),
        scratch_shapes=[pltpu.VMEM((2 * facts.shape[0], quarter, width // 2), jnp.float32)],
        compiler_params=pltpu.CompilerParams(vmem_limit_bytes=VMEM),
        cost_estimate=COST,
        name="patch_weights",
    )(place, sites, facts)


def finish_kernel(*refs, count):
    pieces, scale, out = refs[:count], refs[count], refs[-1]
    total = pieces[0][...].astype(jnp.float32)
    for piece in pieces[1:]:
        total += piece[...].astype(jnp.float32)
    out[...] = total / scale[...]


def finish_chunk(pieces, scale, result, start):
    rows, chunk = pieces[0].shape
    column = pl.BlockSpec((rows, chunk), lambda i: (0, start // chunk))
    specs = [pl.BlockSpec((rows, chunk), lambda i: (0, 0))] * len(pieces) + [column]
    operands = [*pieces, scale]
    aliases = {}
    if result is not None:
        specs.append(pl.BlockSpec(memory_space=pl.ANY))
        aliases = {len(operands): 0}
        operands.append(result)
    return pl.pallas_call(
        functools.partial(finish_kernel, count=len(pieces)),
        out_shape=jax.ShapeDtypeStruct(scale.shape, jnp.float32),
        grid=(1,),
        in_specs=specs,
        out_specs=column,
        input_output_aliases=aliases,
        compiler_params=pltpu.CompilerParams(vmem_limit_bytes=VMEM),
        cost_estimate=pl.CostEstimate(
            flops=len(pieces) * rows * chunk, bytes_accessed=rows * chunk * (2 * len(pieces) + 8), transcendentals=0
        ),
        name="patch_mean",
    )(*operands)


def swapped(value, axis, distance):
    count = lax.axis_size(axis)
    return lax.ppermute(value, axis, [(i, i ^ distance) for i in range(count)])


def scatter_sum(pieces):
    pieces = dict(pieces)
    kept, added = [pieces[0]], []
    for stage, distances in enumerate(stage_distances(len(pieces))):
        for distance in distances:
            received = swapped(pieces[distance], "line", 1 << stage)
            target = distance ^ (1 << stage)
            if target:
                both = pieces[target].astype(jnp.float32) + received.astype(jnp.float32)
                pieces[target] = both.astype(jnp.bfloat16)
                added = [pieces[target]]
            else:
                kept.append(received)
    return kept, added


def per_device(images, psf_coef, phases, col_shift, band_offset, exposure_weight, patch_site):
    image = images[0]
    rows, width = image.shape
    segments = lax.axis_size("seg")
    lines = lax.axis_size("line")
    cores = lax.axis_size("core")
    quarter = BAND_ROWS // segments
    half_cols = width // 2
    slots = patch_site.shape[0] // (lines * cores)
    bands = segments * rows // BAND_ROWS
    place = jnp.stack([lax.axis_index(axis) for axis in ("seg", "line", "core")]).astype(jnp.int32)

    def pairs_from(first):
        pairs = [(i, i + 1) for i in range(first, segments - 1, 2)]
        return pairs + [(j, i) for i, j in pairs]

    is_odd = (place[0] & 1) == 1
    top, bottom = image[:HALO], image[rows - HALO :]
    even = lax.ppermute(jnp.where(is_odd, top, bottom), "seg", pairs_from(0))
    odd = lax.ppermute(jnp.where(is_odd, bottom, top), "seg", pairs_from(1))
    rows_m, cols_m = build_matrices(place, psf_coef, phases, col_shift, rows, width, segments)
    weight = exposure_weight.astype(jnp.float32)

    chunks = []
    start = 0
    for part in PARTS:
        chunks.append((start, half_cols * part // WHOLE))
        start += half_cols * part // WHOLE
    other_offset = swapped(band_offset, "core", 1)
    sites = lax.dynamic_index_in_dim(patch_site.reshape(lines, cores, slots), place[2], 1, keepdims=False).reshape(-1)
    here = rows // BAND_ROWS

    def rows_from(offset):
        relative = sites // 2 - offset
        held = ((relative // here) ^ place[0]) * here + relative % here
        return jnp.where((relative >= 0) & (relative < bands), held, bands) * quarter

    table = jnp.concatenate([sites % 2, rows_from(band_offset), rows_from(other_offset)])
    facts = jnp.stack([col_shift.astype(jnp.float32), band_offset.astype(jnp.float32), weight], axis=1)
    facts = jnp.concatenate([facts, swapped(facts, "core", 1)], axis=0)
    step = 1
    while step < lines:
        facts = jnp.concatenate([facts, swapped(facts, "line", step)], axis=0)
        step *= 2
    scale = patch_weights(place, patch_site, facts, slots, quarter, cores, width, bands)

    def tied(values, others):
        return lax.optimization_barrier((values, others))[0]

    result = None
    count = len(chunks)
    sent, sums, kept, added = [None] * count, [None] * count, [None] * count, [None] * count

    def filtered(index):
        start, chunk = chunks[index]
        held = tied(weight, sums[index - 2]) if index >= 2 else weight
        sent[index] = filter_chunk(held, place, image, even, odd, rows_m, cols_m, start, chunk, segments)

    filtered(0)
    for index, (start, chunk) in enumerate(chunks):
        outgoing = sent[index]
        received = [swapped(outgoing[d], "seg", d) for d in range(1, segments)]
        if index + 1 < count:
            filtered(index + 1)
            received = tied(received, sent[index + 1])
        if index == 0:
            received = tied(received, scale)
        if index >= 1:
            received = tied(received, added[index - 1])
        if index == 1:
            received = tied(received, kept[0][:-1])
        if index >= 2:
            received = tied(received, kept[index - 2])
        mine = joined([outgoing[0]] + received)
        other = swapped(mine, "core", 1)
        sums[index] = pair_sum(place, table, mine, other, slots, lines, quarter)
        kept[index], added[index] = scatter_sum(sums[index])
        result = finish_chunk(kept[index], scale, result, start)
    return result.reshape(slots, quarter, half_cols)


def solution(mesh):
    segments, exposures = mesh.shape["seg"], mesh.shape["exp"]
    parted = Mesh(mesh.devices.reshape(segments, exposures // 2, 2), ("seg", "line", "core"))
    spread = ("line", "core")
    placed = (
        P(spread, "seg", None),
        P(spread, None, None),
        P(spread, None),
        P(spread),
        P(spread),
        P(spread),
        P(),
    )
    return jax.shard_map(
        per_device, mesh=parted, in_specs=placed, out_specs=P(spread, "seg", None), check_vma=False
    )
```

```python
import functools

import jax
import jax.numpy as jnp
import numpy as np
from jax import lax
from jax.experimental import pallas as pl
from jax.experimental.pallas import tpu as pltpu
from jax.sharding import Mesh, PartitionSpec as P

BAND_ROWS = 32
TAPS = 21
PHASES = 16
LANCZOS = 6
SPAN = TAPS + LANCZOS - 1
LEAD = TAPS // 2 + 2
HALO = 16
SIDE = 128
TILE = 256
STRIP = 128
PARTS = (4, 4)
WHOLE = 8
VMEM = 24 * 1024 * 1024
COST = pl.CostEstimate(flops=1, bytes_accessed=1, transcendentals=0)

sigmas = (1.0, 2.0, 3.5)


def basis_table():
    offsets = np.arange(TAPS) - TAPS // 2
    curves = [np.exp(-offsets * offsets / (2.0 * spread * spread)) for spread in sigmas]
    return [[float(value) for value in curve / curve.sum()] for curve in curves]


def lanczos_table():
    shifted = np.arange(LANCZOS)[None, :] - 2.0 - np.arange(PHASES)[:, None] / PHASES
    values = np.sinc(shifted) * np.sinc(shifted / 3.0)
    return (values / values.sum(axis=1, keepdims=True)).astype(np.float32)


def lanczos_taps(phase):
    table = lanczos_table()
    taps = []
    for n in range(LANCZOS):
        tap = jnp.float32(table[0, n])
        for index in range(1, PHASES):
            tap = jnp.where(phase == index, jnp.float32(table[index, n]), tap)
        taps.append(tap)
    return taps


def split(value):
    high = value.astype(jnp.bfloat16)
    return high, (value - high.astype(jnp.float32)).astype(jnp.bfloat16)


def banded(taps, mask_sets, distance):
    kernel, lanczos = taps
    sets = [[jnp.where(mask, lanczos[n], 0.0) for n, mask in enumerate(masks)] for masks in mask_sets]
    matrices = [jnp.zeros(distance.shape, jnp.float32) for _ in sets]
    for t in range(SPAN):
        here = distance == t
        for index, weighted in enumerate(sets):
            row = jnp.zeros_like(weighted[0])
            for n in range(LANCZOS):
                if 0 <= t - n < TAPS:
                    row = row + kernel[t - n] * weighted[n]
            matrices[index] = jnp.where(here, row, matrices[index])
    return matrices


def matrices_kernel(place, coef, phases, shift, rows_out, cols_out, *, rows, width, segments):
    basis = basis_table()

    def taps_of(axis):
        kernel = [sum(coef[0, axis, k] * basis[k][t] for k in range(len(sigmas))) for t in range(TAPS)]
        return kernel, lanczos_taps(phases[0, axis])

    def kept(matched, extent):
        return [(matched + (n - 2) >= 0) & (matched + (n - 2) < extent) for n in range(LANCZOS)]

    taps = taps_of(1)
    offset = shift[0]
    column = lax.broadcasted_iota(jnp.int32, (1, SIDE), 1)
    everything = [jnp.full((1, SIDE), True)] * LANCZOS
    mask_sets = [kept(column - offset, width), everything, kept(column + (width - SIDE) - offset, width)]
    for part, block in ((0, 3), (1, 0)):
        for variant in range(3):
            for term in range(2):
                place_out = (pl.ds(block * SIDE, SIDE), pl.ds(part * SIDE, SIDE))
                cols_out[(variant, term, *place_out)] = jnp.zeros((SIDE, SIDE), jnp.bfloat16)
    for step in range(3):
        distance = (
            lax.broadcasted_iota(jnp.int32, (SIDE, SIDE), 0)
            - lax.broadcasted_iota(jnp.int32, (SIDE, SIDE), 1)
            + (offset + LEAD - SIDE + step * SIDE)
        )
        pairs = [split(matrix) for matrix in banded(taps, mask_sets, distance)]
        for part in range(2):
            for variant in range(3):
                chosen = variant if variant == 2 * part else 1
                for term in range(2):
                    place_out = (pl.ds((part + step) * SIDE, SIDE), pl.ds(part * SIDE, SIDE))
                    cols_out[(variant, term, *place_out)] = pairs[chosen][term]

    taps = taps_of(0)
    span = STRIP + 2 * HALO
    quarter = BAND_ROWS // segments
    bands = STRIP // BAND_ROWS
    order = lax.broadcasted_iota(jnp.int32, (1, STRIP), 1)
    within = lax.rem(order, bands * quarter)
    owner = lax.div(order, bands * quarter) ^ place[0]
    output = lax.div(within, quarter) * BAND_ROWS + owner * quarter + lax.rem(within, quarter)
    distance = lax.broadcasted_iota(jnp.int32, (span, STRIP), 0) - output + (LEAD - HALO)
    mask_sets = [
        kept(place[0] * rows + first + output, rows * segments) for first in (0, STRIP, rows - STRIP)
    ]
    rest = jnp.zeros((cols_pad(3 * span) - 3 * span, STRIP), jnp.float32)
    for variant, matrix in enumerate(banded(taps, mask_sets, distance)):
        high = matrix.astype(jnp.bfloat16).astype(jnp.float32)
        stacked = jnp.concatenate([high, high, matrix - high, rest], axis=0).T
        rows_out[variant] = stacked.astype(jnp.bfloat16)[:, : 3 * span]


def cols_pad(count):
    return -(-count // 128) * 128


def build_matrices(place, coef, phases, shift, rows, width, segments):
    span = 3 * (STRIP + 2 * HALO)
    smem = pl.BlockSpec(memory_space=pltpu.SMEM)
    vmem = pl.BlockSpec(memory_space=pltpu.VMEM)
    return pl.pallas_call(
        functools.partial(matrices_kernel, rows=rows, width=width, segments=segments),
        out_shape=(
            jax.ShapeDtypeStruct((3, STRIP, span), jnp.bfloat16),
            jax.ShapeDtypeStruct((3, 2, TILE + 2 * SIDE, TILE), jnp.bfloat16),
        ),
        in_specs=[smem] * 4,
        out_specs=(vmem, vmem),
        compiler_params=pltpu.CompilerParams(vmem_limit_bytes=VMEM),
        cost_estimate=COST,
        name="band_matrices",
    )(place, coef, phases, shift)


def filter_kernel(weight, place, *rest, first_chunk, last_chunk, segments, pieces):
    sources, (rows_m, cols_m), refs = rest[: 3 * pieces], rest[3 * pieces : 3 * pieces + 2], rest[3 * pieces + 2 :]
    image, even, odd = sources[:pieces], sources[pieces : 2 * pieces], sources[2 * pieces :]
    *outs, ext_high, ext_low, mat_high, mat_low = refs
    half = pl.program_id(0)
    halves = pl.num_programs(0)
    rows = image[0].shape[0]
    chunk = (pieces - 2) * TILE
    at_left = first_chunk & (half == 0)
    at_right = last_chunk & (half == halves - 1)
    span = STRIP + 2 * HALO
    is_odd = (place[0] & 1) == 1

    column = 0
    for index in range(pieces):
        wide = image[index].shape[1]
        low = jnp.where(is_odd, even[index][...], odd[index][...])
        high = jnp.where(is_odd, odd[index][...], even[index][...])
        for row, value in ((0, low), (HALO, image[index][...]), (HALO + rows, high)):
            if index == 0:
                value = jnp.where(at_left, 0.0, value)
            if index == pieces - 1:
                value = jnp.where(at_right, 0.0, value)
            target = (pl.ds(row, value.shape[0]), pl.ds(column, wide))
            ext_high[target], ext_low[target] = split(value)
        column += wide

    strips = rows // STRIP
    for tile in range((chunk + 2 * SIDE) // TILE):
        columns = pl.ds(tile * TILE, TILE)
        for strip in range(strips):
            window = pl.ds(strip * STRIP, span)
            variant = 0 if strip == 0 else (2 if strip == strips - 1 else 1)
            high = ext_high[window, columns]
            stack = jnp.concatenate([high, ext_low[window, columns], high], axis=0)
            matched = jnp.dot(rows_m[variant], stack, preferred_element_type=jnp.float32)
            high, low = split(matched)
            mat_high[pl.ds(strip * STRIP, STRIP), columns] = high
            mat_low[pl.ds(strip * STRIP, STRIP), columns] = low

    tiles = chunk // TILE
    piece = STRIP // segments
    for tile in range(tiles):
        variant = jnp.int32(1)
        if tile == 0:
            variant = jnp.where(at_left, 0, variant)
        if tile == tiles - 1:
            variant = jnp.where(at_right, 2, variant)
        taps_high = cols_m[variant, 0]
        taps_low = cols_m[variant, 1]
        window = pl.ds(tile * TILE, TILE + 2 * SIDE)
        for strip in range(strips):
            place = pl.ds(strip * STRIP, STRIP)
            high = mat_high[place, window]
            warped = jnp.dot(high, taps_high, preferred_element_type=jnp.float32)
            warped += jnp.dot(mat_low[place, window], taps_high, preferred_element_type=jnp.float32)
            warped += jnp.dot(high, taps_low, preferred_element_type=jnp.float32)
            sent = (weight[0] * warped).astype(jnp.bfloat16)
            for owner, out in enumerate(outs):
                out[pl.ds(strip * piece, piece), pl.ds(tile * TILE, TILE)] = sent[owner * piece : (owner + 1) * piece]


def filter_chunk(weight, place, image, even, odd, rows_m, cols_m, start, chunk, segments):
    rows, width = image.shape
    halves = 2
    half_cols = width // halves
    last = width // SIDE - 1

    def left(h):
        return 0, jnp.maximum((h * half_cols + start) // SIDE - 1, 0)

    def right(h):
        return 0, jnp.minimum((h * half_cols + start + chunk) // SIDE, last)

    def inner(index):
        return lambda h: (0, (h * half_cols + start) // TILE + index)

    def whole(array):
        return pl.BlockSpec(array.shape, lambda h: (0,) * array.ndim)

    pieces = chunk // TILE + 2
    specs = [pl.BlockSpec(memory_space=pltpu.SMEM)] * 2
    operands = [weight, place]
    for source in (image, even, odd):
        count = source.shape[0]
        specs.append(pl.BlockSpec((count, SIDE), left))
        specs += [pl.BlockSpec((count, TILE), inner(index)) for index in range(pieces - 2)]
        specs.append(pl.BlockSpec((count, SIDE), right))
        operands += [source] * pieces
    wide = chunk + 2 * SIDE
    return pl.pallas_call(
        functools.partial(
            filter_kernel,
            first_chunk=start == 0,
            last_chunk=start + chunk == width // halves,
            segments=segments,
            pieces=pieces,
        ),
        out_shape=[jax.ShapeDtypeStruct((rows // segments, halves * chunk), jnp.bfloat16)] * segments,
        grid=(halves,),
        in_specs=specs + [whole(rows_m), whole(cols_m)],
        out_specs=[pl.BlockSpec((rows // segments, chunk), lambda h: (0, h))] * segments,
        scratch_shapes=[
            pltpu.VMEM((rows + 2 * HALO, wide), jnp.bfloat16),
            pltpu.VMEM((rows + 2 * HALO, wide), jnp.bfloat16),
            pltpu.VMEM((rows, wide), jnp.bfloat16),
            pltpu.VMEM((rows, wide), jnp.bfloat16),
        ],
        compiler_params=pltpu.CompilerParams(vmem_limit_bytes=VMEM),
        cost_estimate=COST,
        name="warp_filter",
    )(*operands, rows_m, cols_m)


def join_kernel(*refs):
    block = refs[0].shape[0]
    for step, ref in enumerate(refs[:-1]):
        refs[-1][pl.ds(step * block, block), :] = ref[...]


def joined(blocks):
    block, columns = blocks[0].shape
    vmem = pl.BlockSpec(memory_space=pltpu.VMEM)
    return pl.pallas_call(
        join_kernel,
        out_shape=jax.ShapeDtypeStruct((len(blocks) * block, columns), blocks[0].dtype),
        in_specs=[vmem] * len(blocks),
        out_specs=vmem,
        compiler_params=pltpu.CompilerParams(vmem_limit_bytes=VMEM),
        cost_estimate=COST,
        name="join_blocks",
    )(*blocks)


def stage_distances(lines):
    stages = []
    step = 1
    while step < lines:
        stages.append(list(reversed(range(step, lines, 2 * step))))
        step *= 2
    return stages


def pair_kernel(place, table, mine, other, *rest, slots, distances, quarter):
    *outs, mine_all, other_all = rest
    rows = mine.shape[0]
    chunk = outs[0].shape[1]
    count = table.shape[0] // 3
    for source, held in ((mine, mine_all), (other, other_all)):
        held[pl.ds(0, rows), :] = source[...].astype(jnp.float32)
        held[pl.ds(rows, quarter), :] = jnp.zeros((quarter, source.shape[1]), jnp.float32)
    line = place[1]

    for distance, out in zip(distances, outs):
        first = (line ^ distance) * slots

        def summed(slot, first=first):
            column = pl.ds(pl.multiple_of(table[first + slot] * chunk, 128), chunk)
            from_mine = pl.ds(pl.multiple_of(table[count + first + slot], quarter), quarter)
            from_other = pl.ds(pl.multiple_of(table[2 * count + first + slot], quarter), quarter)
            return mine_all[from_mine, column] + other_all[from_other, column]

        for slot in range(0, slots - 1, 2):
            rows_two = jnp.concatenate([summed(slot), summed(slot + 1)], axis=0)
            out[pl.ds(slot * quarter, 2 * quarter), :] = rows_two.astype(jnp.bfloat16)
        if slots % 2:
            out[pl.ds((slots - 1) * quarter, quarter), :] = summed(slots - 1).astype(jnp.bfloat16)


def pair_sum(place, table, mine, other, slots, lines, quarter):
    rows, double = mine.shape
    chunk = double // 2
    distances = sum(stage_distances(lines), []) + [0]
    smem = pl.BlockSpec(memory_space=pltpu.SMEM)
    vmem = pl.BlockSpec(memory_space=pltpu.VMEM)
    outs = pl.pallas_call(
        functools.partial(pair_kernel, slots=slots, distances=distances, quarter=quarter),
        out_shape=[jax.ShapeDtypeStruct((slots * quarter, chunk), jnp.bfloat16)] * lines,
        in_specs=[smem, smem, vmem, vmem],
        out_specs=[vmem] * lines,
        scratch_shapes=[pltpu.VMEM((rows + quarter, double), jnp.float32)] * 2,
        compiler_params=pltpu.CompilerParams(vmem_limit_bytes=VMEM),
        cost_estimate=COST,
        name="pair_sum",
    )(place, table, mine, other)
    return dict(zip(distances, outs))


def weight_kernel(place, sites, facts, out, covers, *, cores, quarter, width, bands):
    slots = out.shape[0] // quarter
    half_cols = out.shape[1]
    exposures = facts.shape[0]
    owner = place[1] * cores + place[2]
    column = lax.broadcasted_iota(jnp.int32, (quarter, half_cols), 1)
    for half in range(2):
        for exposure in range(exposures):
            first = facts[exposure, 0].astype(jnp.int32) - half * half_cols
            inside = (column >= first) & (column < first + width)
            covers[half * exposures + exposure] = jnp.where(inside, facts[exposure, 2], 0.0)

    def one_slot(slot, carry):
        site = sites[owner * slots + slot]
        total = jnp.zeros((quarter, half_cols), jnp.float32)
        for exposure in range(exposures):
            relative = lax.shift_right_logical(site, 1) - facts[exposure, 1].astype(jnp.int32)
            present = jnp.where((relative >= 0) & (relative < bands), jnp.float32(1.0), jnp.float32(0.0))
            total = total + present * covers[(site & 1) * exposures + exposure]
        out[pl.ds(pl.multiple_of(slot * quarter, quarter), quarter), :] = jnp.maximum(total, 1.0)
        return carry

    lax.fori_loop(0, slots, one_slot, 0)


def patch_weights(place, sites, facts, slots, quarter, cores, width, bands):
    smem = pl.BlockSpec(memory_space=pltpu.SMEM)
    return pl.pallas_call(
        functools.partial(weight_kernel, cores=cores, quarter=quarter, width=width, bands=bands),
        out_shape=jax.ShapeDtypeStruct((slots * quarter, width // 2), jnp.float32),
        in_specs=[smem] * 3,
        out_specs=pl.BlockSpec(memory_space=pltpu.VMEM),
        scratch_shapes=[pltpu.VMEM((2 * facts.shape[0], quarter, width // 2), jnp.float32)],
        compiler_params=pltpu.CompilerParams(vmem_limit_bytes=VMEM),
        cost_estimate=COST,
        name="patch_weights",
    )(place, sites, facts)


def finish_kernel(*refs, count):
    pieces, scale, out = refs[:count], refs[count], refs[-1]
    total = pieces[0][...].astype(jnp.float32)
    for piece in pieces[1:]:
        total += piece[...].astype(jnp.float32)
    out[...] = total / scale[...]


def finish_chunk(pieces, scale, result, start):
    rows, chunk = pieces[0].shape
    column = pl.BlockSpec((rows, chunk), lambda i: (0, start // chunk))
    specs = [pl.BlockSpec((rows, chunk), lambda i: (0, 0))] * len(pieces) + [column]
    operands = [*pieces, scale]
    aliases = {}
    if result is not None:
        specs.append(pl.BlockSpec(memory_space=pl.ANY))
        aliases = {len(operands): 0}
        operands.append(result)
    return pl.pallas_call(
        functools.partial(finish_kernel, count=len(pieces)),
        out_shape=jax.ShapeDtypeStruct(scale.shape, jnp.float32),
        grid=(1,),
        in_specs=specs,
        out_specs=column,
        input_output_aliases=aliases,
        compiler_params=pltpu.CompilerParams(vmem_limit_bytes=VMEM),
        cost_estimate=pl.CostEstimate(
            flops=len(pieces) * rows * chunk, bytes_accessed=rows * chunk * (2 * len(pieces) + 8), transcendentals=0
        ),
        name="patch_mean",
    )(*operands)


def swapped(value, axis, distance):
    count = lax.axis_size(axis)
    return lax.ppermute(value, axis, [(i, i ^ distance) for i in range(count)])


def scatter_sum(pieces):
    pieces = dict(pieces)
    kept, added = [pieces[0]], []
    for stage, distances in enumerate(stage_distances(len(pieces))):
        for distance in distances:
            received = swapped(pieces[distance], "line", 1 << stage)
            target = distance ^ (1 << stage)
            if target:
                both = pieces[target].astype(jnp.float32) + received.astype(jnp.float32)
                pieces[target] = both.astype(jnp.bfloat16)
                added = [pieces[target]]
            else:
                kept.append(received)
    return kept, added


def per_device(images, psf_coef, phases, col_shift, band_offset, exposure_weight, patch_site):
    image = images[0]
    rows, width = image.shape
    segments = lax.axis_size("seg")
    lines = lax.axis_size("line")
    cores = lax.axis_size("core")
    quarter = BAND_ROWS // segments
    half_cols = width // 2
    slots = patch_site.shape[0] // (lines * cores)
    bands = segments * rows // BAND_ROWS
    place = jnp.stack([lax.axis_index(axis) for axis in ("seg", "line", "core")]).astype(jnp.int32)

    def pairs_from(first):
        pairs = [(i, i + 1) for i in range(first, segments - 1, 2)]
        return pairs + [(j, i) for i, j in pairs]

    is_odd = (place[0] & 1) == 1
    top, bottom = image[:HALO], image[rows - HALO :]
    even = lax.ppermute(jnp.where(is_odd, top, bottom), "seg", pairs_from(0))
    odd = lax.ppermute(jnp.where(is_odd, bottom, top), "seg", pairs_from(1))
    rows_m, cols_m = build_matrices(place, psf_coef, phases, col_shift, rows, width, segments)
    weight = exposure_weight.astype(jnp.float32)

    chunks = []
    start = 0
    for part in PARTS:
        chunks.append((start, half_cols * part // WHOLE))
        start += half_cols * part // WHOLE
    other_offset = swapped(band_offset, "core", 1)
    sites = lax.dynamic_index_in_dim(patch_site.reshape(lines, cores, slots), place[2], 1, keepdims=False).reshape(-1)
    here = rows // BAND_ROWS

    def rows_from(offset):
        relative = sites // 2 - offset
        held = ((relative // here) ^ place[0]) * here + relative % here
        return jnp.where((relative >= 0) & (relative < bands), held, bands) * quarter

    table = jnp.concatenate([sites % 2, rows_from(band_offset), rows_from(other_offset)])
    facts = jnp.stack([col_shift.astype(jnp.float32), band_offset.astype(jnp.float32), weight], axis=1)
    facts = jnp.concatenate([facts, swapped(facts, "core", 1)], axis=0)
    step = 1
    while step < lines:
        facts = jnp.concatenate([facts, swapped(facts, "line", step)], axis=0)
        step *= 2
    scale = patch_weights(place, patch_site, facts, slots, quarter, cores, width, bands)

    def tied(values, others):
        return lax.optimization_barrier((values, others))[0]

    result = None
    count = len(chunks)
    sent, sums, kept, added = [None] * count, [None] * count, [None] * count, [None] * count

    def filtered(index):
        start, chunk = chunks[index]
        held = tied(weight, sums[index - 2]) if index >= 2 else weight
        sent[index] = filter_chunk(held, place, image, even, odd, rows_m, cols_m, start, chunk, segments)

    filtered(0)
    for index, (start, chunk) in enumerate(chunks):
        outgoing = sent[index]
        received = [swapped(outgoing[d], "seg", d) for d in range(1, segments)]
        if index + 1 < count:
            filtered(index + 1)
            received = tied(received, sent[index + 1])
        if index == 0:
            received = tied(received, scale)
        if index >= 1:
            received = tied(received, kept[index - 1])
        mine = joined([outgoing[0]] + received)
        other = swapped(mine, "core", 1)
        sums[index] = pair_sum(place, table, mine, other, slots, lines, quarter)
        kept[index], added[index] = scatter_sum(sums[index])
        result = finish_chunk(kept[index], scale, result, start)
    return result.reshape(slots, quarter, half_cols)


def solution(mesh):
    segments, exposures = mesh.shape["seg"], mesh.shape["exp"]
    parted = Mesh(mesh.devices.reshape(segments, exposures // 2, 2), ("seg", "line", "core"))
    spread = ("line", "core")
    placed = (
        P(spread, "seg", None),
        P(spread, None, None),
        P(spread, None),
        P(spread),
        P(spread),
        P(spread),
        P(),
    )
    return jax.shard_map(
        per_device, mesh=parted, in_specs=placed, out_specs=P(spread, "seg", None), check_vma=False
    )
```

```python
import functools

import jax
import jax.numpy as jnp
import numpy as np
from jax import lax
from jax.experimental import pallas as pl
from jax.experimental.pallas import tpu as pltpu
from jax.sharding import Mesh, PartitionSpec as P

BAND_ROWS = 32
TAPS = 21
PHASES = 16
LANCZOS = 6
SPAN = TAPS + LANCZOS - 1
LEAD = TAPS // 2 + 2
HALO = 16
SIDE = 128
TILE = 256
STRIP = 128
PARTS = (2, 2)
VMEM = 48 * 1024 * 1024
COST = pl.CostEstimate(flops=1, bytes_accessed=1, transcendentals=0)

sigmas = (1.0, 2.0, 3.5)


def basis_table():
    offsets = np.arange(TAPS) - TAPS // 2
    curves = [np.exp(-offsets * offsets / (2.0 * spread * spread)) for spread in sigmas]
    return [[float(value) for value in curve / curve.sum()] for curve in curves]


def lanczos_table():
    shifted = np.arange(LANCZOS)[None, :] - 2.0 - np.arange(PHASES)[:, None] / PHASES
    values = np.sinc(shifted) * np.sinc(shifted / 3.0)
    return (values / values.sum(axis=1, keepdims=True)).astype(np.float32)


def lanczos_taps(phase):
    table = lanczos_table()
    taps = []
    for n in range(LANCZOS):
        tap = jnp.float32(table[0, n])
        for index in range(1, PHASES):
            tap = jnp.where(phase == index, jnp.float32(table[index, n]), tap)
        taps.append(tap)
    return taps


def split(value):
    high = value.astype(jnp.bfloat16)
    return high, (value - high.astype(jnp.float32)).astype(jnp.bfloat16)


def banded(taps, mask_sets, distance):
    kernel, lanczos = taps
    sets = [[jnp.where(mask, lanczos[n], 0.0) for n, mask in enumerate(masks)] for masks in mask_sets]
    matrices = [jnp.zeros(distance.shape, jnp.float32) for _ in sets]
    for t in range(SPAN):
        here = distance == t
        for index, weighted in enumerate(sets):
            row = jnp.zeros_like(weighted[0])
            for n in range(LANCZOS):
                if 0 <= t - n < TAPS:
                    row = row + kernel[t - n] * weighted[n]
            matrices[index] = jnp.where(here, row, matrices[index])
    return matrices


def matrices_kernel(place, coef, phases, shift, rows_out, cols_out, *, rows, width, segments):
    basis = basis_table()

    def taps_of(axis):
        kernel = [sum(coef[0, axis, k] * basis[k][t] for k in range(len(sigmas))) for t in range(TAPS)]
        return kernel, lanczos_taps(phases[0, axis])

    def kept(matched, extent):
        return [(matched + (n - 2) >= 0) & (matched + (n - 2) < extent) for n in range(LANCZOS)]

    taps = taps_of(1)
    offset = shift[0]
    column = lax.broadcasted_iota(jnp.int32, (1, SIDE), 1)
    everything = [jnp.full((1, SIDE), True)] * LANCZOS
    mask_sets = [kept(column - offset, width), everything, kept(column + (width - SIDE) - offset, width)]
    for part, block in ((0, 3), (1, 0)):
        for variant in range(3):
            for term in range(2):
                place_out = (pl.ds(block * SIDE, SIDE), pl.ds(part * SIDE, SIDE))
                cols_out[(variant, term, *place_out)] = jnp.zeros((SIDE, SIDE), jnp.bfloat16)
    for step in range(3):
        distance = (
            lax.broadcasted_iota(jnp.int32, (SIDE, SIDE), 0)
            - lax.broadcasted_iota(jnp.int32, (SIDE, SIDE), 1)
            + (offset + LEAD - SIDE + step * SIDE)
        )
        pairs = [split(matrix) for matrix in banded(taps, mask_sets, distance)]
        for part in range(2):
            for variant in range(3):
                chosen = variant if variant == 2 * part else 1
                for term in range(2):
                    place_out = (pl.ds((part + step) * SIDE, SIDE), pl.ds(part * SIDE, SIDE))
                    cols_out[(variant, term, *place_out)] = pairs[chosen][term]

    taps = taps_of(0)
    span = STRIP + 2 * HALO
    quarter = BAND_ROWS // segments
    bands = STRIP // BAND_ROWS
    order = lax.broadcasted_iota(jnp.int32, (1, STRIP), 1)
    within = lax.rem(order, bands * quarter)
    owner = lax.div(order, bands * quarter) ^ place[0]
    output = lax.div(within, quarter) * BAND_ROWS + owner * quarter + lax.rem(within, quarter)
    distance = lax.broadcasted_iota(jnp.int32, (span, STRIP), 0) - output + (LEAD - HALO)
    mask_sets = [
        kept(place[0] * rows + first + output, rows * segments) for first in (0, STRIP, rows - STRIP)
    ]
    rest = jnp.zeros((cols_pad(3 * span) - 3 * span, STRIP), jnp.float32)
    for variant, matrix in enumerate(banded(taps, mask_sets, distance)):
        high = matrix.astype(jnp.bfloat16).astype(jnp.float32)
        stacked = jnp.concatenate([high, high, matrix - high, rest], axis=0).T
        rows_out[variant] = stacked.astype(jnp.bfloat16)[:, : 3 * span]


def cols_pad(count):
    return -(-count // 128) * 128


def build_matrices(place, coef, phases, shift, rows, width, segments):
    span = 3 * (STRIP + 2 * HALO)
    smem = pl.BlockSpec(memory_space=pltpu.SMEM)
    vmem = pl.BlockSpec(memory_space=pltpu.VMEM)
    return pl.pallas_call(
        functools.partial(matrices_kernel, rows=rows, width=width, segments=segments),
        out_shape=(
            jax.ShapeDtypeStruct((3, STRIP, span), jnp.bfloat16),
            jax.ShapeDtypeStruct((3, 2, TILE + 2 * SIDE, TILE), jnp.bfloat16),
        ),
        in_specs=[smem] * 4,
        out_specs=(vmem, vmem),
        compiler_params=pltpu.CompilerParams(vmem_limit_bytes=VMEM),
        cost_estimate=COST,
        name="band_matrices",
    )(place, coef, phases, shift)


def filter_kernel(
    weight, low_l, low_c, low_r, mid_l, mid_c, mid_r, high_l, high_c, high_r, rows_m, cols_m, *rest,
    first_chunk, last_chunk, segments,
):
    *outs, ext_high, ext_low, mat_high, mat_low = rest
    half = pl.program_id(0)
    halves = pl.num_programs(0)
    rows, chunk = mid_c.shape
    at_left = first_chunk & (half == 0)
    at_right = last_chunk & (half == halves - 1)
    span = STRIP + 2 * HALO

    for row, parts in (
        (0, (low_l, low_c, low_r)),
        (HALO, (mid_l, mid_c, mid_r)),
        (HALO + rows, (high_l, high_c, high_r)),
    ):
        count = parts[0].shape[0]
        for part, column, outside in zip(parts, (0, SIDE, SIDE + chunk), (at_left, False, at_right)):
            value = part[...].astype(jnp.float32)
            if outside is not False:
                value = jnp.where(outside, 0.0, value)
            high, low = split(value)
            place = (pl.ds(row, count), pl.ds(column, value.shape[1]))
            ext_high[place] = high
            ext_low[place] = low

    strips = rows // STRIP
    for tile in range((chunk + 2 * SIDE) // TILE):
        columns = pl.ds(tile * TILE, TILE)
        for strip in range(strips):
            window = pl.ds(strip * STRIP, span)
            variant = 0 if strip == 0 else (2 if strip == strips - 1 else 1)
            high = ext_high[window, columns]
            stack = jnp.concatenate([high, ext_low[window, columns], high], axis=0)
            matched = jnp.dot(rows_m[variant], stack, preferred_element_type=jnp.float32)
            high, low = split(matched)
            mat_high[pl.ds(strip * STRIP, STRIP), columns] = high
            mat_low[pl.ds(strip * STRIP, STRIP), columns] = low

    tiles = chunk // TILE
    piece = STRIP // segments
    for tile in range(tiles):
        variant = jnp.int32(1)
        if tile == 0:
            variant = jnp.where(at_left, 0, variant)
        if tile == tiles - 1:
            variant = jnp.where(at_right, 2, variant)
        taps_high = cols_m[variant, 0]
        taps_low = cols_m[variant, 1]
        window = pl.ds(tile * TILE, TILE + 2 * SIDE)
        for strip in range(strips):
            place = pl.ds(strip * STRIP, STRIP)
            high = mat_high[place, window]
            warped = jnp.dot(high, taps_high, preferred_element_type=jnp.float32)
            warped += jnp.dot(mat_low[place, window], taps_high, preferred_element_type=jnp.float32)
            warped += jnp.dot(high, taps_low, preferred_element_type=jnp.float32)
            sent = (weight[0] * warped).astype(jnp.bfloat16)
            for owner, out in enumerate(outs):
                out[pl.ds(strip * piece, piece), pl.ds(tile * TILE, TILE)] = sent[owner * piece : (owner + 1) * piece]


def filter_chunk(weight, low, image, high, rows_m, cols_m, start, chunk, segments):
    rows, width = image.shape
    halves = 2
    half_blocks = width // halves // SIDE
    first = start // SIDE
    blocks = chunk // SIDE
    last = width // SIDE - 1

    def left(h):
        return 0, jnp.maximum(h * half_blocks + first - 1, 0)

    def centre(h):
        return 0, h * (half_blocks // blocks) + start // chunk

    def right(h):
        return 0, jnp.minimum(h * half_blocks + first + blocks, last)

    def whole(array):
        return pl.BlockSpec(array.shape, lambda h: (0,) * array.ndim)

    specs = [pl.BlockSpec(memory_space=pltpu.SMEM)]
    for source in (low, image, high):
        specs += [
            pl.BlockSpec((source.shape[0], SIDE), left),
            pl.BlockSpec((source.shape[0], chunk), centre),
            pl.BlockSpec((source.shape[0], SIDE), right),
        ]
    wide = chunk + 2 * SIDE
    return pl.pallas_call(
        functools.partial(
            filter_kernel,
            first_chunk=start == 0,
            last_chunk=start + chunk == width // halves,
            segments=segments,
        ),
        out_shape=[jax.ShapeDtypeStruct((rows // segments, halves * chunk), jnp.bfloat16)] * segments,
        grid=(halves,),
        in_specs=specs + [whole(rows_m), whole(cols_m)],
        out_specs=[pl.BlockSpec((rows // segments, chunk), lambda h: (0, h))] * segments,
        scratch_shapes=[
            pltpu.VMEM((rows + 2 * HALO, wide), jnp.bfloat16),
            pltpu.VMEM((rows + 2 * HALO, wide), jnp.bfloat16),
            pltpu.VMEM((rows, wide), jnp.bfloat16),
            pltpu.VMEM((rows, wide), jnp.bfloat16),
        ],
        compiler_params=pltpu.CompilerParams(vmem_limit_bytes=VMEM),
        cost_estimate=COST,
        name="warp_filter",
    )(weight, *([low] * 3), *([image] * 3), *([high] * 3), rows_m, cols_m)


def join_kernel(*refs):
    block = refs[0].shape[0]
    for step, ref in enumerate(refs[:-1]):
        refs[-1][pl.ds(step * block, block), :] = ref[...]


def joined(blocks):
    block, columns = blocks[0].shape
    vmem = pl.BlockSpec(memory_space=pltpu.VMEM)
    return pl.pallas_call(
        join_kernel,
        out_shape=jax.ShapeDtypeStruct((len(blocks) * block, columns), blocks[0].dtype),
        in_specs=[vmem] * len(blocks),
        out_specs=vmem,
        compiler_params=pltpu.CompilerParams(vmem_limit_bytes=VMEM),
        cost_estimate=COST,
        name="join_blocks",
    )(*blocks)


def stage_distances(lines):
    stages = []
    step = 1
    while step < lines:
        stages.append(list(reversed(range(step, lines, 2 * step))))
        step *= 2
    return stages


def pair_kernel(place, table, mine, other, *rest, slots, distances, quarter):
    *outs, mine_all, other_all = rest
    rows = mine.shape[0]
    chunk = outs[0].shape[1]
    count = table.shape[0] // 3
    for source, held in ((mine, mine_all), (other, other_all)):
        held[pl.ds(0, rows), :] = source[...].astype(jnp.float32)
        held[pl.ds(rows, quarter), :] = jnp.zeros((quarter, source.shape[1]), jnp.float32)
    line = place[1]

    for distance, out in zip(distances, outs):
        first = (line ^ distance) * slots

        def summed(slot, first=first):
            column = pl.ds(pl.multiple_of(table[first + slot] * chunk, 128), chunk)
            from_mine = pl.ds(pl.multiple_of(table[count + first + slot], quarter), quarter)
            from_other = pl.ds(pl.multiple_of(table[2 * count + first + slot], quarter), quarter)
            return mine_all[from_mine, column] + other_all[from_other, column]

        for slot in range(0, slots - 1, 2):
            rows_two = jnp.concatenate([summed(slot), summed(slot + 1)], axis=0)
            out[pl.ds(slot * quarter, 2 * quarter), :] = rows_two.astype(jnp.bfloat16)
        if slots % 2:
            out[pl.ds((slots - 1) * quarter, quarter), :] = summed(slots - 1).astype(jnp.bfloat16)


def pair_sum(place, table, mine, other, slots, lines, quarter):
    rows, double = mine.shape
    chunk = double // 2
    distances = sum(stage_distances(lines), []) + [0]
    smem = pl.BlockSpec(memory_space=pltpu.SMEM)
    vmem = pl.BlockSpec(memory_space=pltpu.VMEM)
    outs = pl.pallas_call(
        functools.partial(pair_kernel, slots=slots, distances=distances, quarter=quarter),
        out_shape=[jax.ShapeDtypeStruct((slots * quarter, chunk), jnp.bfloat16)] * lines,
        in_specs=[smem, smem, vmem, vmem],
        out_specs=[vmem] * lines,
        scratch_shapes=[pltpu.VMEM((rows + quarter, double), jnp.float32)] * 2,
        compiler_params=pltpu.CompilerParams(vmem_limit_bytes=VMEM),
        cost_estimate=COST,
        name="pair_sum",
    )(place, table, mine, other)
    return dict(zip(distances, outs))


def weight_kernel(place, sites, facts, out, covers, *, cores, quarter, width, bands):
    slots = out.shape[0] // quarter
    half_cols = out.shape[1]
    exposures = facts.shape[0]
    owner = place[1] * cores + place[2]
    column = lax.broadcasted_iota(jnp.int32, (quarter, half_cols), 1)
    for half in range(2):
        for exposure in range(exposures):
            first = facts[exposure, 0].astype(jnp.int32) - half * half_cols
            inside = (column >= first) & (column < first + width)
            covers[half * exposures + exposure] = jnp.where(inside, facts[exposure, 2], 0.0)

    def one_slot(slot, carry):
        site = sites[owner * slots + slot]
        total = jnp.zeros((quarter, half_cols), jnp.float32)
        for exposure in range(exposures):
            relative = lax.shift_right_logical(site, 1) - facts[exposure, 1].astype(jnp.int32)
            present = jnp.where((relative >= 0) & (relative < bands), jnp.float32(1.0), jnp.float32(0.0))
            total = total + present * covers[(site & 1) * exposures + exposure]
        out[pl.ds(pl.multiple_of(slot * quarter, quarter), quarter), :] = jnp.maximum(total, 1.0)
        return carry

    lax.fori_loop(0, slots, one_slot, 0)


def patch_weights(place, sites, facts, slots, quarter, cores, width, bands):
    smem = pl.BlockSpec(memory_space=pltpu.SMEM)
    return pl.pallas_call(
        functools.partial(weight_kernel, cores=cores, quarter=quarter, width=width, bands=bands),
        out_shape=jax.ShapeDtypeStruct((slots * quarter, width // 2), jnp.float32),
        in_specs=[smem] * 3,
        out_specs=pl.BlockSpec(memory_space=pltpu.VMEM),
        scratch_shapes=[pltpu.VMEM((2 * facts.shape[0], quarter, width // 2), jnp.float32)],
        compiler_params=pltpu.CompilerParams(vmem_limit_bytes=VMEM),
        cost_estimate=COST,
        name="patch_weights",
    )(place, sites, facts)


def finish_kernel(*refs, count):
    pieces, scale, out = refs[:count], refs[count], refs[-1]
    total = pieces[0][...].astype(jnp.float32)
    for piece in pieces[1:]:
        total += piece[...].astype(jnp.float32)
    out[...] = total / scale[...]


def finish_chunk(pieces, scale, result, start):
    rows, chunk = pieces[0].shape
    column = pl.BlockSpec((rows, chunk), lambda i: (0, start // chunk))
    specs = [pl.BlockSpec((rows, chunk), lambda i: (0, 0))] * len(pieces) + [column]
    operands = [*pieces, scale]
    aliases = {}
    if result is not None:
        specs.append(pl.BlockSpec(memory_space=pl.ANY))
        aliases = {len(operands): 0}
        operands.append(result)
    return pl.pallas_call(
        functools.partial(finish_kernel, count=len(pieces)),
        out_shape=jax.ShapeDtypeStruct(scale.shape, jnp.float32),
        grid=(1,),
        in_specs=specs,
        out_specs=column,
        input_output_aliases=aliases,
        compiler_params=pltpu.CompilerParams(vmem_limit_bytes=VMEM),
        cost_estimate=pl.CostEstimate(
            flops=len(pieces) * rows * chunk, bytes_accessed=rows * chunk * (2 * len(pieces) + 8), transcendentals=0
        ),
        name="patch_mean",
    )(*operands)


def swapped(value, axis, distance):
    count = lax.axis_size(axis)
    return lax.ppermute(value, axis, [(i, i ^ distance) for i in range(count)])


def scatter_sum(pieces):
    pieces = dict(pieces)
    kept, added = [pieces[0]], []
    for stage, distances in enumerate(stage_distances(len(pieces))):
        for distance in distances:
            received = swapped(pieces[distance], "line", 1 << stage)
            target = distance ^ (1 << stage)
            if target:
                both = pieces[target].astype(jnp.float32) + received.astype(jnp.float32)
                pieces[target] = both.astype(jnp.bfloat16)
                added = [pieces[target]]
            else:
                kept.append(received)
    return kept, added


def per_device(images, psf_coef, phases, col_shift, band_offset, exposure_weight, patch_site):
    image = images[0]
    rows, width = image.shape
    segments = lax.axis_size("seg")
    lines = lax.axis_size("line")
    cores = lax.axis_size("core")
    quarter = BAND_ROWS // segments
    half_cols = width // 2
    slots = patch_site.shape[0] // (lines * cores)
    bands = segments * rows // BAND_ROWS
    place = jnp.stack([lax.axis_index(axis) for axis in ("seg", "line", "core")]).astype(jnp.int32)

    forward = [(i, i + 1) for i in range(segments - 1)]
    backward = [(i + 1, i) for i in range(segments - 1)]
    low = lax.ppermute(image[rows - HALO :].astype(jnp.bfloat16), "seg", forward)
    high = lax.ppermute(image[:HALO].astype(jnp.bfloat16), "seg", backward)
    rows_m, cols_m = build_matrices(place, psf_coef, phases, col_shift, rows, width, segments)
    weight = exposure_weight.astype(jnp.float32)

    chunks = []
    start = 0
    for part in PARTS:
        chunks.append((start, half_cols // part))
        start += half_cols // part
    other_offset = swapped(band_offset, "core", 1)
    sites = lax.dynamic_index_in_dim(patch_site.reshape(lines, cores, slots), place[2], 1, keepdims=False).reshape(-1)
    here = rows // BAND_ROWS

    def rows_from(offset):
        relative = sites // 2 - offset
        held = ((relative // here) ^ place[0]) * here + relative % here
        return jnp.where((relative >= 0) & (relative < bands), held, bands) * quarter

    table = jnp.concatenate([sites % 2, rows_from(band_offset), rows_from(other_offset)])
    facts = jnp.stack([col_shift.astype(jnp.float32), band_offset.astype(jnp.float32), weight], axis=1)
    facts = jnp.concatenate([facts, swapped(facts, "core", 1)], axis=0)
    early = facts
    step = 1
    while step < lines:
        early = facts
        facts = jnp.concatenate([facts, swapped(facts, "line", step)], axis=0)
        step *= 2
    scale = patch_weights(place, patch_site, facts, slots, quarter, cores, width, bands)

    def tied(values, others):
        return lax.optimization_barrier((values, others))[0]

    result = None
    count = len(chunks)
    sent, sums, kept, added = [None] * count, [None] * count, [None] * count, [None] * count

    def filtered(index):
        start, chunk = chunks[index]
        held = tied(weight, sums[index - 2]) if index >= 2 else weight
        sent[index] = filter_chunk(held, low, image, high, rows_m, cols_m, start, chunk, segments)

    filtered(0)
    for index, (start, chunk) in enumerate(chunks):
        outgoing = sent[index]
        received = [swapped(outgoing[d], "seg", d) for d in range(1, segments)]
        if index + 1 < count:
            filtered(index + 1)
            received = tied(received, sent[index + 1])
        if index == 0:
            received = tied(received, early)
        if index == 1:
            received = tied(received, scale)
        if index >= 1:
            received = tied(received, (added[index - 1], kept[index - 1][:-1]))
        mine = joined([outgoing[0]] + received)
        other = swapped(mine, "core", 1)
        sums[index] = pair_sum(place, table, mine, other, slots, lines, quarter)
        kept[index], added[index] = scatter_sum(sums[index])
        result = finish_chunk(kept[index], scale, result, start)
    return result.reshape(slots, quarter, half_cols)


def solution(mesh):
    segments, exposures = mesh.shape["seg"], mesh.shape["exp"]
    parted = Mesh(mesh.devices.reshape(segments, exposures // 2, 2), ("seg", "line", "core"))
    spread = ("line", "core")
    placed = (
        P(spread, "seg", None),
        P(spread, None, None),
        P(spread, None),
        P(spread),
        P(spread),
        P(spread),
        P(),
    )
    return jax.shard_map(
        per_device, mesh=parted, in_specs=placed, out_specs=P(spread, "seg", None), check_vma=False
    )
```

```python
import functools

import jax
import jax.numpy as jnp
import numpy as np
from jax import lax
from jax.experimental import pallas as pl
from jax.experimental.pallas import tpu as pltpu
from jax.sharding import Mesh, PartitionSpec as P

BAND_ROWS = 32
TAPS = 21
PHASES = 16
LANCZOS = 6
SPAN = TAPS + LANCZOS - 1
LEAD = TAPS // 2 + 2
HALO = 16
SIDE = 128
TILE = 256
STRIP = 128
PARTS = (2, 2)
VMEM = 48 * 1024 * 1024
COST = pl.CostEstimate(flops=1, bytes_accessed=1, transcendentals=0)

sigmas = (1.0, 2.0, 3.5)


def basis_table():
    offsets = np.arange(TAPS) - TAPS // 2
    curves = [np.exp(-offsets * offsets / (2.0 * spread * spread)) for spread in sigmas]
    return [[float(value) for value in curve / curve.sum()] for curve in curves]


def lanczos_table():
    shifted = np.arange(LANCZOS)[None, :] - 2.0 - np.arange(PHASES)[:, None] / PHASES
    values = np.sinc(shifted) * np.sinc(shifted / 3.0)
    return (values / values.sum(axis=1, keepdims=True)).astype(np.float32)


def lanczos_taps(phase):
    table = lanczos_table()
    taps = []
    for n in range(LANCZOS):
        tap = jnp.float32(table[0, n])
        for index in range(1, PHASES):
            tap = jnp.where(phase == index, jnp.float32(table[index, n]), tap)
        taps.append(tap)
    return taps


def split(value):
    high = value.astype(jnp.bfloat16)
    return high, (value - high.astype(jnp.float32)).astype(jnp.bfloat16)


def banded(taps, mask_sets, distance):
    kernel, lanczos = taps
    sets = [[jnp.where(mask, lanczos[n], 0.0) for n, mask in enumerate(masks)] for masks in mask_sets]
    matrices = [jnp.zeros(distance.shape, jnp.float32) for _ in sets]
    for t in range(SPAN):
        here = distance == t
        for index, weighted in enumerate(sets):
            row = jnp.zeros_like(weighted[0])
            for n in range(LANCZOS):
                if 0 <= t - n < TAPS:
                    row = row + kernel[t - n] * weighted[n]
            matrices[index] = jnp.where(here, row, matrices[index])
    return matrices


def matrices_kernel(place, coef, phases, shift, rows_out, cols_out, *, rows, width, segments):
    basis = basis_table()

    def taps_of(axis):
        kernel = [sum(coef[0, axis, k] * basis[k][t] for k in range(len(sigmas))) for t in range(TAPS)]
        return kernel, lanczos_taps(phases[0, axis])

    def kept(matched, extent):
        return [(matched + (n - 2) >= 0) & (matched + (n - 2) < extent) for n in range(LANCZOS)]

    taps = taps_of(1)
    offset = shift[0]
    column = lax.broadcasted_iota(jnp.int32, (1, SIDE), 1)
    everything = [jnp.full((1, SIDE), True)] * LANCZOS
    mask_sets = [kept(column - offset, width), everything, kept(column + (width - SIDE) - offset, width)]
    for part, block in ((0, 3), (1, 0)):
        for variant in range(3):
            for term in range(2):
                place_out = (pl.ds(block * SIDE, SIDE), pl.ds(part * SIDE, SIDE))
                cols_out[(variant, term, *place_out)] = jnp.zeros((SIDE, SIDE), jnp.bfloat16)
    for step in range(3):
        distance = (
            lax.broadcasted_iota(jnp.int32, (SIDE, SIDE), 0)
            - lax.broadcasted_iota(jnp.int32, (SIDE, SIDE), 1)
            + (offset + LEAD - SIDE + step * SIDE)
        )
        pairs = [split(matrix) for matrix in banded(taps, mask_sets, distance)]
        for part in range(2):
            for variant in range(3):
                chosen = variant if variant == 2 * part else 1
                for term in range(2):
                    place_out = (pl.ds((part + step) * SIDE, SIDE), pl.ds(part * SIDE, SIDE))
                    cols_out[(variant, term, *place_out)] = pairs[chosen][term]

    taps = taps_of(0)
    span = STRIP + 2 * HALO
    quarter = BAND_ROWS // segments
    bands = STRIP // BAND_ROWS
    order = lax.broadcasted_iota(jnp.int32, (1, STRIP), 1)
    within = lax.rem(order, bands * quarter)
    owner = lax.div(order, bands * quarter) ^ place[0]
    output = lax.div(within, quarter) * BAND_ROWS + owner * quarter + lax.rem(within, quarter)
    distance = lax.broadcasted_iota(jnp.int32, (span, STRIP), 0) - output + (LEAD - HALO)
    mask_sets = [
        kept(place[0] * rows + first + output, rows * segments) for first in (0, STRIP, rows - STRIP)
    ]
    rest = jnp.zeros((cols_pad(3 * span) - 3 * span, STRIP), jnp.float32)
    for variant, matrix in enumerate(banded(taps, mask_sets, distance)):
        high = matrix.astype(jnp.bfloat16).astype(jnp.float32)
        stacked = jnp.concatenate([high, high, matrix - high, rest], axis=0).T
        rows_out[variant] = stacked.astype(jnp.bfloat16)[:, : 3 * span]


def cols_pad(count):
    return -(-count // 128) * 128


def build_matrices(place, coef, phases, shift, rows, width, segments):
    span = 3 * (STRIP + 2 * HALO)
    smem = pl.BlockSpec(memory_space=pltpu.SMEM)
    vmem = pl.BlockSpec(memory_space=pltpu.VMEM)
    return pl.pallas_call(
        functools.partial(matrices_kernel, rows=rows, width=width, segments=segments),
        out_shape=(
            jax.ShapeDtypeStruct((3, STRIP, span), jnp.bfloat16),
            jax.ShapeDtypeStruct((3, 2, TILE + 2 * SIDE, TILE), jnp.bfloat16),
        ),
        in_specs=[smem] * 4,
        out_specs=(vmem, vmem),
        compiler_params=pltpu.CompilerParams(vmem_limit_bytes=VMEM),
        cost_estimate=COST,
        name="band_matrices",
    )(place, coef, phases, shift)


def edge_kernel(first, last, top, bottom):
    top[...] = first[...].astype(jnp.bfloat16)
    bottom[...] = last[...].astype(jnp.bfloat16)


def edge_rows(image):
    rows, width = image.shape
    block = (HALO, width)
    shape = jax.ShapeDtypeStruct(block, jnp.bfloat16)
    return pl.pallas_call(
        edge_kernel,
        out_shape=(shape, shape),
        grid=(1,),
        in_specs=[pl.BlockSpec(block, lambda i: (0, 0)), pl.BlockSpec(block, lambda i: (rows // HALO - 1, 0))],
        out_specs=(pl.BlockSpec(block, lambda i: (0, 0)), pl.BlockSpec(block, lambda i: (0, 0))),
        cost_estimate=COST,
        name="edge_rows",
    )(image, image)


def filter_kernel(
    weight, low_l, low_c, low_r, mid_l, mid_c, mid_r, high_l, high_c, high_r, rows_m, cols_m, *rest,
    first_chunk, last_chunk, segments,
):
    *outs, ext_high, ext_low, mat_high, mat_low = rest
    half = pl.program_id(0)
    halves = pl.num_programs(0)
    rows, chunk = mid_c.shape
    at_left = first_chunk & (half == 0)
    at_right = last_chunk & (half == halves - 1)
    span = STRIP + 2 * HALO

    for row, parts in (
        (0, (low_l, low_c, low_r)),
        (HALO, (mid_l, mid_c, mid_r)),
        (HALO + rows, (high_l, high_c, high_r)),
    ):
        count = parts[0].shape[0]
        for part, column, outside in zip(parts, (0, SIDE, SIDE + chunk), (at_left, False, at_right)):
            value = part[...].astype(jnp.float32)
            if outside is not False:
                value = jnp.where(outside, 0.0, value)
            high, low = split(value)
            place = (pl.ds(row, count), pl.ds(column, value.shape[1]))
            ext_high[place] = high
            ext_low[place] = low

    strips = rows // STRIP
    for tile in range((chunk + 2 * SIDE) // TILE):
        columns = pl.ds(tile * TILE, TILE)
        for strip in range(strips):
            window = pl.ds(strip * STRIP, span)
            variant = 0 if strip == 0 else (2 if strip == strips - 1 else 1)
            high = ext_high[window, columns]
            stack = jnp.concatenate([high, ext_low[window, columns], high], axis=0)
            matched = jnp.dot(rows_m[variant], stack, preferred_element_type=jnp.float32)
            high, low = split(matched)
            mat_high[pl.ds(strip * STRIP, STRIP), columns] = high
            mat_low[pl.ds(strip * STRIP, STRIP), columns] = low

    tiles = chunk // TILE
    piece = STRIP // segments
    for tile in range(tiles):
        variant = jnp.int32(1)
        if tile == 0:
            variant = jnp.where(at_left, 0, variant)
        if tile == tiles - 1:
            variant = jnp.where(at_right, 2, variant)
        taps_high = cols_m[variant, 0]
        taps_low = cols_m[variant, 1]
        window = pl.ds(tile * TILE, TILE + 2 * SIDE)
        for strip in range(strips):
            place = pl.ds(strip * STRIP, STRIP)
            high = mat_high[place, window]
            warped = jnp.dot(high, taps_high, preferred_element_type=jnp.float32)
            warped += jnp.dot(mat_low[place, window], taps_high, preferred_element_type=jnp.float32)
            warped += jnp.dot(high, taps_low, preferred_element_type=jnp.float32)
            sent = (weight[0] * warped).astype(jnp.bfloat16)
            for owner, out in enumerate(outs):
                out[pl.ds(strip * piece, piece), pl.ds(tile * TILE, TILE)] = sent[owner * piece : (owner + 1) * piece]


def filter_chunk(weight, low, image, high, rows_m, cols_m, start, chunk, segments):
    rows, width = image.shape
    halves = 2
    half_blocks = width // halves // SIDE
    first = start // SIDE
    blocks = chunk // SIDE
    last = width // SIDE - 1

    def left(h):
        return 0, jnp.maximum(h * half_blocks + first - 1, 0)

    def centre(h):
        return 0, h * (half_blocks // blocks) + start // chunk

    def right(h):
        return 0, jnp.minimum(h * half_blocks + first + blocks, last)

    def whole(array):
        return pl.BlockSpec(array.shape, lambda h: (0,) * array.ndim)

    specs = [pl.BlockSpec(memory_space=pltpu.SMEM)]
    for source in (low, image, high):
        specs += [
            pl.BlockSpec((source.shape[0], SIDE), left),
            pl.BlockSpec((source.shape[0], chunk), centre),
            pl.BlockSpec((source.shape[0], SIDE), right),
        ]
    wide = chunk + 2 * SIDE
    return pl.pallas_call(
        functools.partial(
            filter_kernel,
            first_chunk=start == 0,
            last_chunk=start + chunk == width // halves,
            segments=segments,
        ),
        out_shape=[jax.ShapeDtypeStruct((rows // segments, halves * chunk), jnp.bfloat16)] * segments,
        grid=(halves,),
        in_specs=specs + [whole(rows_m), whole(cols_m)],
        out_specs=[pl.BlockSpec((rows // segments, chunk), lambda h: (0, h))] * segments,
        scratch_shapes=[
            pltpu.VMEM((rows + 2 * HALO, wide), jnp.bfloat16),
            pltpu.VMEM((rows + 2 * HALO, wide), jnp.bfloat16),
            pltpu.VMEM((rows, wide), jnp.bfloat16),
            pltpu.VMEM((rows, wide), jnp.bfloat16),
        ],
        compiler_params=pltpu.CompilerParams(vmem_limit_bytes=VMEM),
        cost_estimate=COST,
        name="warp_filter",
    )(weight, *([low] * 3), *([image] * 3), *([high] * 3), rows_m, cols_m)


def join_kernel(*refs):
    block = refs[0].shape[0]
    for step, ref in enumerate(refs[:-1]):
        refs[-1][pl.ds(step * block, block), :] = ref[...]


def joined(blocks):
    block, columns = blocks[0].shape
    vmem = pl.BlockSpec(memory_space=pltpu.VMEM)
    return pl.pallas_call(
        join_kernel,
        out_shape=jax.ShapeDtypeStruct((len(blocks) * block, columns), blocks[0].dtype),
        in_specs=[vmem] * len(blocks),
        out_specs=vmem,
        compiler_params=pltpu.CompilerParams(vmem_limit_bytes=VMEM),
        cost_estimate=COST,
        name="join_blocks",
    )(*blocks)


def stage_distances(lines):
    stages = []
    step = 1
    while step < lines:
        stages.append(list(reversed(range(step, lines, 2 * step))))
        step *= 2
    return stages


def pair_kernel(place, table, mine, other, *rest, slots, distances, quarter):
    *outs, mine_all, other_all = rest
    rows = mine.shape[0]
    chunk = outs[0].shape[1]
    count = table.shape[0] // 3
    for source, held in ((mine, mine_all), (other, other_all)):
        held[pl.ds(0, rows), :] = source[...].astype(jnp.float32)
        held[pl.ds(rows, quarter), :] = jnp.zeros((quarter, source.shape[1]), jnp.float32)
    line = place[1]

    for distance, out in zip(distances, outs):
        first = (line ^ distance) * slots

        def summed(slot, first=first):
            column = pl.ds(pl.multiple_of(table[first + slot] * chunk, 128), chunk)
            from_mine = pl.ds(pl.multiple_of(table[count + first + slot], quarter), quarter)
            from_other = pl.ds(pl.multiple_of(table[2 * count + first + slot], quarter), quarter)
            return mine_all[from_mine, column] + other_all[from_other, column]

        for slot in range(0, slots - 1, 2):
            rows_two = jnp.concatenate([summed(slot), summed(slot + 1)], axis=0)
            out[pl.ds(slot * quarter, 2 * quarter), :] = rows_two.astype(jnp.bfloat16)
        if slots % 2:
            out[pl.ds((slots - 1) * quarter, quarter), :] = summed(slots - 1).astype(jnp.bfloat16)


def pair_sum(place, table, mine, other, slots, lines, quarter):
    rows, double = mine.shape
    chunk = double // 2
    distances = sum(stage_distances(lines), []) + [0]
    smem = pl.BlockSpec(memory_space=pltpu.SMEM)
    vmem = pl.BlockSpec(memory_space=pltpu.VMEM)
    outs = pl.pallas_call(
        functools.partial(pair_kernel, slots=slots, distances=distances, quarter=quarter),
        out_shape=[jax.ShapeDtypeStruct((slots * quarter, chunk), jnp.bfloat16)] * lines,
        in_specs=[smem, smem, vmem, vmem],
        out_specs=[vmem] * lines,
        scratch_shapes=[pltpu.VMEM((rows + quarter, double), jnp.float32)] * 2,
        compiler_params=pltpu.CompilerParams(vmem_limit_bytes=VMEM),
        cost_estimate=COST,
        name="pair_sum",
    )(place, table, mine, other)
    return dict(zip(distances, outs))


def weight_kernel(place, sites, facts, out, covers, *, cores, quarter, width, bands):
    slots = out.shape[0] // quarter
    half_cols = out.shape[1]
    exposures = facts.shape[0]
    owner = place[1] * cores + place[2]
    column = lax.broadcasted_iota(jnp.int32, (quarter, half_cols), 1)
    for half in range(2):
        for exposure in range(exposures):
            first = facts[exposure, 0].astype(jnp.int32) - half * half_cols
            inside = (column >= first) & (column < first + width)
            covers[half * exposures + exposure] = jnp.where(inside, facts[exposure, 2], 0.0)

    def one_slot(slot, carry):
        site = sites[owner * slots + slot]
        total = jnp.zeros((quarter, half_cols), jnp.float32)
        for exposure in range(exposures):
            relative = lax.shift_right_logical(site, 1) - facts[exposure, 1].astype(jnp.int32)
            present = jnp.where((relative >= 0) & (relative < bands), jnp.float32(1.0), jnp.float32(0.0))
            total = total + present * covers[(site & 1) * exposures + exposure]
        out[pl.ds(pl.multiple_of(slot * quarter, quarter), quarter), :] = jnp.maximum(total, 1.0)
        return carry

    lax.fori_loop(0, slots, one_slot, 0)


def patch_weights(place, sites, facts, slots, quarter, cores, width, bands):
    smem = pl.BlockSpec(memory_space=pltpu.SMEM)
    return pl.pallas_call(
        functools.partial(weight_kernel, cores=cores, quarter=quarter, width=width, bands=bands),
        out_shape=jax.ShapeDtypeStruct((slots * quarter, width // 2), jnp.float32),
        in_specs=[smem] * 3,
        out_specs=pl.BlockSpec(memory_space=pltpu.VMEM),
        scratch_shapes=[pltpu.VMEM((2 * facts.shape[0], quarter, width // 2), jnp.float32)],
        compiler_params=pltpu.CompilerParams(vmem_limit_bytes=VMEM),
        cost_estimate=COST,
        name="patch_weights",
    )(place, sites, facts)


def finish_kernel(*refs, count):
    pieces, scale, out = refs[:count], refs[count], refs[-1]
    total = pieces[0][...].astype(jnp.float32)
    for piece in pieces[1:]:
        total += piece[...].astype(jnp.float32)
    out[...] = total / scale[...]


def finish_chunk(pieces, scale, result, start):
    rows, chunk = pieces[0].shape
    column = pl.BlockSpec((rows, chunk), lambda i: (0, start // chunk))
    specs = [pl.BlockSpec((rows, chunk), lambda i: (0, 0))] * len(pieces) + [column]
    operands = [*pieces, scale]
    aliases = {}
    if result is not None:
        specs.append(pl.BlockSpec(memory_space=pl.ANY))
        aliases = {len(operands): 0}
        operands.append(result)
    return pl.pallas_call(
        functools.partial(finish_kernel, count=len(pieces)),
        out_shape=jax.ShapeDtypeStruct(scale.shape, jnp.float32),
        grid=(1,),
        in_specs=specs,
        out_specs=column,
        input_output_aliases=aliases,
        compiler_params=pltpu.CompilerParams(vmem_limit_bytes=VMEM),
        cost_estimate=pl.CostEstimate(
            flops=len(pieces) * rows * chunk, bytes_accessed=rows * chunk * (2 * len(pieces) + 8), transcendentals=0
        ),
        name="patch_mean",
    )(*operands)


def swapped(value, axis, distance):
    count = lax.axis_size(axis)
    return lax.ppermute(value, axis, [(i, i ^ distance) for i in range(count)])


def scatter_sum(pieces, in_turn):
    pieces = dict(pieces)
    kept, added = [pieces[0]], []
    for stage, distances in enumerate(stage_distances(len(pieces))):
        for distance in distances:
            if in_turn and distance != distances[0]:
                pieces[distance], _ = lax.optimization_barrier((pieces[distance], added))
            received = swapped(pieces[distance], "line", 1 << stage)
            target = distance ^ (1 << stage)
            if target:
                both = pieces[target].astype(jnp.float32) + received.astype(jnp.float32)
                pieces[target] = both.astype(jnp.bfloat16)
                added = [pieces[target]]
            else:
                kept.append(received)
    return kept, added


def per_device(images, psf_coef, phases, col_shift, band_offset, exposure_weight, patch_site):
    image = images[0]
    rows, width = image.shape
    segments = lax.axis_size("seg")
    lines = lax.axis_size("line")
    cores = lax.axis_size("core")
    quarter = BAND_ROWS // segments
    half_cols = width // 2
    slots = patch_site.shape[0] // (lines * cores)
    bands = segments * rows // BAND_ROWS
    place = jnp.stack([lax.axis_index(axis) for axis in ("seg", "line", "core")]).astype(jnp.int32)

    forward = [(i, i + 1) for i in range(segments - 1)]
    backward = [(i + 1, i) for i in range(segments - 1)]
    top, bottom = edge_rows(image)
    low = lax.ppermute(bottom, "seg", forward)
    high = lax.ppermute(top, "seg", backward)
    rows_m, cols_m = build_matrices(place, psf_coef, phases, col_shift, rows, width, segments)
    weight = exposure_weight.astype(jnp.float32)

    chunks = []
    start = 0
    for part in PARTS:
        chunks.append((start, half_cols // part))
        start += half_cols // part
    other_offset = swapped(band_offset, "core", 1)
    sites = lax.dynamic_index_in_dim(patch_site.reshape(lines, cores, slots), place[2], 1, keepdims=False).reshape(-1)
    here = rows // BAND_ROWS

    def rows_from(offset):
        relative = sites // 2 - offset
        held = ((relative // here) ^ place[0]) * here + relative % here
        return jnp.where((relative >= 0) & (relative < bands), held, bands) * quarter

    table = jnp.concatenate([sites % 2, rows_from(band_offset), rows_from(other_offset)])
    facts = jnp.stack([col_shift.astype(jnp.float32), band_offset.astype(jnp.float32), weight], axis=1)
    facts = jnp.concatenate([facts, swapped(facts, "core", 1)], axis=0)
    early = facts
    step = 1
    while step < lines:
        early = facts
        facts = jnp.concatenate([facts, swapped(facts, "line", step)], axis=0)
        step *= 2
    scale = patch_weights(place, patch_site, facts, slots, quarter, cores, width, bands)

    def tied(values, others):
        return lax.optimization_barrier((values, others))[0]

    result = None
    count = len(chunks)
    sent, sums, kept, added = [None] * count, [None] * count, [None] * count, [None] * count

    def filtered(index):
        start, chunk = chunks[index]
        held = tied(weight, sums[index - 2]) if index >= 2 else weight
        sent[index] = filter_chunk(held, low, image, high, rows_m, cols_m, start, chunk, segments)

    filtered(0)
    for index, (start, chunk) in enumerate(chunks):
        outgoing = sent[index]
        received = [swapped(outgoing[d], "seg", d) for d in range(1, segments)]
        if index + 1 < count:
            filtered(index + 1)
            received = tied(received, sent[index + 1])
        if index == 0:
            received = tied(received, early)
        if index == 1:
            received = tied(received, scale)
        if index >= 1:
            received = tied(received, (added[index - 1], kept[index - 1][:-1]))
        mine = joined([outgoing[0]] + received)
        other = swapped(mine, "core", 1)
        sums[index] = pair_sum(place, table, mine, other, slots, lines, quarter)
        kept[index], added[index] = scatter_sum(sums[index], index + 1 == count)
        result = finish_chunk(kept[index], scale, result, start)
    return result.reshape(slots, quarter, half_cols)


def solution(mesh):
    segments, exposures = mesh.shape["seg"], mesh.shape["exp"]
    parted = Mesh(mesh.devices.reshape(segments, exposures // 2, 2), ("seg", "line", "core"))
    spread = ("line", "core")
    placed = (
        P(spread, "seg", None),
        P(spread, None, None),
        P(spread, None),
        P(spread),
        P(spread),
        P(spread),
        P(),
    )
    return jax.shard_map(
        per_device, mesh=parted, in_specs=placed, out_specs=P(spread, "seg", None), check_vma=False
    )
```

```python
import functools

import jax
import jax.numpy as jnp
import numpy as np
from jax import lax
from jax.experimental import pallas as pl
from jax.experimental.pallas import tpu as pltpu
from jax.sharding import Mesh, PartitionSpec as P

BAND_ROWS = 32
TAPS = 21
PHASES = 16
LANCZOS = 6
SPAN = TAPS + LANCZOS - 1
LEAD = TAPS // 2 + 2
HALO = 16
SIDE = 128
TILE = 256
STRIP = 128
PARTS = (2, 2)
VMEM = 48 * 1024 * 1024
COST = pl.CostEstimate(flops=1, bytes_accessed=1, transcendentals=0)

sigmas = (1.0, 2.0, 3.5)


def basis_table():
    offsets = np.arange(TAPS) - TAPS // 2
    curves = [np.exp(-offsets * offsets / (2.0 * spread * spread)) for spread in sigmas]
    return [[float(value) for value in curve / curve.sum()] for curve in curves]


def lanczos_table():
    shifted = np.arange(LANCZOS)[None, :] - 2.0 - np.arange(PHASES)[:, None] / PHASES
    values = np.sinc(shifted) * np.sinc(shifted / 3.0)
    return (values / values.sum(axis=1, keepdims=True)).astype(np.float32)


def lanczos_taps(phase):
    table = lanczos_table()
    taps = []
    for n in range(LANCZOS):
        tap = jnp.float32(table[0, n])
        for index in range(1, PHASES):
            tap = jnp.where(phase == index, jnp.float32(table[index, n]), tap)
        taps.append(tap)
    return taps


def split(value):
    high = value.astype(jnp.bfloat16)
    return high, (value - high.astype(jnp.float32)).astype(jnp.bfloat16)


def banded(taps, mask_sets, distance):
    kernel, lanczos = taps
    sets = [[jnp.where(mask, lanczos[n], 0.0) for n, mask in enumerate(masks)] for masks in mask_sets]
    matrices = [jnp.zeros(distance.shape, jnp.float32) for _ in sets]
    for t in range(SPAN):
        here = distance == t
        for index, weighted in enumerate(sets):
            row = jnp.zeros_like(weighted[0])
            for n in range(LANCZOS):
                if 0 <= t - n < TAPS:
                    row = row + kernel[t - n] * weighted[n]
            matrices[index] = jnp.where(here, row, matrices[index])
    return matrices


def matrices_kernel(place, coef, phases, shift, rows_out, cols_out, *, rows, width, segments):
    basis = basis_table()

    def taps_of(axis):
        kernel = [sum(coef[0, axis, k] * basis[k][t] for k in range(len(sigmas))) for t in range(TAPS)]
        return kernel, lanczos_taps(phases[0, axis])

    def kept(matched, extent):
        return [(matched + (n - 2) >= 0) & (matched + (n - 2) < extent) for n in range(LANCZOS)]

    taps = taps_of(1)
    offset = shift[0]
    column = lax.broadcasted_iota(jnp.int32, (1, SIDE), 1)
    everything = [jnp.full((1, SIDE), True)] * LANCZOS
    mask_sets = [kept(column - offset, width), everything, kept(column + (width - SIDE) - offset, width)]
    for part, block in ((0, 3), (1, 0)):
        for variant in range(3):
            for term in range(2):
                place_out = (pl.ds(block * SIDE, SIDE), pl.ds(part * SIDE, SIDE))
                cols_out[(variant, term, *place_out)] = jnp.zeros((SIDE, SIDE), jnp.bfloat16)
    for step in range(3):
        distance = (
            lax.broadcasted_iota(jnp.int32, (SIDE, SIDE), 0)
            - lax.broadcasted_iota(jnp.int32, (SIDE, SIDE), 1)
            + (offset + LEAD - SIDE + step * SIDE)
        )
        pairs = [split(matrix) for matrix in banded(taps, mask_sets, distance)]
        for part in range(2):
            for variant in range(3):
                chosen = variant if variant == 2 * part else 1
                for term in range(2):
                    place_out = (pl.ds((part + step) * SIDE, SIDE), pl.ds(part * SIDE, SIDE))
                    cols_out[(variant, term, *place_out)] = pairs[chosen][term]

    taps = taps_of(0)
    span = STRIP + 2 * HALO
    quarter = BAND_ROWS // segments
    bands = STRIP // BAND_ROWS
    order = lax.broadcasted_iota(jnp.int32, (1, STRIP), 1)
    within = lax.rem(order, bands * quarter)
    owner = lax.div(order, bands * quarter) ^ place[0]
    output = lax.div(within, quarter) * BAND_ROWS + owner * quarter + lax.rem(within, quarter)
    distance = lax.broadcasted_iota(jnp.int32, (span, STRIP), 0) - output + (LEAD - HALO)
    mask_sets = [
        kept(place[0] * rows + first + output, rows * segments) for first in (0, STRIP, rows - STRIP)
    ]
    rest = jnp.zeros((cols_pad(3 * span) - 3 * span, STRIP), jnp.float32)
    for variant, matrix in enumerate(banded(taps, mask_sets, distance)):
        high = matrix.astype(jnp.bfloat16).astype(jnp.float32)
        stacked = jnp.concatenate([high, high, matrix - high, rest], axis=0).T
        rows_out[variant] = stacked.astype(jnp.bfloat16)[:, : 3 * span]


def cols_pad(count):
    return -(-count // 128) * 128


def build_matrices(place, coef, phases, shift, rows, width, segments):
    span = 3 * (STRIP + 2 * HALO)
    smem = pl.BlockSpec(memory_space=pltpu.SMEM)
    vmem = pl.BlockSpec(memory_space=pltpu.VMEM)
    return pl.pallas_call(
        functools.partial(matrices_kernel, rows=rows, width=width, segments=segments),
        out_shape=(
            jax.ShapeDtypeStruct((3, STRIP, span), jnp.bfloat16),
            jax.ShapeDtypeStruct((3, 2, TILE + 2 * SIDE, TILE), jnp.bfloat16),
        ),
        in_specs=[smem] * 4,
        out_specs=(vmem, vmem),
        compiler_params=pltpu.CompilerParams(vmem_limit_bytes=VMEM),
        cost_estimate=COST,
        name="band_matrices",
    )(place, coef, phases, shift)


def edge_kernel(first, last, top, bottom):
    top[...] = first[...].astype(jnp.bfloat16)
    bottom[...] = last[...].astype(jnp.bfloat16)


def edge_rows(image):
    rows, width = image.shape
    block = (HALO, width)
    shape = jax.ShapeDtypeStruct(block, jnp.bfloat16)
    return pl.pallas_call(
        edge_kernel,
        out_shape=(shape, shape),
        grid=(1,),
        in_specs=[pl.BlockSpec(block, lambda i: (0, 0)), pl.BlockSpec(block, lambda i: (rows // HALO - 1, 0))],
        out_specs=(pl.BlockSpec(block, lambda i: (0, 0)), pl.BlockSpec(block, lambda i: (0, 0))),
        cost_estimate=COST,
        name="edge_rows",
    )(image, image)


def filter_kernel(
    weight, low_l, low_c, low_r, mid_l, mid_c, mid_r, high_l, high_c, high_r, rows_m, cols_m, *rest,
    first_chunk, last_chunk, segments,
):
    *outs, ext_high, ext_low, mat_high, mat_low = rest
    half = pl.program_id(0)
    halves = pl.num_programs(0)
    rows, chunk = mid_c.shape
    at_left = first_chunk & (half == 0)
    at_right = last_chunk & (half == halves - 1)
    span = STRIP + 2 * HALO

    for row, parts in (
        (0, (low_l, low_c, low_r)),
        (HALO, (mid_l, mid_c, mid_r)),
        (HALO + rows, (high_l, high_c, high_r)),
    ):
        count = parts[0].shape[0]
        for part, column, outside in zip(parts, (0, SIDE, SIDE + chunk), (at_left, False, at_right)):
            value = part[...].astype(jnp.float32)
            if outside is not False:
                value = jnp.where(outside, 0.0, value)
            high, low = split(value)
            place = (pl.ds(row, count), pl.ds(column, value.shape[1]))
            ext_high[place] = high
            ext_low[place] = low

    strips = rows // STRIP
    for tile in range((chunk + 2 * SIDE) // TILE):
        columns = pl.ds(tile * TILE, TILE)
        for strip in range(strips):
            window = pl.ds(strip * STRIP, span)
            variant = 0 if strip == 0 else (2 if strip == strips - 1 else 1)
            high = ext_high[window, columns]
            stack = jnp.concatenate([high, ext_low[window, columns], high], axis=0)
            matched = jnp.dot(rows_m[variant], stack, preferred_element_type=jnp.float32)
            high, low = split(matched)
            mat_high[pl.ds(strip * STRIP, STRIP), columns] = high
            mat_low[pl.ds(strip * STRIP, STRIP), columns] = low

    tiles = chunk // TILE
    piece = STRIP // segments
    for tile in range(tiles):
        variant = jnp.int32(1)
        if tile == 0:
            variant = jnp.where(at_left, 0, variant)
        if tile == tiles - 1:
            variant = jnp.where(at_right, 2, variant)
        taps_high = cols_m[variant, 0]
        taps_low = cols_m[variant, 1]
        window = pl.ds(tile * TILE, TILE + 2 * SIDE)
        for strip in range(strips):
            place = pl.ds(strip * STRIP, STRIP)
            high = mat_high[place, window]
            warped = jnp.dot(high, taps_high, preferred_element_type=jnp.float32)
            warped += jnp.dot(mat_low[place, window], taps_high, preferred_element_type=jnp.float32)
            warped += jnp.dot(high, taps_low, preferred_element_type=jnp.float32)
            sent = (weight[0] * warped).astype(jnp.bfloat16)
            for owner, out in enumerate(outs):
                out[pl.ds(strip * piece, piece), pl.ds(tile * TILE, TILE)] = sent[owner * piece : (owner + 1) * piece]


def filter_chunk(weight, low, image, high, rows_m, cols_m, start, chunk, segments):
    rows, width = image.shape
    halves = 2
    half_blocks = width // halves // SIDE
    first = start // SIDE
    blocks = chunk // SIDE
    last = width // SIDE - 1

    def left(h):
        return 0, jnp.maximum(h * half_blocks + first - 1, 0)

    def centre(h):
        return 0, h * (half_blocks // blocks) + start // chunk

    def right(h):
        return 0, jnp.minimum(h * half_blocks + first + blocks, last)

    def whole(array):
        return pl.BlockSpec(array.shape, lambda h: (0,) * array.ndim)

    specs = [pl.BlockSpec(memory_space=pltpu.SMEM)]
    for source in (low, image, high):
        specs += [
            pl.BlockSpec((source.shape[0], SIDE), left),
            pl.BlockSpec((source.shape[0], chunk), centre),
            pl.BlockSpec((source.shape[0], SIDE), right),
        ]
    wide = chunk + 2 * SIDE
    return pl.pallas_call(
        functools.partial(
            filter_kernel,
            first_chunk=start == 0,
            last_chunk=start + chunk == width // halves,
            segments=segments,
        ),
        out_shape=[jax.ShapeDtypeStruct((rows // segments, halves * chunk), jnp.bfloat16)] * segments,
        grid=(halves,),
        in_specs=specs + [whole(rows_m), whole(cols_m)],
        out_specs=[pl.BlockSpec((rows // segments, chunk), lambda h: (0, h))] * segments,
        scratch_shapes=[
            pltpu.VMEM((rows + 2 * HALO, wide), jnp.bfloat16),
            pltpu.VMEM((rows + 2 * HALO, wide), jnp.bfloat16),
            pltpu.VMEM((rows, wide), jnp.bfloat16),
            pltpu.VMEM((rows, wide), jnp.bfloat16),
        ],
        compiler_params=pltpu.CompilerParams(vmem_limit_bytes=VMEM),
        cost_estimate=COST,
        name="warp_filter",
    )(weight, *([low] * 3), *([image] * 3), *([high] * 3), rows_m, cols_m)


def join_kernel(*refs):
    block = refs[0].shape[0]
    for step, ref in enumerate(refs[:-1]):
        refs[-1][pl.ds(step * block, block), :] = ref[...]


def joined(blocks):
    block, columns = blocks[0].shape
    vmem = pl.BlockSpec(memory_space=pltpu.VMEM)
    return pl.pallas_call(
        join_kernel,
        out_shape=jax.ShapeDtypeStruct((len(blocks) * block, columns), blocks[0].dtype),
        in_specs=[vmem] * len(blocks),
        out_specs=vmem,
        compiler_params=pltpu.CompilerParams(vmem_limit_bytes=VMEM),
        cost_estimate=COST,
        name="join_blocks",
    )(*blocks)


def stage_distances(lines):
    stages = []
    step = 1
    while step < lines:
        stages.append(list(reversed(range(step, lines, 2 * step))))
        step *= 2
    return stages


def pair_kernel(place, table, mine, other, *rest, slots, distances, quarter):
    *outs, mine_all, other_all = rest
    rows = mine.shape[0]
    chunk = outs[0].shape[1]
    count = table.shape[0] // 3
    for source, held in ((mine, mine_all), (other, other_all)):
        held[pl.ds(0, rows), :] = source[...].astype(jnp.float32)
        held[pl.ds(rows, quarter), :] = jnp.zeros((quarter, source.shape[1]), jnp.float32)
    line = place[1]

    for distance, out in zip(distances, outs):
        first = (line ^ distance) * slots

        def summed(slot, first=first):
            column = pl.ds(pl.multiple_of(table[first + slot] * chunk, 128), chunk)
            from_mine = pl.ds(pl.multiple_of(table[count + first + slot], quarter), quarter)
            from_other = pl.ds(pl.multiple_of(table[2 * count + first + slot], quarter), quarter)
            return mine_all[from_mine, column] + other_all[from_other, column]

        for slot in range(0, slots - 1, 2):
            rows_two = jnp.concatenate([summed(slot), summed(slot + 1)], axis=0)
            out[pl.ds(slot * quarter, 2 * quarter), :] = rows_two.astype(jnp.bfloat16)
        if slots % 2:
            out[pl.ds((slots - 1) * quarter, quarter), :] = summed(slots - 1).astype(jnp.bfloat16)


def pair_sum(place, table, mine, other, slots, lines, quarter):
    rows, double = mine.shape
    chunk = double // 2
    distances = sum(stage_distances(lines), []) + [0]
    smem = pl.BlockSpec(memory_space=pltpu.SMEM)
    vmem = pl.BlockSpec(memory_space=pltpu.VMEM)
    outs = pl.pallas_call(
        functools.partial(pair_kernel, slots=slots, distances=distances, quarter=quarter),
        out_shape=[jax.ShapeDtypeStruct((slots * quarter, chunk), jnp.bfloat16)] * lines,
        in_specs=[smem, smem, vmem, vmem],
        out_specs=[vmem] * lines,
        scratch_shapes=[pltpu.VMEM((rows + quarter, double), jnp.float32)] * 2,
        compiler_params=pltpu.CompilerParams(vmem_limit_bytes=VMEM),
        cost_estimate=COST,
        name="pair_sum",
    )(place, table, mine, other)
    return dict(zip(distances, outs))


def weight_kernel(place, sites, facts, out, covers, *, cores, quarter, width, bands):
    slots = out.shape[0] // quarter
    half_cols = out.shape[1]
    exposures = facts.shape[0]
    owner = place[1] * cores + place[2]
    column = lax.broadcasted_iota(jnp.int32, (quarter, half_cols), 1)
    for half in range(2):
        for exposure in range(exposures):
            first = facts[exposure, 0].astype(jnp.int32) - half * half_cols
            inside = (column >= first) & (column < first + width)
            covers[half * exposures + exposure] = jnp.where(inside, facts[exposure, 2], 0.0)

    def one_slot(slot, carry):
        site = sites[owner * slots + slot]
        total = jnp.zeros((quarter, half_cols), jnp.float32)
        for exposure in range(exposures):
            relative = lax.shift_right_logical(site, 1) - facts[exposure, 1].astype(jnp.int32)
            present = jnp.where((relative >= 0) & (relative < bands), jnp.float32(1.0), jnp.float32(0.0))
            total = total + present * covers[(site & 1) * exposures + exposure]
        out[pl.ds(pl.multiple_of(slot * quarter, quarter), quarter), :] = jnp.maximum(total, 1.0)
        return carry

    lax.fori_loop(0, slots, one_slot, 0)


def patch_weights(place, sites, facts, slots, quarter, cores, width, bands):
    smem = pl.BlockSpec(memory_space=pltpu.SMEM)
    return pl.pallas_call(
        functools.partial(weight_kernel, cores=cores, quarter=quarter, width=width, bands=bands),
        out_shape=jax.ShapeDtypeStruct((slots * quarter, width // 2), jnp.float32),
        in_specs=[smem] * 3,
        out_specs=pl.BlockSpec(memory_space=pltpu.VMEM),
        scratch_shapes=[pltpu.VMEM((2 * facts.shape[0], quarter, width // 2), jnp.float32)],
        compiler_params=pltpu.CompilerParams(vmem_limit_bytes=VMEM),
        cost_estimate=COST,
        name="patch_weights",
    )(place, sites, facts)


def finish_kernel(*refs, count):
    pieces, scale, out = refs[:count], refs[count], refs[-1]
    total = pieces[0][...].astype(jnp.float32)
    for piece in pieces[1:]:
        total += piece[...].astype(jnp.float32)
    out[...] = total / scale[...]


def finish_chunk(pieces, scale, result, start):
    rows, chunk = pieces[0].shape
    column = pl.BlockSpec((rows, chunk), lambda i: (0, start // chunk))
    specs = [pl.BlockSpec((rows, chunk), lambda i: (0, 0))] * len(pieces) + [column]
    operands = [*pieces, scale]
    aliases = {}
    if result is not None:
        specs.append(pl.BlockSpec(memory_space=pl.ANY))
        aliases = {len(operands): 0}
        operands.append(result)
    return pl.pallas_call(
        functools.partial(finish_kernel, count=len(pieces)),
        out_shape=jax.ShapeDtypeStruct(scale.shape, jnp.float32),
        grid=(1,),
        in_specs=specs,
        out_specs=column,
        input_output_aliases=aliases,
        compiler_params=pltpu.CompilerParams(vmem_limit_bytes=VMEM),
        cost_estimate=pl.CostEstimate(
            flops=len(pieces) * rows * chunk, bytes_accessed=rows * chunk * (2 * len(pieces) + 8), transcendentals=0
        ),
        name="patch_mean",
    )(*operands)


def swapped(value, axis, distance):
    count = lax.axis_size(axis)
    return lax.ppermute(value, axis, [(i, i ^ distance) for i in range(count)])


def scatter_sum(pieces, in_turn, halved, after):
    pieces = dict(pieces)
    kept, added, early = [pieces[0]], [], []
    for stage, distances in enumerate(stage_distances(len(pieces))):
        for distance in distances:
            if in_turn and distance != distances[0]:
                pieces[distance], _ = lax.optimization_barrier((pieces[distance], added))
            if halved and 2 * distance == len(pieces):
                width = pieces[distance].shape[1] // 2
                parts = [swapped(pieces[distance][:, first : first + width], "line", 1 << stage) for first in (0, width)]
                early = parts
                kept.append(jnp.concatenate(parts, axis=1))
                continue
            received = swapped(pieces[distance], "line", 1 << stage)
            target = distance ^ (1 << stage)
            if target:
                both = pieces[target].astype(jnp.float32) + received.astype(jnp.float32)
                pieces[target], _ = lax.optimization_barrier((both.astype(jnp.bfloat16), after))
                added = [pieces[target]]
            else:
                kept.append(received)
    return kept, added, early


def per_device(images, psf_coef, phases, col_shift, band_offset, exposure_weight, patch_site):
    image = images[0]
    rows, width = image.shape
    segments = lax.axis_size("seg")
    lines = lax.axis_size("line")
    cores = lax.axis_size("core")
    quarter = BAND_ROWS // segments
    half_cols = width // 2
    slots = patch_site.shape[0] // (lines * cores)
    bands = segments * rows // BAND_ROWS
    place = jnp.stack([lax.axis_index(axis) for axis in ("seg", "line", "core")]).astype(jnp.int32)

    forward = [(i, i + 1) for i in range(segments - 1)]
    backward = [(i + 1, i) for i in range(segments - 1)]
    top, bottom = edge_rows(image)
    low = lax.ppermute(bottom, "seg", forward)
    high = lax.ppermute(top, "seg", backward)
    rows_m, cols_m = build_matrices(place, psf_coef, phases, col_shift, rows, width, segments)
    weight = exposure_weight.astype(jnp.float32)

    chunks = []
    start = 0
    for part in PARTS:
        chunks.append((start, half_cols // part))
        start += half_cols // part
    other_offset = swapped(band_offset, "core", 1)
    sites = lax.dynamic_index_in_dim(patch_site.reshape(lines, cores, slots), place[2], 1, keepdims=False).reshape(-1)
    here = rows // BAND_ROWS

    def rows_from(offset):
        relative = sites // 2 - offset
        held = ((relative // here) ^ place[0]) * here + relative % here
        return jnp.where((relative >= 0) & (relative < bands), held, bands) * quarter

    table = jnp.concatenate([sites % 2, rows_from(band_offset), rows_from(other_offset)])
    facts = jnp.stack([col_shift.astype(jnp.float32), band_offset.astype(jnp.float32), weight], axis=1)
    facts = jnp.concatenate([facts, swapped(facts, "core", 1)], axis=0)
    early = facts
    step = 1
    while step < lines:
        early = facts
        facts = jnp.concatenate([facts, swapped(facts, "line", step)], axis=0)
        step *= 2
    scale = patch_weights(place, patch_site, facts, slots, quarter, cores, width, bands)

    def tied(values, others):
        return lax.optimization_barrier((values, others))[0]

    result = None
    count = len(chunks)
    sent, sums, kept, added, parts = ([None] * count for _ in range(5))

    def filtered(index):
        start, chunk = chunks[index]
        held = tied(weight, sums[index - 2]) if index >= 2 else weight
        sent[index] = filter_chunk(held, low, image, high, rows_m, cols_m, start, chunk, segments)

    filtered(0)
    for index, (start, chunk) in enumerate(chunks):
        outgoing = sent[index]
        received = [swapped(outgoing[d], "seg", d) for d in range(1, segments)]
        if index + 1 < count:
            filtered(index + 1)
            received = tied(received, sent[index + 1])
        if index == 0:
            received = tied(received, early)
        if index == 1:
            received = tied(received, scale)
        if index >= 1:
            received = tied(received, (added[index - 1], kept[index - 1][:-1]))
        mine = joined([outgoing[0]] + received)
        other = swapped(mine, "core", 1)
        if index >= 1:
            other = tied(other, parts[index - 1][:1])
        sums[index] = pair_sum(place, table, mine, other, slots, lines, quarter)
        kept[index], added[index], parts[index] = scatter_sum(
            sums[index], index + 1 == count, index + 1 < count, parts[index - 1][1:] if index else []
        )
        result = finish_chunk(kept[index], scale, result, start)
    return result.reshape(slots, quarter, half_cols)


def solution(mesh):
    segments, exposures = mesh.shape["seg"], mesh.shape["exp"]
    parted = Mesh(mesh.devices.reshape(segments, exposures // 2, 2), ("seg", "line", "core"))
    spread = ("line", "core")
    placed = (
        P(spread, "seg", None),
        P(spread, None, None),
        P(spread, None),
        P(spread),
        P(spread),
        P(spread),
        P(),
    )
    return jax.shard_map(
        per_device, mesh=parted, in_specs=placed, out_specs=P(spread, "seg", None), check_vma=False
    )
```

```python
import functools

import jax
import jax.numpy as jnp
import numpy as np
from jax import lax
from jax.experimental import pallas as pl
from jax.experimental.pallas import tpu as pltpu
from jax.sharding import Mesh, PartitionSpec as P

BAND_ROWS = 32
TAPS = 21
PHASES = 16
LANCZOS = 6
SPAN = TAPS + LANCZOS - 1
LEAD = TAPS // 2 + 2
HALO = 16
SIDE = 128
TILE = 256
STRIP = 128
PARTS = (2, 2)
VMEM = 48 * 1024 * 1024
COST = pl.CostEstimate(flops=1, bytes_accessed=1, transcendentals=0)

sigmas = (1.0, 2.0, 3.5)


def basis_table():
    offsets = np.arange(TAPS) - TAPS // 2
    curves = [np.exp(-offsets * offsets / (2.0 * spread * spread)) for spread in sigmas]
    return [[float(value) for value in curve / curve.sum()] for curve in curves]


def lanczos_table():
    shifted = np.arange(LANCZOS)[None, :] - 2.0 - np.arange(PHASES)[:, None] / PHASES
    values = np.sinc(shifted) * np.sinc(shifted / 3.0)
    return (values / values.sum(axis=1, keepdims=True)).astype(np.float32)


def lanczos_taps(phase):
    table = lanczos_table()
    taps = []
    for n in range(LANCZOS):
        tap = jnp.float32(table[0, n])
        for index in range(1, PHASES):
            tap = jnp.where(phase == index, jnp.float32(table[index, n]), tap)
        taps.append(tap)
    return taps


def split(value):
    high = value.astype(jnp.bfloat16)
    return high, (value - high.astype(jnp.float32)).astype(jnp.bfloat16)


def banded(taps, mask_sets, distance):
    kernel, lanczos = taps
    sets = [[jnp.where(mask, lanczos[n], 0.0) for n, mask in enumerate(masks)] for masks in mask_sets]
    matrices = [jnp.zeros(distance.shape, jnp.float32) for _ in sets]
    for t in range(SPAN):
        here = distance == t
        for index, weighted in enumerate(sets):
            row = jnp.zeros_like(weighted[0])
            for n in range(LANCZOS):
                if 0 <= t - n < TAPS:
                    row = row + kernel[t - n] * weighted[n]
            matrices[index] = jnp.where(here, row, matrices[index])
    return matrices


def matrices_kernel(place, coef, phases, shift, rows_out, cols_out, *, rows, width, segments):
    basis = basis_table()

    def taps_of(axis):
        kernel = [sum(coef[0, axis, k] * basis[k][t] for k in range(len(sigmas))) for t in range(TAPS)]
        return kernel, lanczos_taps(phases[0, axis])

    def kept(matched, extent):
        return [(matched + (n - 2) >= 0) & (matched + (n - 2) < extent) for n in range(LANCZOS)]

    taps = taps_of(1)
    offset = shift[0]
    column = lax.broadcasted_iota(jnp.int32, (1, SIDE), 1)
    everything = [jnp.full((1, SIDE), True)] * LANCZOS
    mask_sets = [kept(column - offset, width), everything, kept(column + (width - SIDE) - offset, width)]
    for part, block in ((0, 3), (1, 0)):
        for variant in range(3):
            for term in range(2):
                place_out = (pl.ds(block * SIDE, SIDE), pl.ds(part * SIDE, SIDE))
                cols_out[(variant, term, *place_out)] = jnp.zeros((SIDE, SIDE), jnp.bfloat16)
    for step in range(3):
        distance = (
            lax.broadcasted_iota(jnp.int32, (SIDE, SIDE), 0)
            - lax.broadcasted_iota(jnp.int32, (SIDE, SIDE), 1)
            + (offset + LEAD - SIDE + step * SIDE)
        )
        pairs = [split(matrix) for matrix in banded(taps, mask_sets, distance)]
        for part in range(2):
            for variant in range(3):
                chosen = variant if variant == 2 * part else 1
                for term in range(2):
                    place_out = (pl.ds((part + step) * SIDE, SIDE), pl.ds(part * SIDE, SIDE))
                    cols_out[(variant, term, *place_out)] = pairs[chosen][term]

    taps = taps_of(0)
    span = STRIP + 2 * HALO
    quarter = BAND_ROWS // segments
    bands = STRIP // BAND_ROWS
    order = lax.broadcasted_iota(jnp.int32, (1, STRIP), 1)
    within = lax.rem(order, bands * quarter)
    owner = lax.div(order, bands * quarter) ^ place[0]
    output = lax.div(within, quarter) * BAND_ROWS + owner * quarter + lax.rem(within, quarter)
    distance = lax.broadcasted_iota(jnp.int32, (span, STRIP), 0) - output + (LEAD - HALO)
    mask_sets = [
        kept(place[0] * rows + first + output, rows * segments) for first in (0, STRIP, rows - STRIP)
    ]
    rest = jnp.zeros((cols_pad(3 * span) - 3 * span, STRIP), jnp.float32)
    for variant, matrix in enumerate(banded(taps, mask_sets, distance)):
        high = matrix.astype(jnp.bfloat16).astype(jnp.float32)
        stacked = jnp.concatenate([high, high, matrix - high, rest], axis=0).T
        rows_out[variant] = stacked.astype(jnp.bfloat16)[:, : 3 * span]


def cols_pad(count):
    return -(-count // 128) * 128


def build_matrices(place, coef, phases, shift, rows, width, segments):
    span = 3 * (STRIP + 2 * HALO)
    smem = pl.BlockSpec(memory_space=pltpu.SMEM)
    vmem = pl.BlockSpec(memory_space=pltpu.VMEM)
    return pl.pallas_call(
        functools.partial(matrices_kernel, rows=rows, width=width, segments=segments),
        out_shape=(
            jax.ShapeDtypeStruct((3, STRIP, span), jnp.bfloat16),
            jax.ShapeDtypeStruct((3, 2, TILE + 2 * SIDE, TILE), jnp.bfloat16),
        ),
        in_specs=[smem] * 4,
        out_specs=(vmem, vmem),
        compiler_params=pltpu.CompilerParams(vmem_limit_bytes=VMEM),
        cost_estimate=COST,
        name="band_matrices",
    )(place, coef, phases, shift)


def edge_kernel(first, last, top, bottom):
    top[...] = first[...].astype(jnp.bfloat16)
    bottom[...] = last[...].astype(jnp.bfloat16)


def edge_rows(image):
    rows, width = image.shape
    block = (HALO, width)
    shape = jax.ShapeDtypeStruct(block, jnp.bfloat16)
    return pl.pallas_call(
        edge_kernel,
        out_shape=(shape, shape),
        grid=(1,),
        in_specs=[pl.BlockSpec(block, lambda i: (0, 0)), pl.BlockSpec(block, lambda i: (rows // HALO - 1, 0))],
        out_specs=(pl.BlockSpec(block, lambda i: (0, 0)), pl.BlockSpec(block, lambda i: (0, 0))),
        cost_estimate=COST,
        name="edge_rows",
    )(image, image)


def filter_kernel(
    weight, low_l, low_c, low_r, mid_l, mid_c, mid_r, high_l, high_c, high_r, rows_m, cols_m, *rest,
    first_chunk, last_chunk, segments,
):
    *outs, ext_high, ext_low, mat_high, mat_low = rest
    half = pl.program_id(0)
    halves = pl.num_programs(0)
    rows, chunk = mid_c.shape
    at_left = first_chunk & (half == 0)
    at_right = last_chunk & (half == halves - 1)
    span = STRIP + 2 * HALO

    for row, parts in (
        (0, (low_l, low_c, low_r)),
        (HALO, (mid_l, mid_c, mid_r)),
        (HALO + rows, (high_l, high_c, high_r)),
    ):
        count = parts[0].shape[0]
        for part, column, outside in zip(parts, (0, SIDE, SIDE + chunk), (at_left, False, at_right)):
            value = part[...].astype(jnp.float32)
            if outside is not False:
                value = jnp.where(outside, 0.0, value)
            high, low = split(value)
            place = (pl.ds(row, count), pl.ds(column, value.shape[1]))
            ext_high[place] = high
            ext_low[place] = low

    strips = rows // STRIP
    for tile in range((chunk + 2 * SIDE) // TILE):
        columns = pl.ds(tile * TILE, TILE)
        for strip in range(strips):
            window = pl.ds(strip * STRIP, span)
            variant = 0 if strip == 0 else (2 if strip == strips - 1 else 1)
            high = ext_high[window, columns]
            stack = jnp.concatenate([high, ext_low[window, columns], high], axis=0)
            matched = jnp.dot(rows_m[variant], stack, preferred_element_type=jnp.float32)
            high, low = split(matched)
            mat_high[pl.ds(strip * STRIP, STRIP), columns] = high
            mat_low[pl.ds(strip * STRIP, STRIP), columns] = low

    tiles = chunk // TILE
    piece = STRIP // segments
    for tile in range(tiles):
        variant = jnp.int32(1)
        if tile == 0:
            variant = jnp.where(at_left, 0, variant)
        if tile == tiles - 1:
            variant = jnp.where(at_right, 2, variant)
        taps_high = cols_m[variant, 0]
        taps_low = cols_m[variant, 1]
        window = pl.ds(tile * TILE, TILE + 2 * SIDE)
        for strip in range(strips):
            place = pl.ds(strip * STRIP, STRIP)
            high = mat_high[place, window]
            warped = jnp.dot(high, taps_high, preferred_element_type=jnp.float32)
            warped += jnp.dot(mat_low[place, window], taps_high, preferred_element_type=jnp.float32)
            warped += jnp.dot(high, taps_low, preferred_element_type=jnp.float32)
            sent = (weight[0] * warped).astype(jnp.bfloat16)
            for owner, out in enumerate(outs):
                out[pl.ds(strip * piece, piece), pl.ds(tile * TILE, TILE)] = sent[owner * piece : (owner + 1) * piece]


def filter_chunk(weight, low, image, high, rows_m, cols_m, start, chunk, segments):
    rows, width = image.shape
    halves = 2
    half_blocks = width // halves // SIDE
    first = start // SIDE
    blocks = chunk // SIDE
    last = width // SIDE - 1

    def left(h):
        return 0, jnp.maximum(h * half_blocks + first - 1, 0)

    def centre(h):
        return 0, h * (half_blocks // blocks) + start // chunk

    def right(h):
        return 0, jnp.minimum(h * half_blocks + first + blocks, last)

    def whole(array):
        return pl.BlockSpec(array.shape, lambda h: (0,) * array.ndim)

    specs = [pl.BlockSpec(memory_space=pltpu.SMEM)]
    for source in (low, image, high):
        specs += [
            pl.BlockSpec((source.shape[0], SIDE), left),
            pl.BlockSpec((source.shape[0], chunk), centre),
            pl.BlockSpec((source.shape[0], SIDE), right),
        ]
    wide = chunk + 2 * SIDE
    return pl.pallas_call(
        functools.partial(
            filter_kernel,
            first_chunk=start == 0,
            last_chunk=start + chunk == width // halves,
            segments=segments,
        ),
        out_shape=[jax.ShapeDtypeStruct((rows // segments, halves * chunk), jnp.bfloat16)] * segments,
        grid=(halves,),
        in_specs=specs + [whole(rows_m), whole(cols_m)],
        out_specs=[pl.BlockSpec((rows // segments, chunk), lambda h: (0, h))] * segments,
        scratch_shapes=[
            pltpu.VMEM((rows + 2 * HALO, wide), jnp.bfloat16),
            pltpu.VMEM((rows + 2 * HALO, wide), jnp.bfloat16),
            pltpu.VMEM((rows, wide), jnp.bfloat16),
            pltpu.VMEM((rows, wide), jnp.bfloat16),
        ],
        compiler_params=pltpu.CompilerParams(vmem_limit_bytes=VMEM),
        cost_estimate=COST,
        name="warp_filter",
    )(weight, *([low] * 3), *([image] * 3), *([high] * 3), rows_m, cols_m)


def join_kernel(*refs):
    block = refs[0].shape[0]
    for step, ref in enumerate(refs[:-1]):
        refs[-1][pl.ds(step * block, block), :] = ref[...]


def joined(blocks):
    block, columns = blocks[0].shape
    vmem = pl.BlockSpec(memory_space=pltpu.VMEM)
    return pl.pallas_call(
        join_kernel,
        out_shape=jax.ShapeDtypeStruct((len(blocks) * block, columns), blocks[0].dtype),
        in_specs=[vmem] * len(blocks),
        out_specs=vmem,
        compiler_params=pltpu.CompilerParams(vmem_limit_bytes=VMEM),
        cost_estimate=COST,
        name="join_blocks",
    )(*blocks)


def stage_distances(lines):
    stages = []
    step = 1
    while step < lines:
        stages.append(list(reversed(range(step, lines, 2 * step))))
        step *= 2
    return stages


def pair_kernel(place, table, mine, other, *rest, slots, distances, quarter):
    *outs, mine_all, other_all = rest
    rows = mine.shape[0]
    chunk = outs[0].shape[1]
    count = table.shape[0] // 3
    for source, held in ((mine, mine_all), (other, other_all)):
        held[pl.ds(0, rows), :] = source[...].astype(jnp.float32)
        held[pl.ds(rows, quarter), :] = jnp.zeros((quarter, source.shape[1]), jnp.float32)
    line = place[1]

    for distance, out in zip(distances, outs):
        first = (line ^ distance) * slots

        def summed(slot, first=first):
            column = pl.ds(pl.multiple_of(table[first + slot] * chunk, 128), chunk)
            from_mine = pl.ds(pl.multiple_of(table[count + first + slot], quarter), quarter)
            from_other = pl.ds(pl.multiple_of(table[2 * count + first + slot], quarter), quarter)
            return mine_all[from_mine, column] + other_all[from_other, column]

        for slot in range(0, slots - 1, 2):
            rows_two = jnp.concatenate([summed(slot), summed(slot + 1)], axis=0)
            out[pl.ds(slot * quarter, 2 * quarter), :] = rows_two.astype(jnp.bfloat16)
        if slots % 2:
            out[pl.ds((slots - 1) * quarter, quarter), :] = summed(slots - 1).astype(jnp.bfloat16)


def pair_sum(place, table, mine, other, slots, lines, quarter):
    rows, double = mine.shape
    chunk = double // 2
    distances = sum(stage_distances(lines), []) + [0]
    smem = pl.BlockSpec(memory_space=pltpu.SMEM)
    vmem = pl.BlockSpec(memory_space=pltpu.VMEM)
    outs = pl.pallas_call(
        functools.partial(pair_kernel, slots=slots, distances=distances, quarter=quarter),
        out_shape=[jax.ShapeDtypeStruct((slots * quarter, chunk), jnp.bfloat16)] * lines,
        in_specs=[smem, smem, vmem, vmem],
        out_specs=[vmem] * lines,
        scratch_shapes=[pltpu.VMEM((rows + quarter, double), jnp.float32)] * 2,
        compiler_params=pltpu.CompilerParams(vmem_limit_bytes=VMEM),
        cost_estimate=COST,
        name="pair_sum",
    )(place, table, mine, other)
    return dict(zip(distances, outs))


def weight_kernel(place, sites, facts, out, covers, *, cores, quarter, width, bands):
    slots = out.shape[0] // quarter
    half_cols = out.shape[1]
    exposures = facts.shape[0]
    owner = place[1] * cores + place[2]
    column = lax.broadcasted_iota(jnp.int32, (quarter, half_cols), 1)
    for half in range(2):
        for exposure in range(exposures):
            first = facts[exposure, 0].astype(jnp.int32) - half * half_cols
            inside = (column >= first) & (column < first + width)
            covers[half * exposures + exposure] = jnp.where(inside, facts[exposure, 2], 0.0)

    def one_slot(slot, carry):
        site = sites[owner * slots + slot]
        total = jnp.zeros((quarter, half_cols), jnp.float32)
        for exposure in range(exposures):
            relative = lax.shift_right_logical(site, 1) - facts[exposure, 1].astype(jnp.int32)
            present = jnp.where((relative >= 0) & (relative < bands), jnp.float32(1.0), jnp.float32(0.0))
            total = total + present * covers[(site & 1) * exposures + exposure]
        out[pl.ds(pl.multiple_of(slot * quarter, quarter), quarter), :] = jnp.maximum(total, 1.0)
        return carry

    lax.fori_loop(0, slots, one_slot, 0)


def patch_weights(place, sites, facts, slots, quarter, cores, width, bands):
    smem = pl.BlockSpec(memory_space=pltpu.SMEM)
    return pl.pallas_call(
        functools.partial(weight_kernel, cores=cores, quarter=quarter, width=width, bands=bands),
        out_shape=jax.ShapeDtypeStruct((slots * quarter, width // 2), jnp.float32),
        in_specs=[smem] * 3,
        out_specs=pl.BlockSpec(memory_space=pltpu.VMEM),
        scratch_shapes=[pltpu.VMEM((2 * facts.shape[0], quarter, width // 2), jnp.float32)],
        compiler_params=pltpu.CompilerParams(vmem_limit_bytes=VMEM),
        cost_estimate=COST,
        name="patch_weights",
    )(place, sites, facts)


def finish_kernel(*refs, count):
    pieces, scale, out = refs[:count], refs[count], refs[-1]
    total = pieces[0][...].astype(jnp.float32)
    for piece in pieces[1:]:
        total += piece[...].astype(jnp.float32)
    out[...] = total / scale[...]


def finish_chunk(pieces, scale, result, start):
    rows, chunk = pieces[0].shape
    column = pl.BlockSpec((rows, chunk), lambda i: (0, start // chunk))
    specs = [pl.BlockSpec((rows, chunk), lambda i: (0, 0))] * len(pieces) + [column]
    operands = [*pieces, scale]
    aliases = {}
    if result is not None:
        specs.append(pl.BlockSpec(memory_space=pl.ANY))
        aliases = {len(operands): 0}
        operands.append(result)
    return pl.pallas_call(
        functools.partial(finish_kernel, count=len(pieces)),
        out_shape=jax.ShapeDtypeStruct(scale.shape, jnp.float32),
        grid=(1,),
        in_specs=specs,
        out_specs=column,
        input_output_aliases=aliases,
        compiler_params=pltpu.CompilerParams(vmem_limit_bytes=VMEM),
        cost_estimate=pl.CostEstimate(
            flops=len(pieces) * rows * chunk, bytes_accessed=rows * chunk * (2 * len(pieces) + 8), transcendentals=0
        ),
        name="patch_mean",
    )(*operands)


def swapped(value, axis, distance):
    count = lax.axis_size(axis)
    return lax.ppermute(value, axis, [(i, i ^ distance) for i in range(count)])


def scatter_sum(pieces, in_turn):
    pieces = dict(pieces)
    kept, added = [pieces[0]], []
    for stage, distances in enumerate(stage_distances(len(pieces))):
        for distance in distances:
            if in_turn and distance != distances[0]:
                pieces[distance], _ = lax.optimization_barrier((pieces[distance], added))
            received = swapped(pieces[distance], "line", 1 << stage)
            target = distance ^ (1 << stage)
            if target:
                both = pieces[target].astype(jnp.float32) + received.astype(jnp.float32)
                pieces[target] = both.astype(jnp.bfloat16)
                added = [pieces[target]]
            else:
                kept.append(received)
    return kept, added


def per_device(images, psf_coef, phases, col_shift, band_offset, exposure_weight, patch_site):
    image = images[0]
    rows, width = image.shape
    segments = lax.axis_size("seg")
    lines = lax.axis_size("line")
    cores = lax.axis_size("core")
    quarter = BAND_ROWS // segments
    half_cols = width // 2
    slots = patch_site.shape[0] // (lines * cores)
    bands = segments * rows // BAND_ROWS
    place = jnp.stack([lax.axis_index(axis) for axis in ("seg", "line", "core")]).astype(jnp.int32)

    forward = [(i, i + 1) for i in range(segments - 1)]
    backward = [(i + 1, i) for i in range(segments - 1)]
    top, bottom = edge_rows(image)
    low = lax.ppermute(bottom, "seg", forward)
    high = lax.ppermute(top, "seg", backward)
    rows_m, cols_m = build_matrices(place, psf_coef, phases, col_shift, rows, width, segments)
    weight = exposure_weight.astype(jnp.float32)

    chunks = []
    start = 0
    for part in PARTS:
        chunks.append((start, half_cols // part))
        start += half_cols // part
    other_offset = swapped(band_offset, "core", 1)
    sites = lax.dynamic_index_in_dim(patch_site.reshape(lines, cores, slots), place[2], 1, keepdims=False).reshape(-1)
    here = rows // BAND_ROWS

    def rows_from(offset):
        relative = sites // 2 - offset
        held = ((relative // here) ^ place[0]) * here + relative % here
        return jnp.where((relative >= 0) & (relative < bands), held, bands) * quarter

    table = jnp.concatenate([sites % 2, rows_from(band_offset), rows_from(other_offset)])
    facts = jnp.stack([col_shift.astype(jnp.float32), band_offset.astype(jnp.float32), weight], axis=1)
    facts = jnp.concatenate([facts, swapped(facts, "core", 1)], axis=0)
    early = facts
    step = 1
    while step < lines:
        early = facts
        facts = jnp.concatenate([facts, swapped(facts, "line", step)], axis=0)
        step *= 2
    scale = patch_weights(place, patch_site, facts, slots, quarter, cores, width, bands)

    def tied(values, others):
        return lax.optimization_barrier((values, others))[0]

    result = None
    count = len(chunks)
    sent, sums, kept, added = [None] * count, [None] * count, [None] * count, [None] * count

    def filtered(index):
        start, chunk = chunks[index]
        held = tied(weight, sums[index - 2]) if index >= 2 else weight
        sent[index] = filter_chunk(held, low, image, high, rows_m, cols_m, start, chunk, segments)

    filtered(0)
    for index, (start, chunk) in enumerate(chunks):
        outgoing = sent[index]
        received = [swapped(outgoing[d], "seg", d) for d in range(1, segments)]
        if index + 1 < count:
            filtered(index + 1)
            received = tied(received, sent[index + 1])
        if index == 0:
            received = tied(received, scale)
        if index == 1:
            received = tied(received, scale)
        if index >= 1:
            received = tied(received, (added[index - 1], kept[index - 1][:-1]))
        mine = joined([outgoing[0]] + received)
        other = swapped(mine, "core", 1)
        sums[index] = pair_sum(place, table, mine, other, slots, lines, quarter)
        kept[index], added[index] = scatter_sum(sums[index], index + 1 == count)
        result = finish_chunk(kept[index], scale, result, start)
    return result.reshape(slots, quarter, half_cols)


def solution(mesh):
    segments, exposures = mesh.shape["seg"], mesh.shape["exp"]
    parted = Mesh(mesh.devices.reshape(segments, exposures // 2, 2), ("seg", "line", "core"))
    spread = ("line", "core")
    placed = (
        P(spread, "seg", None),
        P(spread, None, None),
        P(spread, None),
        P(spread),
        P(spread),
        P(spread),
        P(),
    )
    return jax.shard_map(
        per_device, mesh=parted, in_specs=placed, out_specs=P(spread, "seg", None), check_vma=False
    )
```
